32 devices in a mesh: shard: 4 (over z), ctx: 4 (over y, x), tp: 2 (over core).
Axes of the slice: x: 2, y: 2, z: 4, core: 2. Of those that a mesh axis runs over, the one named last changes fastest.
Arguments:
- tokens: bfloat16 [4, 2048, 1536], P('shard', 'ctx'), may hold values from -6 to 6
- cotangent: bfloat16 [4, 2048, 1536], P('shard', 'ctx'), may hold values from -6 to 6
- norm1_gain: bfloat16 [1536], replicated, may hold values from 0.5 to 1.5
- w_query: bfloat16 [1536, 1536], P('shard', 'tp'), may hold values from -0.15625 to 0.15625
- b_query: bfloat16 [1536], P('tp'), may hold values from -4 to 4
- w_key: bfloat16 [1536, 256], P('shard', 'tp'), may hold values from -0.15625 to 0.15625
- b_key: bfloat16 [256], P('tp'), may hold values from -4 to 4
- w_value: bfloat16 [1536, 256], P('shard', 'tp'), may hold values from -0.15625 to 0.15625
- b_value: bfloat16 [256], P('tp'), may hold values from -4 to 4
- w_out: bfloat16 [1536, 1536], P('shard', 'tp'), may hold values from -0.5 to 0.5
- norm2_gain: bfloat16 [1536], replicated, may hold values from 0.5 to 1.5
- w_gate: bfloat16 [1536, 8960], P('shard', 'tp'), may hold values from -0.15625 to 0.15625
- w_up: bfloat16 [1536, 8960], P('shard', 'tp'), may hold values from -0.15625 to 0.15625
- w_down: bfloat16 [1536, 8960], P('shard', 'tp'), may hold values from -0.0625 to 0.0625
- parents: int32 [4, 9], P('shard'), may hold values from 0 to 8, as said below
- segment_ids: int32 [4, 2048], P('shard'), may hold values from 0 to 8, as said below
- positions: int32 [4, 2048], P('shard'), may hold values from 0 to 1279, as said below
Outputs:
- output: bfloat16 [4, 2048, 1536], P('shard', 'ctx')
- grad_tokens: bfloat16 [4, 2048, 1536], P('shard', 'ctx')
- grad_norm1: float32 [1536], replicated
- grad_wq: float32 [1536, 1536], P('shard', 'tp')
- grad_bq: float32 [1536], P('tp')
- grad_wk: float32 [1536, 256], P('shard', 'tp')
- grad_bk: float32 [256], P('tp')
- grad_wv: float32 [1536, 256], P('shard', 'tp')
- grad_bv: float32 [256], P('tp')
- grad_wo: float32 [1536, 1536], P('shard', 'tp')
- grad_norm2: float32 [1536], replicated
- grad_wg: float32 [1536, 8960], P('shard', 'tp')
- grad_wu: float32 [1536, 8960], P('shard', 'tp')
- grad_wd: float32 [1536, 8960], P('shard', 'tp')
The draws below stay inside these ranges and needn't reach their ends.
Inputs may be any that keep to these rules, and one draw needn't show every extreme that they name: `parents`: in each tree one segment, the trunk, is its own parent; four branch segments have the trunk as parent; four leaf segments each have a different branch as parent; segment numbers are shuffled. `segment_ids`: the trunk's 1024 tokens come first; the eight other segments follow with 128 tokens each, in any order. `positions`: trunk tokens count 0 up; a branch's tokens count from 1024, a leaf's from 1152, rising by one along the segment.
All inputs are finite; a program needn't handle non-finite values.
Results may differ from the reference program's by a relative error of at most 0.019.
Values may be sent and summed in bfloat16 or wider, within the bound.
No kernel may reach another device: no remote copies, remote signals or barrier semaphores. Data moves between devices by JAX's collectives and lax.ppermute only.
A program may use at most 320 MiB of HBM per device.

```python
import jax
import jax.numpy as jnp
from jax import lax

D = 1536
H = 12
KVH = 2
HD = 128
FF = 8960
TREE_LEN = 2048
SEGS = 9
TRUNK = 1024
BRANCH = 128
TREES = 4
QW = 1536
KW = 256


def layout_one(key):
    key_labels, key_order, key_under = jax.random.split(key, 3)
    labels = jax.random.permutation(key_labels, SEGS).astype(jnp.int32)
    order = (jax.random.permutation(key_order, SEGS - 1) + 1).astype(jnp.int32)
    branches = (SEGS - 1) // 2
    under = (jax.random.permutation(key_under, branches) + 1).astype(jnp.int32)
    roles = jnp.arange(SEGS, dtype=jnp.int32)
    leaf_index = jnp.clip(roles - branches - 1, 0, branches - 1)
    parent_role = jnp.where(roles <= branches, 0, jnp.take(under, leaf_index))
    parents = jnp.zeros((SEGS,), jnp.int32).at[labels].set(jnp.take(labels, parent_role))
    tok = jnp.arange(TREE_LEN, dtype=jnp.int32)
    slot = jnp.clip((tok - TRUNK) // BRANCH, 0, SEGS - 2)
    role = jnp.where(tok < TRUNK, 0, jnp.take(order, slot))
    offset = jnp.mod(tok - TRUNK, BRANCH)
    pos = jnp.where(tok < TRUNK, tok, jnp.where(role <= branches, TRUNK + offset, TRUNK + BRANCH + offset))
    return (parents, jnp.take(labels, role), pos.astype(jnp.int32))


def layout(key):
    keys = jax.random.split(key, TREES)
    return jax.vmap(layout_one)(keys)


def draw_parents(key, part):
    return layout(key)[0].astype(jnp.int32)


def draw_segment_ids(key, part):
    return layout(key)[1].astype(jnp.int32)


def draw_positions(key, part):
    return layout(key)[2].astype(jnp.int32)


def steps_of(rng, shape, cuts, smallest, high):
    def one(dim, blocks):
        steps = jax.random.uniform(jax.random.fold_in(jax.random.fold_in(rng, 6), dim), (blocks,), jnp.float32, smallest / len(cuts), high / len(cuts))
        return jnp.repeat(jnp.exp(steps), shape[dim] // blocks).reshape((-1,) + (1,) * (len(shape) - dim - 1))

    loudness = one(*cuts[0])
    for cut in cuts[1:]:
        loudness = loudness * one(*cut)
    return loudness


def gaussian(key, dims, width, most, pieces=(), kind=jnp.bfloat16):
    values = width * jax.random.normal(key, dims, jnp.float32)
    if pieces:
        values = values * steps_of(key, dims, pieces, -0.22, 0.18)
    return jnp.clip(values, -most, most).astype(kind)


def setup_inputs(seed: int = 0) -> dict:
    splits = jax.random.split(jax.random.key(seed), 18)
    return {
        "tokens": gaussian(splits[0], (TREES, TREE_LEN, D), 1.0, 6.0, ((0, 4), (1, 4))),
        "cotangent": gaussian(splits[1], (TREES, TREE_LEN, D), 1.0, 6.0, ((0, 4), (1, 4))),
        "norm1_gain": jnp.clip(1.0 + 0.1 * jax.random.normal(splits[2], (D,), jnp.float32), 0.5, 1.5).astype(jnp.bfloat16),
        "w_query": gaussian(splits[3], (D, QW), D ** -0.5, 0.15625, ((0, 4), (1, 2))),
        "b_query": gaussian(splits[4], (QW,), 0.3, 4.0, ((0, 2),)),
        "w_key": gaussian(splits[5], (D, KW), D ** -0.5, 0.15625, ((0, 4), (1, 2))),
        "b_key": gaussian(splits[6], (KW,), 0.3, 4.0, ((0, 2),)),
        "w_value": gaussian(splits[7], (D, KW), D ** -0.5, 0.15625, ((0, 4), (1, 2))),
        "b_value": gaussian(splits[8], (KW,), 0.3, 4.0, ((0, 2),)),
        "w_out": gaussian(splits[9], (D, QW), HD ** -0.5, 0.5, ((0, 4), (1, 2))),
        "norm2_gain": jnp.clip(1.0 + 0.1 * jax.random.normal(splits[10], (D,), jnp.float32), 0.5, 1.5).astype(jnp.bfloat16),
        "w_gate": gaussian(splits[11], (D, FF), D ** -0.5, 0.15625, ((0, 4), (1, 2))),
        "w_up": gaussian(splits[12], (D, FF), D ** -0.5, 0.15625, ((0, 4), (1, 2))),
        "w_down": gaussian(splits[13], (D, FF), FF ** -0.5, 0.0625, ((0, 4), (1, 2))),
        "parents": draw_parents(jax.random.fold_in(splits[17], 71), 0),
        "segment_ids": draw_segment_ids(jax.random.fold_in(splits[17], 71), 0),
        "positions": draw_positions(jax.random.fold_in(splits[17], 71), 0),
    }


EPS = 1e-06
THETA = 1000000.0
NEG = -1e+30
HIGH = lax.Precision.HIGHEST

@jax.custom_vjp
def low(v):
    return lax.optimization_barrier(v.astype(jnp.bfloat16)).astype(jnp.float32)

@jax.custom_vjp
def low_back(v):
    return v

def low_keep(v):
    return (low(v), None)

def low_pass(kept, grad):
    return (grad,)

def back_keep(v):
    return (v, None)

def back_low(kept, grad):
    return (low(grad),)
low.defvjp(low_keep, low_pass)
low_back.defvjp(back_keep, back_low)

def ancestor_codes(parents):
    count = parents.shape[0]
    ids = jnp.arange(count, dtype=jnp.int32)
    chain = ids
    codes = jnp.left_shift(jnp.ones((count,), jnp.int32), ids)
    for step in range(count - 1):
        chain = lax.optimization_barrier(jnp.sum(jnp.where(chain[:, None] == ids[None, :], parents[None, :], 0), axis=1)).astype(jnp.int32)
        codes = jnp.bitwise_or(codes, jnp.left_shift(jnp.ones((count,), jnp.int32), chain))
    return codes

def rope_tables(pos):
    inverse = THETA ** (-jnp.arange(0, HD, 2, dtype=jnp.float32) / HD)
    angle = pos.astype(jnp.float32)[:, None] * inverse[None, :]
    return (jnp.concatenate([jnp.cos(angle)] * 2, axis=-1), jnp.concatenate([jnp.sin(angle)] * 2, axis=-1))

def rotate_half(v):
    half = v.shape[-1] // 2
    return jnp.concatenate([-v[..., half:], v[..., :half]], axis=-1)

def rope(v, cosine, sine):
    return v * cosine[:, None, :] + rotate_half(v) * sine[:, None, :]

def one_tree(params, items):
    g1, wq, bq, wk, bk, wv, bv, wo, g2, wg, wu, wd = params
    x, seg, pos, parents = items
    length = x.shape[0]
    first_root_mean = lax.rsqrt(lax.optimization_barrier(jnp.mean(x * x, axis=-1, keepdims=True)) + EPS)
    first_normed = low(x * first_root_mean * g1)
    query_lin = low_back(jnp.dot(first_normed, wq, precision=HIGH) + bq)
    key_lin = low_back(jnp.dot(first_normed, wk, precision=HIGH) + bk)
    value = low(low_back(jnp.dot(first_normed, wv, precision=HIGH) + bv))
    cosine, sine = rope_tables(pos)
    query = low(rope(query_lin.reshape(length, H, HD), cosine, sine))
    keys = low(rope(key_lin.reshape(length, KVH, HD), cosine, sine))
    keys = jnp.repeat(keys, H // KVH, axis=1)
    values = jnp.repeat(value.reshape(length, KVH, HD), H // KVH, axis=1)
    codes = ancestor_codes(parents)
    code_rows = codes[seg]
    allowed = (jnp.right_shift(code_rows[:, None], seg[None, :]) & 1 == 1) & (pos[None, :] <= pos[:, None])
    raw = low_back(jnp.einsum('qhd,khd->hqk', query, keys, precision=HIGH))
    scores = jnp.where(allowed[None], raw * HD ** (-0.5), NEG)
    top = lax.optimization_barrier(jnp.max(scores, axis=-1, keepdims=True))
    expo = jnp.exp(scores - top)
    probs = low(expo / lax.optimization_barrier(jnp.sum(expo, axis=-1, keepdims=True)))
    mixed = low(low_back(jnp.einsum('hqk,khd->qhd', probs, values, precision=HIGH))).reshape(length, H * HD)
    residual = x + low_back(jnp.dot(mixed, wo.T, precision=HIGH))
    second_root_mean = lax.rsqrt(lax.optimization_barrier(jnp.mean(residual * residual, axis=-1, keepdims=True)) + EPS)
    second_normed = low(residual * second_root_mean * g2)
    gate = low_back(jnp.dot(second_normed, wg, precision=HIGH))
    up = low_back(jnp.dot(second_normed, wu, precision=HIGH))
    act = low(jax.nn.silu(gate) * up)
    return residual + low_back(jnp.dot(act, wd.T, precision=HIGH))

def reference(tokens, cotangent, norm1_gain, w_query, b_query, w_key, b_key, w_value, b_value, w_out, norm2_gain, w_gate, w_up, w_down, parents, segment_ids, positions):
    floats = tuple((v.astype(jnp.float32) for v in (tokens, norm1_gain, w_query, b_query, w_key, b_key, w_value, b_value, w_out, norm2_gain, w_gate, w_up, w_down)))
    saved = jax.checkpoint(one_tree)

    def forward(x, *params):
        return lax.map(lambda items: saved(params, items), (x, segment_ids, positions, parents))
    result, pullback = jax.vjp(forward, *floats)
    grads = pullback(cotangent.astype(jnp.float32))
    return (result.astype(jnp.bfloat16), grads[0].astype(jnp.bfloat16), grads[1], grads[2], grads[3], grads[4], grads[5], grads[6], grads[7], grads[8], grads[9], grads[10], grads[11], grads[12])
```

```python
import functools

import jax
import jax.numpy as jnp
from jax import lax
from jax.experimental import pallas as pl
from jax.experimental.pallas import tpu as pltpu
from jax.sharding import PartitionSpec as P

HD = 128


EPS = 1e-06
THETA = 1000000.0
NEG = -1e30


def ancestor_codes(parents):
    count = parents.shape[0]
    ids = jnp.arange(count, dtype=jnp.int32)
    chain = ids
    codes = jnp.left_shift(jnp.ones((count,), jnp.int32), ids)
    for step in range(count - 1):
        chain = jnp.sum(jnp.where(chain[:, None] == ids[None, :], parents[None, :], 0), axis=1)
        codes = jnp.bitwise_or(codes, jnp.left_shift(jnp.ones((count,), jnp.int32), chain))
    return codes


def rope_tables(pos):
    inverse = THETA ** (-jnp.arange(0, HD, 2, dtype=jnp.float32) / HD)
    angle = pos.astype(jnp.float32)[:, None] * inverse[None, :]
    return (
        jnp.concatenate([jnp.cos(angle)] * 2, axis=-1),
        jnp.concatenate([jnp.sin(angle)] * 2, axis=-1),
    )


def rotate_half(v):
    half = v.shape[-1] // 2
    return jnp.concatenate([-v[..., half:], v[..., :half]], axis=-1)


def rope(v, cosine, sine):
    return v * cosine[:, None, :] + rotate_half(v) * sine[:, None, :]


def rope_back(grad, cosine, sine):
    return grad * cosine[:, None, :] - rotate_half(grad * sine[:, None, :])


def contract_last(left, right):
    return lax.dot_general(
        left, right, (((1,), (1,)), ((), ())), preferred_element_type=jnp.float32
    )


def contract_first(left, right):
    return lax.dot_general(
        left, right, (((0,), (0,)), ((), ())), preferred_element_type=jnp.float32
    )


def norm_backward(normed_gradient, normalized_input, root_mean_square, norm_gain):
    scaled_rows = normed_gradient * norm_gain
    return root_mean_square * (
        scaled_rows
        - normalized_input * jnp.mean(scaled_rows * normalized_input, axis=-1, keepdims=True)
    )


def swap(value, axis, distance):
    size = lax.axis_size(axis)
    return lax.ppermute(value, axis, [(i, i ^ distance) for i in range(size)])


def context_gather(value):
    if lax.axis_size("ctx") != 4:
        return [[value]] + [[swap(value, "ctx", k)] for k in range(1, lax.axis_size("ctx"))]
    half = value.shape[0] // 2
    first = swap(value, "ctx", 1)
    second = swap(value, "ctx", 2)
    far_low = swap(first[:half], "ctx", 2)
    far_high = swap(second[half:], "ctx", 1)
    return [[value], [first], [second], [far_low, far_high]]


def add_narrow(left, right):
    return (left.astype(jnp.float32) + right.astype(jnp.float32)).astype(jnp.bfloat16)


def context_scatter(blocks):
    if lax.axis_size("ctx") != 4:
        total = blocks[0].astype(jnp.float32)
        for k in range(1, lax.axis_size("ctx")):
            total = total + swap(blocks[k].astype(jnp.bfloat16), "ctx", k).astype(jnp.float32)
        return total
    narrow = [block.astype(jnp.bfloat16) for block in blocks[1:]]
    half = blocks[0].shape[0] // 2
    far_low = swap(narrow[2][:half], "ctx", 1)
    far_high = swap(narrow[2][half:], "ctx", 2)
    second = jnp.concatenate(
        [add_narrow(blocks[2][:half], far_low), narrow[1][half:]], axis=0
    )
    first = jnp.concatenate(
        [narrow[0][:half], add_narrow(blocks[1][half:], far_high)], axis=0
    )
    first = swap(first, "ctx", 1)
    second = swap(second, "ctx", 2)
    return blocks[0].astype(jnp.float32) + first.astype(jnp.float32) + second.astype(jnp.float32)


def shard_scatter(terms):
    size = lax.axis_size("shard")
    if size > 4:
        return lax.psum_scatter(terms, "shard", scatter_dimension=0, tiled=False)
    me = lax.axis_index("shard")

    def take(index):
        return lax.dynamic_index_in_dim(
            terms, jnp.clip(index, 0, size - 1), axis=0, keepdims=False
        )

    rising = None
    falling = None
    for step in range(size - 1):
        upward = take(size - 1 - step + me)
        downward = take(me - (size - 1) + step)
        if step:
            upward = add_narrow(upward, rising)
            downward = add_narrow(downward, falling)
        rising = lax.ppermute(upward, "shard", [(i, i + 1) for i in range(step + 1)])
        falling = lax.ppermute(
            downward, "shard", [(i, i - 1) for i in range(size - 1 - step, size)]
        )
    own = take(me).astype(jnp.float32)
    return (own + rising.astype(jnp.float32) + falling.astype(jnp.float32)).astype(jnp.bfloat16)


def spread_kernel(plan, width, total, context_ref, *refs):
    count = len(plan)
    outs = refs[count:]
    context = context_ref[0]
    for ref, (distance, offset, columns) in zip(refs[:count], plan):
        start = jnp.bitwise_xor(context, distance) * width + offset
        size = ref.shape[0]
        for matrix, out in enumerate(outs):
            for piece in range(0, columns, 128):
                place = start + piece

                @pl.when(place < total)
                def _():
                    out[:, pl.ds(pl.multiple_of(place, 128), 128)] = ref[
                        :, pl.ds(matrix * columns + piece, 128)
                    ].astype(jnp.float32)


def spread(blocks, plan, width, total, context):
    rows = blocks[0].shape[0]
    tile = 48 if rows % 48 == 0 else rows
    return pl.pallas_call(
        functools.partial(spread_kernel, plan, width, total),
        grid=(rows // tile,),
        in_specs=[pl.BlockSpec(memory_space=pltpu.SMEM)]
        + [pl.BlockSpec((tile, block.shape[1]), lambda i: (i, 0)) for block in blocks],
        out_specs=[pl.BlockSpec((tile, total), lambda i: (i, 0))] * 3,
        out_shape=[jax.ShapeDtypeStruct((rows, total), jnp.float32)] * 3,
        compiler_params=pltpu.CompilerParams(vmem_limit_bytes=40 * 1024 * 1024),
    )(context.reshape(1), *blocks)


def body(
    tokens,
    cotangent,
    norm1_gain,
    w_query,
    b_query,
    w_key,
    b_key,
    w_value,
    b_value,
    w_out,
    norm2_gain,
    w_gate,
    w_up,
    w_down,
    parents,
    segment_ids,
    positions,
):
    narrow_dtype = jnp.bfloat16
    rows = tokens.shape[1]
    half = rows // 2
    depth = w_query.shape[0]
    model = tokens.shape[2]
    qwp = w_query.shape[1]
    kwp = w_key.shape[1]
    head_loc = qwp // HD
    kv_loc = kwp // HD
    group = head_loc // kv_loc
    ffp = w_gate.shape[1]
    scale = HD ** (-0.5)
    shards = lax.axis_size("shard")
    contexts = lax.axis_size("ctx")
    context = lax.axis_index("ctx")
    core = lax.axis_index("tp")
    first_row = context * rows
    distances = [jnp.bitwise_xor(context, k) for k in range(contexts)]

    def core_half(value):
        return lax.dynamic_slice_in_dim(value, core * half, half)

    def core_join(value):
        other = swap(value, "tp", 1)
        low = jnp.where(core == 0, value, other)
        high = jnp.where(core == 0, other, value)
        return jnp.concatenate([low, high], axis=0)

    def core_reduce(value, count):
        mine = lax.dynamic_slice_in_dim(value, core * count, count)
        other = lax.dynamic_slice_in_dim(value, (1 - core) * count, count)
        return mine.astype(jnp.float32) + swap(other.astype(narrow_dtype), "tp", 1).astype(
            jnp.float32
        )

    def tree_gather(value):
        mine = jnp.concatenate(sum(context_gather(value), []), axis=0)
        return jnp.concatenate([mine, swap(mine, "tp", 1)], axis=0)

    def tree_scatter(value):
        count = value.shape[0] // 2
        mine = value[:count].astype(jnp.float32) + swap(
            value[count:].astype(narrow_dtype), "tp", 1
        ).astype(jnp.float32)
        return context_scatter([mine[k * half : (k + 1) * half] for k in range(contexts)])

    part = depth // contexts
    attention_columns = [w_query, w_key, w_value, w_out]
    inner = qwp + 2 * kwp
    own_rows = jnp.concatenate(
        [lax.dynamic_slice_in_dim(w, context * part, part) for w in attention_columns], axis=1
    )

    def whole_weight(piece):
        columns = piece.shape[1]
        gathered = lax.all_gather(piece, "shard", axis=0, tiled=False)
        blocks = context_gather(gathered)
        whole = jnp.zeros((shards, contexts, part, columns), narrow_dtype)
        for k, block in enumerate(blocks):
            block = jnp.concatenate(block, axis=0)
            whole = lax.dynamic_update_slice(whole, block[:, None], (0, distances[k], 0, 0))
        return whole.reshape(model, columns)

    w_qkv = whole_weight(own_rows[:, :inner])
    wo_all = whole_weight(own_rows[:, inner:])

    width = -(-ffp // (contexts * 128)) * 128
    first_width = width // 256 * 128
    spans = [(0, first_width), (first_width, width - first_width)]
    padding = ((0, 0), (0, width * contexts - ffp))
    gate_pad, up_pad, down_pad = (jnp.pad(w, padding) for w in (w_gate, w_up, w_down))
    ff_weights = []
    for offset, size in spans:
        piece = jnp.concatenate(
            [
                lax.dynamic_slice_in_dim(w, context * width + offset, size, axis=1)
                for w in (gate_pad, up_pad, down_pad)
            ],
            axis=1,
        )
        ff_weights.append(lax.all_gather(piece, "shard", axis=0, tiled=True))

    seg_all = jnp.concatenate(
        [lax.dynamic_slice_in_dim(segment_ids[0], d * rows, rows) for d in distances]
    )
    pos_all = jnp.concatenate(
        [lax.dynamic_slice_in_dim(positions[0], d * rows, rows) for d in distances]
    )
    seg_own = seg_all[:rows]
    pos_own = pos_all[:rows]
    codes = ancestor_codes(parents[0])
    seg_range = jnp.arange(codes.shape[0], dtype=jnp.int32)
    code_own = jnp.sum(jnp.where(seg_own[:, None] == seg_range[None, :], codes[None, :], 0), axis=1)
    allowed = (jnp.right_shift(code_own[:, None], seg_all[None, :]) & 1 == 1) & (
        pos_all[None, :] <= pos_own[:, None]
    )
    cosine, sine = rope_tables(pos_own)
    first_gain = norm1_gain.astype(jnp.float32)
    second_gain = norm2_gain.astype(jnp.float32)
    source_rows = tokens[0].astype(jnp.float32)
    first_root_mean = lax.rsqrt(jnp.mean(source_rows * source_rows, axis=-1, keepdims=True) + EPS)
    first_normalized = source_rows * first_root_mean
    first_normed = (first_normalized * first_gain).astype(narrow_dtype)
    lin = jnp.dot(first_normed, w_qkv, preferred_element_type=jnp.float32)
    query_lin = lin[:, :qwp] + b_query.astype(jnp.float32)
    key_lin = lin[:, qwp : qwp + kwp] + b_key.astype(jnp.float32)
    value_b = (lin[:, qwp + kwp :] + b_value.astype(jnp.float32)).astype(narrow_dtype)
    query_b = rope(query_lin.reshape(rows, head_loc, HD), cosine, sine).astype(narrow_dtype)
    key_b = (
        rope(key_lin.reshape(rows, kv_loc, HD), cosine, sine)
        .astype(narrow_dtype)
        .reshape(rows, kv_loc * HD)
    )
    pairs = jnp.concatenate(
        sum(context_gather(jnp.concatenate([key_b, value_b], axis=1)), []), axis=0
    )
    keys_all, values_all = pairs[:, :kwp], pairs[:, kwp:]
    query_heads = jnp.transpose(query_b, (1, 0, 2))

    def attend(query_h):
        scores = jnp.where(allowed, contract_last(query_h, keys_all) * scale, NEG)
        top = jnp.max(scores, axis=1, keepdims=True)
        expo = jnp.exp(scores - top)
        total = jnp.sum(expo, axis=1, keepdims=True)
        probs = (expo / total).astype(narrow_dtype)
        return (
            jnp.dot(probs, values_all, preferred_element_type=jnp.float32),
            (top + jnp.log(total))[:, 0],
        )

    mixed, logsum = lax.map(attend, query_heads)
    mixed_b = jnp.transpose(mixed.astype(narrow_dtype), (1, 0, 2)).reshape(rows, head_loc * HD)

    output_gradient = cotangent[0]
    gradient_half = core_half(output_gradient).astype(jnp.float32)
    tree_gradient = tree_gather(core_half(output_gradient))

    source_half = core_half(source_rows)
    residual = source_half + core_reduce(contract_last(mixed_b, wo_all), half)
    second_root_mean = lax.rsqrt(jnp.mean(residual * residual, axis=-1, keepdims=True) + EPS)
    second_normalized = residual * second_root_mean
    second_normed = (second_normalized * second_gain).astype(narrow_dtype)
    tree_normed = tree_gather(second_normed)

    mlp = 0.0
    normed_gradient = 0.0
    ff_grads = []
    for (offset, size), weights in zip(spans, ff_weights):
        gate_up_w, down_w = weights[:, : 2 * size], weights[:, 2 * size :]
        gate_up = jnp.dot(tree_normed, gate_up_w, preferred_element_type=jnp.float32)
        gate, up = gate_up[:, :size], gate_up[:, size:]
        sigma = jax.nn.sigmoid(gate)
        act_b = (gate * sigma * up).astype(narrow_dtype)
        grad_act = jnp.dot(tree_gradient, down_w, preferred_element_type=jnp.float32)
        grad_up_b = (grad_act * gate * sigma).astype(narrow_dtype)
        grad_gate_b = (grad_act * up * sigma * (1.0 + gate * (1.0 - sigma))).astype(narrow_dtype)
        grads = jnp.concatenate(
            [
                contract_first(tree_normed, grad_gate_b).astype(narrow_dtype),
                contract_first(tree_normed, grad_up_b).astype(narrow_dtype),
                contract_first(tree_gradient, act_b).astype(narrow_dtype),
            ],
            axis=1,
        )
        ff_grads.append(shard_scatter(grads.reshape(shards, depth, 3 * size)))
        mlp = mlp + contract_last(act_b, down_w)
        normed_gradient = (
            normed_gradient
            + contract_last(grad_gate_b, gate_up_w[:, :size])
            + contract_last(grad_up_b, gate_up_w[:, size:])
        )
    second_normed_gradient = tree_scatter(normed_gradient)
    residual_gradient = gradient_half + norm_backward(
        second_normed_gradient, second_normalized, second_root_mean, second_gain
    )
    grad_attn_b = core_join(residual_gradient.astype(narrow_dtype))
    output = core_join((residual + tree_scatter(mlp)).astype(narrow_dtype))
    grad_mixed = jnp.dot(grad_attn_b, wo_all, preferred_element_type=jnp.float32).astype(
        narrow_dtype
    )
    grad_heads = jnp.transpose(grad_mixed.reshape(rows, head_loc, HD), (1, 0, 2))
    kv_zero = jnp.zeros((keys_all.shape[0], kv_loc * HD), jnp.float32)

    def attend_back(carry, items):
        query_h, grad_h, lse_h = items
        scores = jnp.where(allowed, contract_last(query_h, keys_all) * scale, NEG)
        probs = jnp.exp(scores - lse_h[:, None])
        grad_p = contract_last(grad_h, values_all)
        delta = jnp.sum(probs * grad_p, axis=1, keepdims=True)
        grad_s = (probs * (grad_p - delta) * scale).astype(narrow_dtype)
        grad_q = jnp.dot(grad_s, keys_all, preferred_element_type=jnp.float32)
        grad_k = contract_first(grad_s, query_h)
        grad_v = contract_first(probs.astype(narrow_dtype), grad_h)
        key_acc, value_acc = carry
        return ((key_acc + grad_k, value_acc + grad_v), grad_q)

    (grad_keys, grad_values), grad_query = lax.scan(
        attend_back, (kv_zero, kv_zero), (query_heads, grad_heads, logsum)
    )
    grad_pairs = jnp.concatenate([grad_keys, grad_values], axis=1)
    grad_pairs = context_scatter(
        [grad_pairs[k * rows : (k + 1) * rows] for k in range(contexts)]
    )
    grad_key_own, grad_value_own = grad_pairs[:, :kwp], grad_pairs[:, kwp:]
    grad_q_b = (
        rope_back(jnp.transpose(grad_query, (1, 0, 2)), cosine, sine)
        .astype(narrow_dtype)
        .reshape(rows, head_loc * HD)
    )
    grad_k_b = (
        rope_back(grad_key_own.reshape(rows, kv_loc, HD), cosine, sine)
        .astype(narrow_dtype)
        .reshape(rows, kv_loc * HD)
    )
    grad_v_b = grad_value_own.astype(narrow_dtype)
    grad_qkv = jnp.concatenate([grad_q_b, grad_k_b, grad_v_b], axis=1)
    first_normed_gradient = core_reduce(contract_last(grad_qkv, w_qkv), half)
    source_gradient = core_join(
        (
            residual_gradient
            + norm_backward(
                first_normed_gradient,
                core_half(first_normalized),
                core_half(first_root_mean),
                first_gain,
            )
        ).astype(narrow_dtype)
    )
    gain_sums = jnp.stack(
        [
            jnp.sum(first_normed_gradient * core_half(first_normalized), axis=0),
            jnp.sum(second_normed_gradient * second_normalized, axis=0),
        ]
    )
    bias_sums = jnp.sum(grad_qkv.astype(jnp.float32), axis=0)
    gain_sums = gain_sums + swap(gain_sums, "tp", 1)
    small = lax.psum(
        jnp.concatenate([gain_sums.reshape(-1), bias_sums]),
        ("shard", "ctx"),
    )

    attention_grads = jnp.concatenate(
        [contract_first(first_normed, grad_qkv), contract_first(grad_attn_b, mixed_b)], axis=1
    ).astype(narrow_dtype)
    columns = inner + qwp
    attention_grads = attention_grads.reshape(shards, contexts, part, columns)
    terms = [
        lax.dynamic_index_in_dim(attention_grads, d, axis=1, keepdims=False) for d in distances
    ]
    attention_sum = shard_scatter(context_scatter(terms).astype(narrow_dtype))
    whole = jnp.zeros((contexts, part, columns), narrow_dtype)
    for k, block in enumerate(context_gather(attention_sum)):
        block = jnp.concatenate(block, axis=0)
        whole = lax.dynamic_update_slice(whole, block[None], (distances[k], 0, 0))
    whole = whole.reshape(depth, columns).astype(jnp.float32)

    blocks = []
    plan = []
    for (offset, size), grads in zip(spans, ff_grads):
        for k, block in enumerate(context_gather(grads)):
            blocks.append(jnp.concatenate(block, axis=0))
            plan.append((k, offset, size))
    grad_wg, grad_wu, grad_wd = spread(blocks, tuple(plan), width, ffp, context)

    edges = [0, model, 2 * model, 2 * model + qwp, 2 * model + qwp + kwp, small.shape[0]]
    sums = [small[edges[i] : edges[i + 1]] for i in range(5)]
    return (
        output[None],
        source_gradient[None],
        sums[0],
        whole[:, :qwp],
        sums[2],
        whole[:, qwp : qwp + kwp],
        sums[3],
        whole[:, qwp + kwp : inner],
        sums[4],
        whole[:, inner:],
        sums[1],
        grad_wg,
        grad_wu,
        grad_wd,
    )


def solution(mesh):
    return jax.shard_map(
        body,
        mesh=mesh,
        in_specs=(
            P("shard", "ctx", None),
            P("shard", "ctx", None),
            P(),
            P("shard", "tp"),
            P("tp"),
            P("shard", "tp"),
            P("tp"),
            P("shard", "tp"),
            P("tp"),
            P("shard", "tp"),
            P(),
            P("shard", "tp"),
            P("shard", "tp"),
            P("shard", "tp"),
            P("shard", None),
            P("shard", None),
            P("shard", None),
        ),
        out_specs=(
            P("shard", "ctx", None),
            P("shard", "ctx", None),
            P(),
            P("shard", "tp"),
            P("tp"),
            P("shard", "tp"),
            P("tp"),
            P("shard", "tp"),
            P("tp"),
            P("shard", "tp"),
            P(),
            P("shard", "tp"),
            P("shard", "tp"),
            P("shard", "tp"),
        ),
        check_vma=False,
    )
```

```python
import functools

import jax
import jax.numpy as jnp
from jax import lax
from jax.experimental import pallas as pl
from jax.experimental.pallas import tpu as pltpu
from jax.sharding import PartitionSpec as P

HD = 128


EPS = 1e-06
THETA = 1000000.0
NEG = -1e30


def ancestor_codes(parents):
    count = parents.shape[0]
    ids = jnp.arange(count, dtype=jnp.int32)
    chain = ids
    codes = jnp.left_shift(jnp.ones((count,), jnp.int32), ids)
    for step in range(count - 1):
        chain = jnp.sum(jnp.where(chain[:, None] == ids[None, :], parents[None, :], 0), axis=1)
        codes = jnp.bitwise_or(codes, jnp.left_shift(jnp.ones((count,), jnp.int32), chain))
    return codes


def rope_tables(pos):
    inverse = THETA ** (-jnp.arange(0, HD, 2, dtype=jnp.float32) / HD)
    angle = pos.astype(jnp.float32)[:, None] * inverse[None, :]
    return (
        jnp.concatenate([jnp.cos(angle)] * 2, axis=-1),
        jnp.concatenate([jnp.sin(angle)] * 2, axis=-1),
    )


def rotate_half(v):
    half = v.shape[-1] // 2
    return jnp.concatenate([-v[..., half:], v[..., :half]], axis=-1)


def rope(v, cosine, sine):
    return v * cosine[:, None, :] + rotate_half(v) * sine[:, None, :]


def rope_back(grad, cosine, sine):
    return grad * cosine[:, None, :] - rotate_half(grad * sine[:, None, :])


def contract_last(left, right):
    return lax.dot_general(
        left, right, (((1,), (1,)), ((), ())), preferred_element_type=jnp.float32
    )


def contract_first(left, right):
    return lax.dot_general(
        left, right, (((0,), (0,)), ((), ())), preferred_element_type=jnp.float32
    )


def norm_backward(normed_gradient, normalized_input, root_mean_square, norm_gain):
    scaled_rows = normed_gradient * norm_gain
    return root_mean_square * (
        scaled_rows
        - normalized_input * jnp.mean(scaled_rows * normalized_input, axis=-1, keepdims=True)
    )


def swap(value, axis, distance):
    size = lax.axis_size(axis)
    return lax.ppermute(value, axis, [(i, i ^ distance) for i in range(size)])


def after(value, *others):
    return lax.optimization_barrier((value, *others))[0]


def context_gather_start(value):
    return swap(value, "ctx", 1), swap(value, "ctx", 2)


def context_gather_end(value, first, second):
    half = value.shape[0] // 2
    far_low = swap(first[:half], "ctx", 2)
    far_high = swap(second[half:], "ctx", 1)
    return [[value], [first], [second], [far_low, far_high]]


def context_gather(value):
    return context_gather_end(value, *context_gather_start(value))


def context_send(blocks):
    return [blocks[0]] + [swap(blocks[k], "ctx", k) for k in range(1, len(blocks))]


def context_sum(blocks):
    received = context_send([block.astype(jnp.bfloat16) for block in blocks])
    return sum(block.astype(jnp.float32) for block in (blocks[0], *received[1:]))


def spread_kernel(plan, width, total, context_ref, *refs):
    count = len(plan)
    outs = refs[count:]
    context = context_ref[0]
    for ref, (distance, offset, columns, matrices) in zip(refs[:count], plan):
        start = jnp.bitwise_xor(context, distance) * width + offset
        for slot, matrix in enumerate(matrices):
            out = outs[matrix]
            for piece in range(0, columns, 128):
                place = start + piece

                @pl.when(place < total)
                def _():
                    out[:, pl.ds(pl.multiple_of(place, 128), 128)] = ref[
                        :, pl.ds(slot * columns + piece, 128)
                    ].astype(jnp.float32)


def spread(blocks, plan, width, total, context):
    rows = blocks[0].shape[0]
    tile = 48 if rows % 48 == 0 else rows
    return pl.pallas_call(
        functools.partial(spread_kernel, plan, width, total),
        grid=(rows // tile,),
        in_specs=[pl.BlockSpec(memory_space=pltpu.SMEM)]
        + [pl.BlockSpec((tile, block.shape[1]), lambda i: (i, 0)) for block in blocks],
        out_specs=[pl.BlockSpec((tile, total), lambda i: (i, 0))] * 3,
        out_shape=[jax.ShapeDtypeStruct((rows, total), jnp.float32)] * 3,
        compiler_params=pltpu.CompilerParams(vmem_limit_bytes=40 * 1024 * 1024),
    )(context.reshape(1), *blocks)


def place_kernel(count, context_ref, *refs):
    query_ref, key_ref, value_ref, out_ref = refs[2 * count :]
    context = context_ref[0]
    quarter = refs[0].shape[1]
    part = refs[count].shape[0]
    whole = query_ref.shape[1] // quarter
    keys = key_ref.shape[1]
    for k in range(count):
        place = jnp.bitwise_xor(context, k)
        block = refs[k][...].astype(jnp.float32)

        @pl.when(place < whole)
        def _():
            query_ref[:, pl.ds(pl.multiple_of(place * quarter, 128), quarter)] = block

        @pl.when(place == whole)
        def _():
            key_ref[...] = block[:, :keys]
            value_ref[...] = block[:, keys:]

        row = pl.multiple_of(place * part, 8)
        out_ref[pl.ds(row, part), :] = refs[count + k][...].astype(jnp.float32)


def place_attention(columns, rows, query_width, key_width, context):
    count = len(columns)
    depth = columns[0].shape[0]
    widths = (query_width, key_width, key_width, query_width)
    vmem = pl.BlockSpec(memory_space=pltpu.VMEM)
    return pl.pallas_call(
        functools.partial(place_kernel, count),
        in_specs=[pl.BlockSpec(memory_space=pltpu.SMEM)] + [vmem] * (2 * count),
        out_specs=[vmem] * 4,
        out_shape=[jax.ShapeDtypeStruct((depth, width), jnp.float32) for width in widths],
        compiler_params=pltpu.CompilerParams(vmem_limit_bytes=VMEM_LIMIT),
    )(context.reshape(1), *columns, *rows)


NT = (((1,), (1,)), ((), ()))
NN = (((1,), (0,)), ((), ()))
TN = (((0,), (0,)), ((), ()))
VMEM_LIMIT = 56 * 1024 * 1024


def multiply(left, right, dims):
    return lax.dot_general(left, right, dims, preferred_element_type=jnp.float32)


def ff_kernel(size, first, normed_ref, gradient_ref, weight_ref, *refs):
    inputs, (acts_ref, *outs) = ((), refs) if first else (refs[:4], refs[4:])
    normed = normed_ref[...]
    gate_up = multiply(normed, weight_ref[:, : 2 * size], NN)
    gate, up = gate_up[:, :size], gate_up[:, size:]
    grad_act = multiply(gradient_ref[...], weight_ref[:, 2 * size :], NN)
    sigma = 1.0 / (1.0 + jnp.exp(-gate))
    silu = gate * sigma
    act = (silu * up).astype(jnp.bfloat16)
    grad_up = (grad_act * silu).astype(jnp.bfloat16)
    grad_gate = (grad_act * up * (sigma * (1.0 + gate * (1.0 - sigma)))).astype(jnp.bfloat16)
    acts_ref[:, :size] = grad_gate
    acts_ref[:, size : 2 * size] = grad_up
    acts_ref[:, 2 * size :] = act
    back = multiply(grad_gate, weight_ref[:, :size], NT) + multiply(
        grad_up, weight_ref[:, size : 2 * size], NT
    )
    mlp = multiply(act, weight_ref[:, 2 * size :], NT)
    late = pl.program_id(0) >= pl.num_programs(0) // 2
    for side in range(2):

        @pl.when(late == (side == 1))
        def _():
            for which, value in enumerate((mlp, back)):
                if not first:
                    value = value + inputs[2 * which + side][...].astype(jnp.float32)
                outs[2 * which + side][...] = value.astype(jnp.bfloat16)


def feed_forward(normed, gradient, weights, previous=(), tile=256):
    rows, model = normed.shape
    columns = weights.shape[1]
    steps = rows // tile // 2
    row = pl.BlockSpec((tile, model), lambda i: (i, 0))
    sides = [
        pl.BlockSpec((tile, model), lambda i: (jnp.minimum(i, steps - 1), 0)),
        pl.BlockSpec((tile, model), lambda i: (jnp.maximum(i - steps, 0), 0)),
    ] * 2
    return pl.pallas_call(
        functools.partial(ff_kernel, columns // 3, not previous),
        grid=(rows // tile,),
        in_specs=[row, row, pl.BlockSpec((model, columns), lambda i: (0, 0))]
        + sides[: len(previous)],
        out_specs=[pl.BlockSpec((tile, columns), lambda i: (i, 0))] + sides,
        out_shape=[jax.ShapeDtypeStruct((rows, columns), jnp.bfloat16)]
        + [jax.ShapeDtypeStruct((rows // 2, model), jnp.bfloat16)] * 4,
        compiler_params=pltpu.CompilerParams(vmem_limit_bytes=VMEM_LIMIT),
        cost_estimate=pl.CostEstimate(
            flops=4 * rows * model * columns,
            bytes_accessed=2 * (rows * columns + 4 * rows * model + model * columns),
            transcendentals=rows * columns // 3,
        ),
    )(normed, gradient, weights, *previous)


def ff_grads_kernel(size, normed_ref, gradient_ref, acts_ref, *outs):
    gate_up = multiply(normed_ref[...], acts_ref[:, : 2 * size], TN).astype(jnp.bfloat16)
    down = multiply(gradient_ref[...], acts_ref[:, 2 * size :], TN).astype(jnp.bfloat16)
    if len(outs) == 2:
        outs[0][...] = gate_up
        outs[1][...] = down
    else:
        outs[0][:, : 2 * size] = gate_up
        outs[0][:, 2 * size :] = down


def ff_grads(normed, gradient, acts, split, tile=384):
    rows, model = normed.shape
    columns = acts.shape[1]
    widths = (columns // 3 * 2, columns // 3) if split else (columns,)
    column = pl.BlockSpec((rows, tile), lambda i: (0, i))
    return pl.pallas_call(
        functools.partial(ff_grads_kernel, columns // 3),
        grid=(model // tile,),
        in_specs=[column, column, pl.BlockSpec((rows, columns), lambda i: (0, 0))],
        out_specs=[pl.BlockSpec((tile, width), lambda i: (i, 0)) for width in widths],
        out_shape=[jax.ShapeDtypeStruct((model, width), jnp.bfloat16) for width in widths],
        compiler_params=pltpu.CompilerParams(vmem_limit_bytes=VMEM_LIMIT),
        cost_estimate=pl.CostEstimate(
            flops=2 * rows * model * columns,
            bytes_accessed=2 * (rows * columns + 2 * rows * model + model * columns),
            transcendentals=0,
        ),
    )(normed, gradient, acts)


def rotate_lanes(value):
    half = HD // 2
    rolled = pltpu.roll(value, half, 1)
    lane = lax.broadcasted_iota(jnp.int32, value.shape, 1)
    return jnp.where(lane < half, -rolled, rolled)


def set_mask(mask_ref, code_ref, pos_ref, seg_all_ref, pos_all_ref):
    allowed = (jnp.right_shift(code_ref[...], seg_all_ref[...]) & 1 == 1) & (
        pos_all_ref[...] <= pos_ref[...]
    )
    mask_ref[...] = jnp.where(allowed, 0.0, NEG)


def attend_kernel(
    query_ref,
    key_ref,
    value_ref,
    code_ref,
    pos_ref,
    seg_all_ref,
    pos_all_ref,
    mixed_ref,
    logsum_ref,
    mask_ref,
    value_t_ref,
):
    head = pl.program_id(1)

    @pl.when(head == 0)
    def _():
        set_mask(mask_ref, code_ref, pos_ref, seg_all_ref, pos_all_ref)
        value_t_ref[...] = value_ref[...].T

    scores = multiply(key_ref[...], query_ref[0], NT) * (HD ** (-0.5)) + mask_ref[...]
    top = jnp.max(scores, axis=0, keepdims=True)
    expo = jnp.exp(scores - top)
    total = jnp.sum(expo, axis=0, keepdims=True)
    mixed = multiply(value_t_ref[...], expo.astype(jnp.bfloat16), NN) * (1.0 / total)
    mixed_ref[...] = mixed.T.astype(jnp.bfloat16)
    logsum_ref[pl.ds(head, 1), :] = top + jnp.log(total)


def attention_specs(tile, total):
    query = pl.BlockSpec((1, tile, HD), lambda i, h: (h // 2, i, h % 2))
    block = pl.BlockSpec((tile, HD), lambda i, h: (i, h))
    key = pl.BlockSpec((total, HD), lambda i, h: (0, 0))
    value = pl.BlockSpec((total, HD), lambda i, h: (0, 1))
    line = pl.BlockSpec((1, tile), lambda i, h: (0, i))
    whole = pl.BlockSpec((total, 1), lambda i, h: (0, 0))
    logsum = pl.BlockSpec((8, tile), lambda i, h: (0, i))
    return query, block, key, value, line, whole, logsum


def attend(queries, pairs, code, pos, seg_all, pos_all, heads):
    rows = queries.shape[1]
    total = pairs.shape[0]
    tile = min(rows, 512)
    query, block, key, value, line, whole, logsum = attention_specs(tile, total)
    return pl.pallas_call(
        attend_kernel,
        grid=(rows // tile, heads),
        in_specs=[query, key, value, line, line, whole, whole],
        out_specs=[block, logsum],
        out_shape=[
            jax.ShapeDtypeStruct((rows, heads * HD), jnp.bfloat16),
            jax.ShapeDtypeStruct((8, rows), jnp.float32),
        ],
        scratch_shapes=[
            pltpu.VMEM((total, tile), jnp.float32),
            pltpu.VMEM((HD, total), jnp.bfloat16),
        ],
        compiler_params=pltpu.CompilerParams(vmem_limit_bytes=VMEM_LIMIT),
        cost_estimate=pl.CostEstimate(
            flops=8 * rows * total * HD * heads,
            bytes_accessed=rows * heads * HD * 6,
            transcendentals=rows * total * heads,
        ),
    )(queries, pairs, pairs, code, pos, seg_all, pos_all)


def attend_back_kernel(
    query_ref,
    grad_ref,
    cosine_ref,
    sine_ref,
    key_ref,
    value_ref,
    code_ref,
    pos_ref,
    seg_all_ref,
    pos_all_ref,
    logsum_ref,
    grad_query_ref,
    grad_pairs_ref,
    mask_ref,
    key_t_ref,
):
    head = pl.program_id(1)

    @pl.when(head == 0)
    def _():
        set_mask(mask_ref, code_ref, pos_ref, seg_all_ref, pos_all_ref)
        key_t_ref[...] = key_ref[...].T

    @pl.when((head == 0) & (pl.program_id(0) == 0))
    def _():
        grad_pairs_ref[...] = jnp.zeros_like(grad_pairs_ref)

    scale = HD ** (-0.5)
    query = query_ref[0]
    grad = grad_ref[...]
    scores = multiply(key_ref[...], query, NT) * scale + mask_ref[...]
    probs = jnp.exp(scores - logsum_ref[pl.ds(head, 1), :])
    grad_p = multiply(value_ref[...], grad, NT)
    delta = jnp.sum(probs * grad_p, axis=0, keepdims=True)
    grad_s = (probs * (grad_p - delta) * scale).astype(jnp.bfloat16)
    grad_query = multiply(key_t_ref[...], grad_s, NN).T
    grad_pairs_ref[:, :HD] += multiply(grad_s, query, NN)
    grad_pairs_ref[:, HD:] += multiply(probs.astype(jnp.bfloat16), grad, NN)
    grad_query_ref[0] = (
        grad_query * cosine_ref[...] - rotate_lanes(grad_query * sine_ref[...])
    ).astype(jnp.bfloat16)


def attend_back(queries, grad, cosine, sine, pairs, code, pos, seg_all, pos_all, logsum, heads):
    rows = queries.shape[1]
    total = pairs.shape[0]
    tile = min(rows, 512)
    query, block, key, value, line, whole, sums = attention_specs(tile, total)
    table = pl.BlockSpec((tile, HD), lambda i, h: (i, 0))
    return pl.pallas_call(
        attend_back_kernel,
        grid=(rows // tile, heads),
        in_specs=[query, block, table, table, key, value, line, line, whole, whole, sums],
        out_specs=[query, pl.BlockSpec((total, 2 * HD), lambda i, h: (0, 0))],
        out_shape=[
            jax.ShapeDtypeStruct((heads // 2, rows, 2 * HD), jnp.bfloat16),
            jax.ShapeDtypeStruct((total, 2 * HD), jnp.float32),
        ],
        scratch_shapes=[
            pltpu.VMEM((total, tile), jnp.float32),
            pltpu.VMEM((HD, total), jnp.bfloat16),
        ],
        compiler_params=pltpu.CompilerParams(vmem_limit_bytes=VMEM_LIMIT),
        cost_estimate=pl.CostEstimate(
            flops=20 * rows * total * HD * heads,
            bytes_accessed=rows * heads * HD * 6,
            transcendentals=rows * total * heads,
        ),
    )(queries, grad, cosine, sine, pairs, pairs, code, pos, seg_all, pos_all, logsum)


def shard_gather_small(piece):
    size = lax.axis_size("shard")
    me = lax.axis_index("shard")
    if size > 4:
        return lax.all_gather(piece, "shard", axis=0, tiled=False)
    parts = [piece] + [
        lax.ppermute(piece, "shard", [(i, (i + k) % size) for i in range(size)])
        for k in range(1, size)
    ]
    whole = jnp.zeros((size,) + piece.shape, piece.dtype)
    for k, part in enumerate(parts):
        whole = lax.dynamic_update_slice(whole, part[None], (lax.rem(me - k + size, size), 0, 0))
    return whole


def body(
    tokens,
    cotangent,
    norm1_gain,
    w_query,
    b_query,
    w_key,
    b_key,
    w_value,
    b_value,
    w_out,
    norm2_gain,
    w_gate,
    w_up,
    w_down,
    parents,
    segment_ids,
    positions,
):
    narrow_dtype = jnp.bfloat16
    rows = tokens.shape[1]
    half = rows // 2
    depth = w_query.shape[0]
    model = tokens.shape[2]
    qwp = w_query.shape[1]
    kwp = w_key.shape[1]
    head_loc = qwp // HD
    ffp = w_gate.shape[1]
    shards = lax.axis_size("shard")
    contexts = lax.axis_size("ctx")
    context = lax.axis_index("ctx")
    core = lax.axis_index("tp")
    inner = qwp + 2 * kwp
    quarter = inner // contexts
    distances = [jnp.bitwise_xor(context, k) for k in range(contexts)]
    bar = lax.optimization_barrier

    def core_half(value):
        return lax.dynamic_slice_in_dim(value, core * half, half)

    def core_order(mine, other):
        low = jnp.where(core == 0, mine, other)
        high = jnp.where(core == 0, other, mine)
        return jnp.concatenate([low, high], axis=0)

    def core_join(value):
        return core_order(value, swap(value, "tp", 1))

    def core_reduce(value):
        mine = lax.dynamic_slice_in_dim(value, core * half, half)
        other = lax.dynamic_slice_in_dim(value, (1 - core) * half, half)
        return mine.astype(jnp.float32) + swap(other.astype(narrow_dtype), "tp", 1).astype(
            jnp.float32
        )

    def tree_gather(value):
        mine = jnp.concatenate(sum(context_gather(value), []), axis=0)
        return jnp.concatenate([mine, swap(mine, "tp", 1)], axis=0)

    def tree_terms(mine, other):
        mine = mine.astype(jnp.float32) + other.astype(jnp.float32)
        return [mine[k * half : (k + 1) * half] for k in range(contexts)]

    def tree_block(value, k):
        count = value.shape[0] // 2
        return core_order(
            value[k * half : (k + 1) * half], value[count + k * half : count + (k + 1) * half]
        )

    def tree_line(line):
        return jnp.concatenate(
            [
                lax.dynamic_slice_in_dim(line, d * rows + side * half, half)
                for side in (core, 1 - core)
                for d in distances
            ]
        )

    first_gain = norm1_gain.astype(jnp.float32)
    second_gain = norm2_gain.astype(jnp.float32)
    source_half = core_half(tokens[0]).astype(jnp.float32)
    first_root_mean = lax.rsqrt(jnp.mean(source_half * source_half, axis=-1, keepdims=True) + EPS)
    first_normalized = source_half * first_root_mean
    first_normed = tree_gather((first_normalized * first_gain).astype(narrow_dtype))

    joined = jnp.concatenate([w_query, w_key, w_value], axis=1)
    quarter_own = lax.dynamic_slice_in_dim(joined, context * quarter, quarter, axis=1)
    columns_all = shard_gather_small(
        jnp.concatenate([quarter_own, joined[:, qwp:]], axis=1)
    ).reshape(model, quarter + 2 * kwp)

    pos_all = tree_line(positions[0])
    cosine_all, sine_all = rope_tables(pos_all)
    first_normed, w_out, parent_line, segment_line, w_gate_late, w_up_late, w_down_late = bar(
        (first_normed, w_out, parents[0], segment_ids[0], w_gate, w_up, w_down)
    )
    seg_all = tree_line(segment_line)
    first_row = context * rows
    seg_own = lax.dynamic_slice_in_dim(segment_line, first_row, rows)
    pos_own = lax.dynamic_slice_in_dim(positions[0], first_row, rows)
    labels = jnp.arange(parents.shape[1], dtype=jnp.int32)

    def parent_of(segment):
        return jnp.sum(jnp.where(segment[:, None] == labels[None], parent_line[None], 0), axis=1)

    above = parent_of(labels)
    code_line = 1 << labels | 1 << above | 1 << parent_of(above)
    code_own = jnp.sum(jnp.where(seg_own[:, None] == labels[None], code_line[None], 0), axis=1)
    mask_lines = (code_own[None], pos_own[None], seg_all[:, None], pos_all[:, None])
    cosine, sine = rope_tables(pos_own)

    lin = jnp.dot(first_normed, columns_all, preferred_element_type=jnp.float32)
    biases = jnp.concatenate([b_query, b_key, b_value]).astype(jnp.float32)

    def turned(value, bias):
        value = (value + bias).reshape(value.shape[0], -1, HD)
        return rope(value, cosine_all, sine_all).reshape(value.shape[0], -1)

    queries_all = turned(
        lin[:, :quarter], lax.dynamic_slice_in_dim(biases, context * quarter, quarter)
    ).astype(narrow_dtype)
    pairs = jnp.concatenate(
        [
            turned(lin[:, quarter : quarter + kwp], biases[qwp : qwp + kwp]),
            lin[:, quarter + kwp :] + biases[qwp + kwp :],
        ],
        axis=1,
    ).astype(narrow_dtype)
    queries = jnp.zeros((contexts, rows, quarter), narrow_dtype)
    exchanged = context_send([tree_block(queries_all, k) for k in range(contexts)])
    for k, block in enumerate(exchanged):
        queries = lax.dynamic_update_slice(queries, block[None], (distances[k], 0, 0))

    part = depth // contexts
    wo_piece = lax.dynamic_slice_in_dim(w_out, context * part, part)
    wo_all = jnp.zeros((shards, contexts, part, qwp), narrow_dtype)
    for k, block in enumerate(context_gather(shard_gather_small(wo_piece))):
        block = jnp.concatenate(block, axis=0)
        wo_all = lax.dynamic_update_slice(wo_all, block[:, None], (0, distances[k], 0, 0))
    wo_all = wo_all.reshape(model, qwp)

    width = -(-ffp // (contexts * 128)) * 128
    first_width = width // 192 * 128
    spans = [(0, first_width), (first_width, width - first_width)]
    padding = ((0, 0), (0, width * contexts - ffp))
    ff_weights = []
    for (offset, size), group in zip(
        spans, ((w_gate, w_up, w_down), (w_gate_late, w_up_late, w_down_late))
    ):
        piece = jnp.concatenate(
            [
                lax.dynamic_slice_in_dim(
                    jnp.pad(w, padding), context * width + offset, size, axis=1
                )
                for w in group
            ],
            axis=1,
        )
        ff_weights.append(lax.all_gather(piece, "shard", axis=0, tiled=True))

    queries, cotangent_late = bar((queries, cotangent))
    gradient_half = core_half(cotangent_late[0])
    tree_gradient = tree_gather(gradient_half)
    mixed_b, logsum = attend(queries, pairs, *mask_lines, head_loc)


    residual = source_half + core_reduce(contract_last(mixed_b, wo_all))
    second_root_mean = lax.rsqrt(jnp.mean(residual * residual, axis=-1, keepdims=True) + EPS)
    second_normalized = residual * second_root_mean
    second_normed = (second_normalized * second_gain).astype(narrow_dtype)
    tree_normed = tree_gather(second_normed)
    tree_normed, quarter_late = bar((tree_normed, columns_all[:, :quarter]))
    quarter_blocks = context_send([quarter_late] * contexts)

    acts, *sums = feed_forward(tree_normed, tree_gradient, ff_weights[0])
    (grads,) = ff_grads(tree_normed, tree_gradient, acts, False)
    grads, late_weights = bar((grads, ff_weights[1]))
    late_acts, *sums = feed_forward(
        tree_normed, tree_gradient, late_weights, tuple(sums)
    )
    (late_grads,) = ff_grads(tree_normed, tree_gradient, late_acts, False)

    def over_shard(value):
        return lax.psum_scatter(
            value.reshape(shards, depth, value.shape[1]), "shard", scatter_dimension=0, tiled=False
        )

    ff_sums = [over_shard(grads)]

    mlp_mine, mlp_other, back_mine, back_other = sums
    back_mine, back_other, late_grads = bar((back_mine, swap(back_other, "tp", 1), late_grads))
    second_normed_gradient = context_sum(tree_terms(back_mine, back_other))
    second_normed_gradient, mlp_mine, mlp_other = bar(
        (second_normed_gradient, mlp_mine, mlp_other)
    )
    mlp = context_sum(tree_terms(mlp_mine, swap(mlp_other, "tp", 1)))
    residual_gradient = gradient_half.astype(jnp.float32) + norm_backward(
        second_normed_gradient, second_normalized, second_root_mean, second_gain
    )
    grad_attn_b = core_join(residual_gradient.astype(narrow_dtype))
    grad_mixed = jnp.dot(grad_attn_b, wo_all, preferred_element_type=jnp.float32).astype(
        narrow_dtype
    )

    groups = qwp // quarter
    grad_wo = contract_first(grad_attn_b, mixed_b).astype(narrow_dtype)
    grad_wo = grad_wo.reshape(shards, contexts, part, qwp)
    grad_wo = [lax.dynamic_index_in_dim(grad_wo, d, axis=1, keepdims=False) for d in distances]
    grad_wo = context_sum(grad_wo).astype(narrow_dtype)
    grad_query, grad_pairs = attend_back(
        queries, grad_mixed, cosine, sine, pairs, *mask_lines, logsum, head_loc
    )
    grad_query, grad_pairs, ff_sums[0], late_grads = bar(
        (grad_query, grad_pairs, ff_sums[0], late_grads)
    )
    ff_sums.append(over_shard(late_grads))
    early_near = context_gather_start(ff_sums[0])
    grad_pairs = context_sum([tree_block(grad_pairs, k) for k in range(contexts)])
    grad_keys = rope_back(grad_pairs[:, :kwp].reshape(rows, -1, HD), cosine, sine)
    grad_pairs = jnp.concatenate(
        [grad_keys.reshape(rows, kwp), grad_pairs[:, kwp:]], axis=1
    ).astype(narrow_dtype)
    grad_quarters = jnp.concatenate([grad_query, grad_pairs[None]], axis=0)
    relative_grads = [
        lax.dynamic_index_in_dim(grad_quarters, d, axis=0, keepdims=False) for d in distances
    ]
    exchanged = context_send(relative_grads)
    exchanged, early_near, grad_wo, ff_sums[1] = bar(
        (exchanged, early_near, grad_wo, ff_sums[1])
    )
    early_blocks = context_gather_end(ff_sums[0], *early_near)
    late_near = context_gather_start(ff_sums[1])
    normed_gradient = sum(
        contract_last(grads, block) for grads, block in zip(relative_grads, quarter_blocks)
    )
    first_normed_gradient = core_reduce(normed_gradient)
    source_gradient = (
        residual_gradient
        + norm_backward(first_normed_gradient, first_normalized, first_root_mean, first_gain)
    ).astype(narrow_dtype)
    source_gradient = core_join(source_gradient)
    small = jnp.concatenate(
        [
            jnp.sum(first_normed_gradient * first_normalized, axis=0),
            jnp.sum(second_normed_gradient * second_normalized, axis=0),
        ]
    )
    small = small + swap(small, "tp", 1)
    small = jnp.concatenate([small, jnp.sum(grad_quarters.astype(jnp.float32), axis=1).reshape(-1)])

    exchanged = jnp.concatenate(
        [
            lax.dynamic_slice_in_dim(block, side * half, half)
            for side in (core, 1 - core)
            for block in exchanged
        ],
        axis=0,
    )
    grad_columns = contract_first(first_normed, exchanged).astype(narrow_dtype)

    def packed(value):
        value = value.reshape(-1, quarter)
        high = value.astype(narrow_dtype)
        return high, (value - high.astype(jnp.float32)).astype(narrow_dtype)

    def unpacked(value):
        count = value.shape[-2] // 2
        value = value.astype(jnp.float32)
        return value[..., :count, :] + value[..., count:, :]

    me = lax.axis_index("shard")
    terms = jnp.concatenate(
        [grad_columns.reshape(shards, depth, quarter)]
        + [grad_wo[:, :, g * quarter : (g + 1) * quarter] for g in range(groups)]
        + [jnp.broadcast_to(half_value, (shards,) + half_value.shape) for half_value in packed(small)],
        axis=1,
    )
    if shards > 4:
        received = [lax.all_to_all(terms, "shard", 0, 0)[k] for k in range(shards)]
    else:
        received = [lax.dynamic_index_in_dim(terms, me, axis=0, keepdims=False)]
        for k in range(1, shards):
            received.append(
                lax.ppermute(
                    lax.dynamic_index_in_dim(terms, lax.rem(me + k, shards), keepdims=False),
                    "shard",
                    [(i, (i + k) % shards) for i in range(shards)],
                )
            )
    received, early_blocks, late_near, mlp = bar((received, early_blocks, late_near, mlp))
    output = core_join((residual + mlp).astype(narrow_dtype))
    late_blocks = context_gather_end(ff_sums[1], *late_near)
    count = depth + groups * part
    weight_sums = sum(value[:count].astype(jnp.float32) for value in received).astype(narrow_dtype)
    small = sum(unpacked(value[count:]) for value in received)
    blocks = context_send([jnp.concatenate([weight_sums, *packed(small)], axis=0)] * contexts)
    small = sum(unpacked(block[count:]) for block in blocks).reshape(-1)
    column_blocks = [block[:depth] for block in blocks]
    row_blocks = [
        jnp.concatenate(
            [block[depth + g * part : depth + (g + 1) * part] for g in range(groups)], axis=1
        )
        for block in blocks
    ]
    grad_wq, grad_wk, grad_wv, grad_wo = place_attention(
        column_blocks, row_blocks, qwp, kwp, context
    )

    early_blocks, late_blocks, output, source_gradient, small, grad_wq = bar(
        (early_blocks, late_blocks, output, source_gradient, small, grad_wq)
    )
    plan = [
        (k, offset, size, (0, 1, 2)) for offset, size in spans for k in range(contexts)
    ]
    grad_wg, grad_wu, grad_wd = spread(
        [jnp.concatenate(block, axis=0) for block in early_blocks + late_blocks], tuple(plan), width, ffp, context
    )

    edges = [0, model, 2 * model, 2 * model + qwp, 2 * model + qwp + kwp, small.shape[0]]
    sums = [small[edges[i] : edges[i + 1]] for i in range(5)]
    return (
        output[None],
        source_gradient[None],
        sums[0],
        grad_wq,
        sums[2],
        grad_wk,
        sums[3],
        grad_wv,
        sums[4],
        grad_wo,
        sums[1],
        grad_wg,
        grad_wu,
        grad_wd,
    )


def solution(mesh):
    return jax.shard_map(
        body,
        mesh=mesh,
        in_specs=(
            P("shard", "ctx", None),
            P("shard", "ctx", None),
            P(),
            P("shard", "tp"),
            P("tp"),
            P("shard", "tp"),
            P("tp"),
            P("shard", "tp"),
            P("tp"),
            P("shard", "tp"),
            P(),
            P("shard", "tp"),
            P("shard", "tp"),
            P("shard", "tp"),
            P("shard", None),
            P("shard", None),
            P("shard", None),
        ),
        out_specs=(
            P("shard", "ctx", None),
            P("shard", "ctx", None),
            P(),
            P("shard", "tp"),
            P("tp"),
            P("shard", "tp"),
            P("tp"),
            P("shard", "tp"),
            P("tp"),
            P("shard", "tp"),
            P(),
            P("shard", "tp"),
            P("shard", "tp"),
            P("shard", "tp"),
        ),
        check_vma=False,
    )
```

```python
import functools

import jax
import jax.numpy as jnp
from jax import lax
from jax.experimental import pallas as pl
from jax.experimental.pallas import tpu as pltpu
from jax.sharding import PartitionSpec as P

HD = 128


EPS = 1e-06
THETA = 1000000.0
NEG = -1e30


def rope_tables(pos):
    inverse = THETA ** (-jnp.arange(0, HD, 2, dtype=jnp.float32) / HD)
    angle = pos.astype(jnp.float32)[:, None] * inverse[None, :]
    return (
        jnp.concatenate([jnp.cos(angle)] * 2, axis=-1),
        jnp.concatenate([jnp.sin(angle)] * 2, axis=-1),
    )


def rotate_half(v):
    half = v.shape[-1] // 2
    return jnp.concatenate([-v[..., half:], v[..., :half]], axis=-1)


def rope(v, cosine, sine):
    return v * cosine[:, None, :] + rotate_half(v) * sine[:, None, :]


def rope_back(grad, cosine, sine):
    return grad * cosine[:, None, :] - rotate_half(grad * sine[:, None, :])


def contract_last(left, right):
    return lax.dot_general(
        left, right, (((1,), (1,)), ((), ())), preferred_element_type=jnp.float32
    )


def contract_first(left, right):
    return lax.dot_general(
        left, right, (((0,), (0,)), ((), ())), preferred_element_type=jnp.float32
    )


def norm_backward(normed_gradient, normalized_input, root_mean_square, norm_gain):
    scaled_rows = normed_gradient * norm_gain
    return root_mean_square * (
        scaled_rows
        - normalized_input * jnp.mean(scaled_rows * normalized_input, axis=-1, keepdims=True)
    )


def swap(value, axis, distance):
    size = lax.axis_size(axis)
    return lax.ppermute(value, axis, [(i, i ^ distance) for i in range(size)])


def after(value, *others):
    return lax.optimization_barrier((value, *others))[0]


def context_gather_start(value):
    return swap(value, "ctx", 1), swap(value, "ctx", 2)


def context_gather_end(value, first, second):
    half = value.shape[0] // 2
    far_low = swap(first[:half], "ctx", 2)
    far_high = swap(second[half:], "ctx", 1)
    return [[value], [first], [second], [far_low, far_high]]


def context_gather(value):
    return context_gather_end(value, *context_gather_start(value))


def context_send(blocks):
    return [blocks[0]] + [swap(blocks[k], "ctx", k) for k in range(1, len(blocks))]


def context_sum(blocks):
    received = context_send([block.astype(jnp.bfloat16) for block in blocks])
    return sum(block.astype(jnp.float32) for block in (blocks[0], *received[1:]))


def spread_kernel(plan, spans, width, total, context_ref, *refs):
    count = len(plan)
    outs = refs[count:]
    context = context_ref[0]
    late = pl.program_id(0) >= pl.num_programs(0) // 2
    for ref, (distance, half) in zip(refs[:count], plan):
        start = jnp.bitwise_xor(context, distance) * width

        def write():
            base = 0
            for offset, columns in spans:
                for out in outs:
                    for piece in range(0, columns, 128):
                        place = start + offset + piece

                        @pl.when(place < total)
                        def _():
                            out[:, pl.ds(pl.multiple_of(place, 128), 128)] = ref[
                                :, pl.ds(base + piece, 128)
                            ].astype(jnp.float32)

                    base += columns

        if half is None:
            write()
        else:
            pl.when(late == (half == 1))(write)


def spread(blocks, spans, width, total, context):
    rows = blocks[0][0].shape[0]
    tile = 48 if rows % 96 == 0 else rows // 2
    steps = rows // tile // 2
    maps = {
        None: lambda i: (i, 0),
        0: lambda i: (jnp.minimum(i, steps - 1), 0),
        1: lambda i: (jnp.maximum(i - steps, 0), 0),
    }
    arrays = []
    plan = []
    for distance, pieces in enumerate(blocks):
        for half, piece in enumerate(pieces):
            arrays.append(piece)
            plan.append((distance, None if len(pieces) == 1 else half))
    return pl.pallas_call(
        functools.partial(spread_kernel, tuple(plan), spans, width, total),
        grid=(rows // tile,),
        in_specs=[pl.BlockSpec(memory_space=pltpu.SMEM)]
        + [
            pl.BlockSpec((tile, array.shape[1]), maps[half])
            for array, (_, half) in zip(arrays, plan)
        ],
        out_specs=[pl.BlockSpec((tile, total), lambda i: (i, 0))] * 3,
        out_shape=[jax.ShapeDtypeStruct((rows, total), jnp.float32)] * 3,
        compiler_params=pltpu.CompilerParams(vmem_limit_bytes=40 * 1024 * 1024),
    )(context.reshape(1), *arrays)


def place_kernel(count, part, context_ref, *refs):
    query_ref, key_ref, value_ref, out_ref = refs[count:]
    context = context_ref[0]
    depth = query_ref.shape[0]
    quarter = refs[0].shape[1]
    whole = query_ref.shape[1] // quarter
    keys = key_ref.shape[1]
    for k in range(count):
        place = jnp.bitwise_xor(context, k)
        block = refs[k][:depth].astype(jnp.float32)

        @pl.when(place < whole)
        def _():
            query_ref[:, pl.ds(pl.multiple_of(place * quarter, 128), quarter)] = block

        @pl.when(place == whole)
        def _():
            key_ref[...] = block[:, :keys]
            value_ref[...] = block[:, keys:]

        row = pl.multiple_of(place * part, 8)
        for g in range(whole):
            start = depth + g * part
            out_ref[pl.ds(row, part), g * quarter : (g + 1) * quarter] = refs[k][
                start : start + part
            ].astype(jnp.float32)


def place_attention(blocks, depth, part, query_width, key_width, context):
    count = len(blocks)
    widths = (query_width, key_width, key_width, query_width)
    vmem = pl.BlockSpec(memory_space=pltpu.VMEM)
    return pl.pallas_call(
        functools.partial(place_kernel, count, part),
        in_specs=[pl.BlockSpec(memory_space=pltpu.SMEM)] + [vmem] * count,
        out_specs=[vmem] * 4,
        out_shape=[jax.ShapeDtypeStruct((depth, width), jnp.float32) for width in widths],
        compiler_params=pltpu.CompilerParams(vmem_limit_bytes=VMEM_LIMIT),
    )(context.reshape(1), *blocks)


NT = (((1,), (1,)), ((), ()))
NN = (((1,), (0,)), ((), ()))
TN = (((0,), (0,)), ((), ()))
VMEM_LIMIT = 56 * 1024 * 1024


def multiply(left, right, dims):
    return lax.dot_general(left, right, dims, preferred_element_type=jnp.float32)


def terms_kernel(count, core_ref, normed_ref, *refs):
    blocks, (wo_ref, small_ref, out_ref, rows_ref) = refs[:count], refs[count:]
    core = core_ref[0]
    half = blocks[0].shape[0] // 2
    depth = normed_ref.shape[1]
    part = wo_ref.shape[1]
    quarter = out_ref.shape[2]

    @pl.when(pl.program_id(0) == 0)
    def _():
        for side in range(2):
            start = pl.multiple_of((core if side == 0 else 1 - core) * half, half)
            for k, block in enumerate(blocks):
                place = (side * count + k) * half
                rows_ref[place : place + half] = block[pl.ds(start, half), :]

    out_ref[0, :depth] = multiply(normed_ref[...], rows_ref[...], TN).astype(jnp.bfloat16)
    place = depth
    for column in range(0, wo_ref.shape[2], quarter):
        out_ref[0, place : place + part] = wo_ref[0, :, column : column + quarter]
        place += part
    size = small_ref.shape[0]
    high = small_ref[...].astype(jnp.bfloat16)
    out_ref[0, place : place + size] = high
    out_ref[0, place + size :] = (small_ref[...] - high.astype(jnp.float32)).astype(jnp.bfloat16)


def attention_terms(normed, blocks, grad_wo, small, core):
    rows, model = normed.shape
    shards, part, width = grad_wo.shape
    depth = model // shards
    quarter = blocks[0].shape[1]
    count = depth + part * (width // quarter) + 2 * small.shape[0]
    if depth % 128:
        half = blocks[0].shape[0] // 2
        ordered = [
            lax.dynamic_slice_in_dim(block, side * half, half)
            for side in (core, 1 - core)
            for block in blocks
        ]
        columns = contract_first(normed, jnp.concatenate(ordered, axis=0)).astype(jnp.bfloat16)
        high = small.astype(jnp.bfloat16)
        low = (small - high.astype(jnp.float32)).astype(jnp.bfloat16)
        return jnp.concatenate(
            [columns.reshape(shards, depth, quarter)]
            + [grad_wo[:, :, i : i + quarter] for i in range(0, width, quarter)]
            + [jnp.broadcast_to(value, (shards,) + value.shape) for value in (high, low)],
            axis=1,
        )
    whole = lambda value: pl.BlockSpec(value.shape, lambda i: (0, 0))
    return pl.pallas_call(
        functools.partial(terms_kernel, len(blocks)),
        grid=(shards,),
        in_specs=[
            pl.BlockSpec(memory_space=pltpu.SMEM),
            pl.BlockSpec((rows, depth), lambda i: (0, i)),
            *(whole(block) for block in blocks),
            pl.BlockSpec((1, part, width), lambda i: (i, 0, 0)),
            whole(small),
        ],
        out_specs=pl.BlockSpec((1, count, quarter), lambda i: (i, 0, 0)),
        out_shape=jax.ShapeDtypeStruct((shards, count, quarter), jnp.bfloat16),
        scratch_shapes=[pltpu.VMEM((rows, quarter), jnp.bfloat16)],
        compiler_params=pltpu.CompilerParams(vmem_limit_bytes=VMEM_LIMIT),
        cost_estimate=pl.CostEstimate(
            flops=2 * rows * model * quarter,
            bytes_accessed=2 * (rows * model + rows * quarter + shards * count * quarter),
            transcendentals=0,
        ),
    )(core.reshape(1), normed, *blocks, grad_wo, small)


def ff_kernel(size, first, normed_ref, gradient_ref, weight_ref, *refs):
    inputs, (acts_ref, *outs) = ((), refs) if first else (refs[:4], refs[4:])
    normed = normed_ref[...]
    gate_up = multiply(normed, weight_ref[:, : 2 * size], NN)
    gate, up = gate_up[:, :size], gate_up[:, size:]
    grad_act = multiply(gradient_ref[...], weight_ref[:, 2 * size :], NN)
    sigma = 1.0 / (1.0 + jnp.exp(-gate))
    silu = gate * sigma
    act = (silu * up).astype(jnp.bfloat16)
    grad_up = (grad_act * silu).astype(jnp.bfloat16)
    grad_gate = (grad_act * up * (sigma * (1.0 + gate * (1.0 - sigma)))).astype(jnp.bfloat16)
    acts_ref[:, :size] = grad_gate
    acts_ref[:, size : 2 * size] = grad_up
    acts_ref[:, 2 * size :] = act
    back = multiply(grad_gate, weight_ref[:, :size], NT) + multiply(
        grad_up, weight_ref[:, size : 2 * size], NT
    )
    mlp = multiply(act, weight_ref[:, 2 * size :], NT)
    late = pl.program_id(0) >= pl.num_programs(0) // 2
    for side in range(2):

        @pl.when(late == (side == 1))
        def _():
            for which, value in enumerate((mlp, back)):
                if not first:
                    value = value + inputs[2 * which + side][...].astype(jnp.float32)
                outs[2 * which + side][...] = value.astype(jnp.bfloat16)


def feed_forward(normed, gradient, weights, previous=(), tile=256):
    rows, model = normed.shape
    columns = weights.shape[1]
    steps = rows // tile // 2
    row = pl.BlockSpec((tile, model), lambda i: (i, 0))
    sides = [
        pl.BlockSpec((tile, model), lambda i: (jnp.minimum(i, steps - 1), 0)),
        pl.BlockSpec((tile, model), lambda i: (jnp.maximum(i - steps, 0), 0)),
    ] * 2
    return pl.pallas_call(
        functools.partial(ff_kernel, columns // 3, not previous),
        grid=(rows // tile,),
        in_specs=[row, row, pl.BlockSpec((model, columns), lambda i: (0, 0))]
        + sides[: len(previous)],
        out_specs=[pl.BlockSpec((tile, columns), lambda i: (i, 0))] + sides,
        out_shape=[jax.ShapeDtypeStruct((rows, columns), jnp.bfloat16)]
        + [jax.ShapeDtypeStruct((rows // 2, model), jnp.bfloat16)] * 4,
        compiler_params=pltpu.CompilerParams(vmem_limit_bytes=VMEM_LIMIT),
        cost_estimate=pl.CostEstimate(
            flops=4 * rows * model * columns,
            bytes_accessed=2 * (rows * columns + 4 * rows * model + model * columns),
            transcendentals=rows * columns // 3,
        ),
    )(normed, gradient, weights, *previous)


def ff_grads_kernel(size, normed_ref, gradient_ref, acts_ref, *outs):
    gate_up = multiply(normed_ref[...], acts_ref[:, : 2 * size], TN).astype(jnp.bfloat16)
    down = multiply(gradient_ref[...], acts_ref[:, 2 * size :], TN).astype(jnp.bfloat16)
    if len(outs) == 2:
        outs[0][...] = gate_up
        outs[1][...] = down
    else:
        outs[0][:, : 2 * size] = gate_up
        outs[0][:, 2 * size :] = down


def ff_grads(normed, gradient, acts, split, tile=384):
    rows, model = normed.shape
    columns = acts.shape[1]
    widths = (columns // 3 * 2, columns // 3) if split else (columns,)
    column = pl.BlockSpec((rows, tile), lambda i: (0, i))
    return pl.pallas_call(
        functools.partial(ff_grads_kernel, columns // 3),
        grid=(model // tile,),
        in_specs=[column, column, pl.BlockSpec((rows, columns), lambda i: (0, 0))],
        out_specs=[pl.BlockSpec((tile, width), lambda i: (i, 0)) for width in widths],
        out_shape=[jax.ShapeDtypeStruct((model, width), jnp.bfloat16) for width in widths],
        compiler_params=pltpu.CompilerParams(vmem_limit_bytes=VMEM_LIMIT),
        cost_estimate=pl.CostEstimate(
            flops=2 * rows * model * columns,
            bytes_accessed=2 * (rows * columns + 2 * rows * model + model * columns),
            transcendentals=0,
        ),
    )(normed, gradient, acts)


def rotate_lanes(value):
    half = HD // 2
    rolled = pltpu.roll(value, half, 1)
    lane = lax.broadcasted_iota(jnp.int32, value.shape, 1)
    return jnp.where(lane < half, -rolled, rolled)


def set_mask(mask_ref, code_ref, pos_ref, seg_all_ref, pos_all_ref):
    allowed = (jnp.right_shift(code_ref[...], seg_all_ref[...]) & 1 == 1) & (
        pos_all_ref[...] <= pos_ref[...]
    )
    mask_ref[...] = jnp.where(allowed, 0.0, NEG)


def attend_kernel(
    query_ref,
    key_ref,
    value_ref,
    code_ref,
    pos_ref,
    seg_all_ref,
    pos_all_ref,
    mixed_ref,
    logsum_ref,
    mask_ref,
    value_t_ref,
):
    head = pl.program_id(1)

    @pl.when(head == 0)
    def _():
        set_mask(mask_ref, code_ref, pos_ref, seg_all_ref, pos_all_ref)
        value_t_ref[...] = value_ref[...].T

    scores = multiply(key_ref[...], query_ref[0], NT) * (HD ** (-0.5)) + mask_ref[...]
    top = jnp.max(scores, axis=0, keepdims=True)
    expo = jnp.exp(scores - top)
    total = jnp.sum(expo, axis=0, keepdims=True)
    mixed = multiply(value_t_ref[...], expo.astype(jnp.bfloat16), NN) * (1.0 / total)
    mixed_ref[...] = mixed.T.astype(jnp.bfloat16)
    logsum_ref[pl.ds(head, 1), :] = top + jnp.log(total)


def attention_specs(tile, total):
    query = pl.BlockSpec((1, tile, HD), lambda i, h: (h // 2, i, h % 2))
    block = pl.BlockSpec((tile, HD), lambda i, h: (i, h))
    key = pl.BlockSpec((total, HD), lambda i, h: (0, 0))
    value = pl.BlockSpec((total, HD), lambda i, h: (0, 1))
    line = pl.BlockSpec((1, tile), lambda i, h: (0, i))
    whole = pl.BlockSpec((total, 1), lambda i, h: (0, 0))
    logsum = pl.BlockSpec((8, tile), lambda i, h: (0, i))
    return query, block, key, value, line, whole, logsum


def attend(queries, pairs, code, pos, seg_all, pos_all, heads):
    rows = queries.shape[1]
    total = pairs.shape[0]
    tile = min(rows, 512)
    query, block, key, value, line, whole, logsum = attention_specs(tile, total)
    return pl.pallas_call(
        attend_kernel,
        grid=(rows // tile, heads),
        in_specs=[query, key, value, line, line, whole, whole],
        out_specs=[block, logsum],
        out_shape=[
            jax.ShapeDtypeStruct((rows, heads * HD), jnp.bfloat16),
            jax.ShapeDtypeStruct((8, rows), jnp.float32),
        ],
        scratch_shapes=[
            pltpu.VMEM((total, tile), jnp.float32),
            pltpu.VMEM((HD, total), jnp.bfloat16),
        ],
        compiler_params=pltpu.CompilerParams(vmem_limit_bytes=VMEM_LIMIT),
        cost_estimate=pl.CostEstimate(
            flops=8 * rows * total * HD * heads,
            bytes_accessed=rows * heads * HD * 6,
            transcendentals=rows * total * heads,
        ),
    )(queries, pairs, pairs, code, pos, seg_all, pos_all)


def attend_back_kernel(
    query_ref,
    grad_ref,
    cosine_ref,
    sine_ref,
    key_ref,
    value_ref,
    code_ref,
    pos_ref,
    seg_all_ref,
    pos_all_ref,
    logsum_ref,
    grad_query_ref,
    grad_pairs_ref,
    mask_ref,
    key_t_ref,
):
    head = pl.program_id(1)

    @pl.when(head == 0)
    def _():
        set_mask(mask_ref, code_ref, pos_ref, seg_all_ref, pos_all_ref)
        key_t_ref[...] = key_ref[...].T

    @pl.when((head == 0) & (pl.program_id(0) == 0))
    def _():
        grad_pairs_ref[...] = jnp.zeros_like(grad_pairs_ref)

    scale = HD ** (-0.5)
    query = query_ref[0]
    grad = grad_ref[...]
    scores = multiply(key_ref[...], query, NT) * scale + mask_ref[...]
    probs = jnp.exp(scores - logsum_ref[pl.ds(head, 1), :])
    grad_p = multiply(value_ref[...], grad, NT)
    delta = jnp.sum(probs * grad_p, axis=0, keepdims=True)
    grad_s = (probs * (grad_p - delta) * scale).astype(jnp.bfloat16)
    grad_query = multiply(key_t_ref[...], grad_s, NN).T
    grad_pairs_ref[:, :HD] += multiply(grad_s, query, NN)
    grad_pairs_ref[:, HD:] += multiply(probs.astype(jnp.bfloat16), grad, NN)
    grad_query_ref[0] = (
        grad_query * cosine_ref[...] - rotate_lanes(grad_query * sine_ref[...])
    ).astype(jnp.bfloat16)


def attend_back(queries, grad, cosine, sine, pairs, code, pos, seg_all, pos_all, logsum, heads):
    rows = queries.shape[1]
    total = pairs.shape[0]
    tile = min(rows, 512)
    query, block, key, value, line, whole, sums = attention_specs(tile, total)
    table = pl.BlockSpec((tile, HD), lambda i, h: (i, 0))
    return pl.pallas_call(
        attend_back_kernel,
        grid=(rows // tile, heads),
        in_specs=[query, block, table, table, key, value, line, line, whole, whole, sums],
        out_specs=[query, pl.BlockSpec((total, 2 * HD), lambda i, h: (0, 0))],
        out_shape=[
            jax.ShapeDtypeStruct((heads // 2, rows, 2 * HD), jnp.bfloat16),
            jax.ShapeDtypeStruct((total, 2 * HD), jnp.float32),
        ],
        scratch_shapes=[
            pltpu.VMEM((total, tile), jnp.float32),
            pltpu.VMEM((HD, total), jnp.bfloat16),
        ],
        compiler_params=pltpu.CompilerParams(vmem_limit_bytes=VMEM_LIMIT),
        cost_estimate=pl.CostEstimate(
            flops=20 * rows * total * HD * heads,
            bytes_accessed=rows * heads * HD * 6,
            transcendentals=rows * total * heads,
        ),
    )(queries, grad, cosine, sine, pairs, pairs, code, pos, seg_all, pos_all, logsum)


def shard_gather_small(piece):
    size = lax.axis_size("shard")
    me = lax.axis_index("shard")
    if size > 4:
        return lax.all_gather(piece, "shard", axis=0, tiled=False)
    parts = [piece] + [
        lax.ppermute(piece, "shard", [(i, (i + k) % size) for i in range(size)])
        for k in range(1, size)
    ]
    whole = jnp.zeros((size,) + piece.shape, piece.dtype)
    for k, part in enumerate(parts):
        whole = lax.dynamic_update_slice(whole, part[None], (lax.rem(me - k + size, size), 0, 0))
    return whole


def body(
    tokens,
    cotangent,
    norm1_gain,
    w_query,
    b_query,
    w_key,
    b_key,
    w_value,
    b_value,
    w_out,
    norm2_gain,
    w_gate,
    w_up,
    w_down,
    parents,
    segment_ids,
    positions,
):
    narrow_dtype = jnp.bfloat16
    rows = tokens.shape[1]
    half = rows // 2
    depth = w_query.shape[0]
    model = tokens.shape[2]
    qwp = w_query.shape[1]
    kwp = w_key.shape[1]
    head_loc = qwp // HD
    ffp = w_gate.shape[1]
    shards = lax.axis_size("shard")
    contexts = lax.axis_size("ctx")
    context = lax.axis_index("ctx")
    core = lax.axis_index("tp")
    inner = qwp + 2 * kwp
    quarter = inner // contexts
    distances = [jnp.bitwise_xor(context, k) for k in range(contexts)]
    bar = lax.optimization_barrier

    def core_half(value):
        return lax.dynamic_slice_in_dim(value, core * half, half)

    def core_order(mine, other):
        low = jnp.where(core == 0, mine, other)
        high = jnp.where(core == 0, other, mine)
        return jnp.concatenate([low, high], axis=0)

    def core_join(value):
        return core_order(value, swap(value, "tp", 1))

    def core_reduce(value):
        mine = lax.dynamic_slice_in_dim(value, core * half, half)
        other = lax.dynamic_slice_in_dim(value, (1 - core) * half, half)
        return mine.astype(jnp.float32) + swap(other.astype(narrow_dtype), "tp", 1).astype(
            jnp.float32
        )

    def tree_gather(value):
        mine = jnp.concatenate(sum(context_gather(value), []), axis=0)
        return jnp.concatenate([mine, swap(mine, "tp", 1)], axis=0)

    def tree_terms(mine, other):
        mine = mine.astype(jnp.float32) + other.astype(jnp.float32)
        return [mine[k * half : (k + 1) * half] for k in range(contexts)]

    def tree_block(value, k):
        count = value.shape[0] // 2
        return core_order(
            value[k * half : (k + 1) * half], value[count + k * half : count + (k + 1) * half]
        )

    def tree_line(line):
        return jnp.concatenate(
            [
                lax.dynamic_slice_in_dim(line, d * rows + side * half, half)
                for side in (core, 1 - core)
                for d in distances
            ]
        )

    first_gain = norm1_gain.astype(jnp.float32)
    second_gain = norm2_gain.astype(jnp.float32)
    source_half = core_half(tokens[0]).astype(jnp.float32)
    first_root_mean = lax.rsqrt(jnp.mean(source_half * source_half, axis=-1, keepdims=True) + EPS)
    first_normalized = source_half * first_root_mean
    first_normed = tree_gather((first_normalized * first_gain).astype(narrow_dtype))

    joined = jnp.concatenate([w_query, w_key, w_value], axis=1)
    quarter_own = lax.dynamic_slice_in_dim(joined, context * quarter, quarter, axis=1)
    columns_all = shard_gather_small(
        jnp.concatenate([quarter_own, joined[:, qwp:]], axis=1)
    ).reshape(model, quarter + 2 * kwp)

    pos_all = tree_line(positions[0])
    cosine_all, sine_all = rope_tables(pos_all)
    first_normed, w_out, parent_line, segment_line, w_gate_late, w_up_late, w_down_late = bar(
        (first_normed, w_out, parents[0], segment_ids[0], w_gate, w_up, w_down)
    )
    seg_all = tree_line(segment_line)
    first_row = context * rows
    seg_own = lax.dynamic_slice_in_dim(segment_line, first_row, rows)
    pos_own = lax.dynamic_slice_in_dim(positions[0], first_row, rows)
    labels = jnp.arange(parents.shape[1], dtype=jnp.int32)

    def parent_of(segment):
        return jnp.sum(jnp.where(segment[:, None] == labels[None], parent_line[None], 0), axis=1)

    above = parent_of(labels)
    code_line = 1 << labels | 1 << above | 1 << parent_of(above)
    code_own = jnp.sum(jnp.where(seg_own[:, None] == labels[None], code_line[None], 0), axis=1)
    mask_lines = (code_own[None], pos_own[None], seg_all[:, None], pos_all[:, None])
    cosine, sine = rope_tables(pos_own)

    lin = jnp.dot(first_normed, columns_all, preferred_element_type=jnp.float32)
    biases = jnp.concatenate([b_query, b_key, b_value]).astype(jnp.float32)

    def turned(value, bias):
        value = (value + bias).reshape(value.shape[0], -1, HD)
        return rope(value, cosine_all, sine_all).reshape(value.shape[0], -1)

    queries_all = turned(
        lin[:, :quarter], lax.dynamic_slice_in_dim(biases, context * quarter, quarter)
    ).astype(narrow_dtype)
    pairs = jnp.concatenate(
        [
            turned(lin[:, quarter : quarter + kwp], biases[qwp : qwp + kwp]),
            lin[:, quarter + kwp :] + biases[qwp + kwp :],
        ],
        axis=1,
    ).astype(narrow_dtype)
    queries = jnp.zeros((contexts, rows, quarter), narrow_dtype)
    exchanged = context_send([tree_block(queries_all, k) for k in range(contexts)])
    for k, block in enumerate(exchanged):
        queries = lax.dynamic_update_slice(queries, block[None], (distances[k], 0, 0))

    part = depth // contexts
    wo_piece = lax.dynamic_slice_in_dim(w_out, context * part, part)
    wo_all = jnp.zeros((shards, contexts, part, qwp), narrow_dtype)
    for k, block in enumerate(context_gather(shard_gather_small(wo_piece))):
        block = jnp.concatenate(block, axis=0)
        wo_all = lax.dynamic_update_slice(wo_all, block[:, None], (0, distances[k], 0, 0))
    wo_all = wo_all.reshape(model, qwp)

    width = -(-ffp // (contexts * 128)) * 128
    first_width = width // 192 * 128
    spans = [(0, first_width), (first_width, width - first_width)]
    padding = ((0, 0), (0, width * contexts - ffp))
    ff_weights = []
    for (offset, size), group in zip(
        spans, ((w_gate, w_up, w_down), (w_gate_late, w_up_late, w_down_late))
    ):
        piece = jnp.concatenate(
            [
                lax.dynamic_slice_in_dim(
                    jnp.pad(w, padding), context * width + offset, size, axis=1
                )
                for w in group
            ],
            axis=1,
        )
        ff_weights.append(lax.all_gather(piece, "shard", axis=0, tiled=True))

    queries, cotangent_late = bar((queries, cotangent))
    gradient_half = core_half(cotangent_late[0])
    tree_gradient = tree_gather(gradient_half)
    mixed_b, logsum = attend(queries, pairs, *mask_lines, head_loc)


    residual = source_half + core_reduce(contract_last(mixed_b, wo_all))
    second_root_mean = lax.rsqrt(jnp.mean(residual * residual, axis=-1, keepdims=True) + EPS)
    second_normalized = residual * second_root_mean
    second_normed = (second_normalized * second_gain).astype(narrow_dtype)
    tree_normed = tree_gather(second_normed)
    tree_normed, quarter_late = bar((tree_normed, columns_all[:, :quarter]))
    quarter_blocks = context_send([quarter_late] * contexts)

    acts, *sums = feed_forward(tree_normed, tree_gradient, ff_weights[0])
    acts, quarter_blocks = bar((acts, quarter_blocks))
    (grads,) = ff_grads(tree_normed, tree_gradient, acts, False)
    grads, late_weights = bar((grads, ff_weights[1]))
    late_acts, *sums = feed_forward(
        tree_normed, tree_gradient, late_weights, tuple(sums)
    )
    (late_grads,) = ff_grads(tree_normed, tree_gradient, late_acts, False)

    def over_shard(value):
        return lax.psum_scatter(
            value.reshape(shards, depth, value.shape[1]), "shard", scatter_dimension=0, tiled=False
        )

    ff_sums = [over_shard(grads)]

    mlp_mine, mlp_other, back_mine, back_other = sums
    back_mine, back_other, late_grads = bar((back_mine, swap(back_other, "tp", 1), late_grads))
    second_normed_gradient = context_sum(tree_terms(back_mine, back_other))
    second_normed_gradient, mlp_mine, mlp_other = bar(
        (second_normed_gradient, mlp_mine, mlp_other)
    )
    mlp = context_sum(tree_terms(mlp_mine, swap(mlp_other, "tp", 1)))
    residual_gradient = gradient_half.astype(jnp.float32) + norm_backward(
        second_normed_gradient, second_normalized, second_root_mean, second_gain
    )
    grad_attn_b = core_join(residual_gradient.astype(narrow_dtype))
    grad_mixed = jnp.dot(grad_attn_b, wo_all, preferred_element_type=jnp.float32).astype(
        narrow_dtype
    )

    groups = qwp // quarter
    grad_wo = contract_first(grad_attn_b, mixed_b).astype(narrow_dtype)
    grad_wo = grad_wo.reshape(shards, contexts, part, qwp)
    grad_wo = [lax.dynamic_index_in_dim(grad_wo, d, axis=1, keepdims=False) for d in distances]
    grad_wo = context_sum(grad_wo).astype(narrow_dtype)
    grad_query, grad_pairs = attend_back(
        queries, grad_mixed, cosine, sine, pairs, *mask_lines, logsum, head_loc
    )
    grad_query, grad_pairs, ff_sums[0] = bar((grad_query, grad_pairs, ff_sums[0]))
    ff_sums.append(over_shard(late_grads))
    grad_pairs, grad_wo, mlp = bar((grad_pairs, grad_wo, mlp))
    grad_pairs = context_sum([tree_block(grad_pairs, k) for k in range(contexts)])
    grad_keys = rope_back(grad_pairs[:, :kwp].reshape(rows, -1, HD), cosine, sine)
    grad_pairs = jnp.concatenate(
        [grad_keys.reshape(rows, kwp), grad_pairs[:, kwp:]], axis=1
    ).astype(narrow_dtype)
    grad_quarters = jnp.concatenate([grad_query, grad_pairs[None]], axis=0)
    relative_grads = [
        lax.dynamic_index_in_dim(grad_quarters, d, axis=0, keepdims=False) for d in distances
    ]
    exchanged = context_send(relative_grads)
    exchanged, *ff_sums = bar((exchanged, *ff_sums))
    ff_grads_own = jnp.concatenate(ff_sums, axis=1)
    ff_near = context_gather_start(ff_grads_own)
    normed_gradient = sum(
        contract_last(grads, block) for grads, block in zip(relative_grads, quarter_blocks)
    )
    first_normed_gradient = core_reduce(normed_gradient)
    source_gradient = (
        residual_gradient
        + norm_backward(first_normed_gradient, first_normalized, first_root_mean, first_gain)
    ).astype(narrow_dtype)
    source_gradient = core_join(source_gradient)
    small = jnp.concatenate(
        [
            jnp.sum(first_normed_gradient * first_normalized, axis=0),
            jnp.sum(second_normed_gradient * second_normalized, axis=0),
        ]
    )
    small = small + swap(small, "tp", 1)
    small = jnp.concatenate([small, jnp.sum(grad_quarters.astype(jnp.float32), axis=1).reshape(-1)])

    def packed(value):
        value = value.reshape(-1, quarter)
        high = value.astype(narrow_dtype)
        return high, (value - high.astype(jnp.float32)).astype(narrow_dtype)

    def unpacked(value):
        count = value.shape[-2] // 2
        value = value.astype(jnp.float32)
        return value[..., :count, :] + value[..., count:, :]

    me = lax.axis_index("shard")
    terms = attention_terms(first_normed, exchanged, grad_wo, small.reshape(-1, quarter), core)
    if shards > 4:
        received = [lax.all_to_all(terms, "shard", 0, 0)[k] for k in range(shards)]
    else:
        received = [lax.dynamic_index_in_dim(terms, me, axis=0, keepdims=False)]
        for k in range(1, shards):
            received.append(
                lax.ppermute(
                    lax.dynamic_index_in_dim(terms, lax.rem(me + k, shards), keepdims=False),
                    "shard",
                    [(i, (i + k) % shards) for i in range(shards)],
                )
            )
    received, ff_near = bar((received, ff_near))
    ff_blocks = context_gather_end(ff_grads_own, *ff_near)
    output = core_join((residual + mlp).astype(narrow_dtype))
    count = depth + groups * part
    weight_sums = sum(value[:count].astype(jnp.float32) for value in received).astype(narrow_dtype)
    small = sum(unpacked(value[count:]) for value in received)
    blocks = context_send([jnp.concatenate([weight_sums, *packed(small)], axis=0)] * contexts)
    small = sum(unpacked(block[count:]) for block in blocks).reshape(-1)
    grad_wq, grad_wk, grad_wv, grad_wo = place_attention(blocks, depth, part, qwp, kwp, context)

    ff_blocks, output, source_gradient, small, grad_wq = bar(
        (ff_blocks, output, source_gradient, small, grad_wq)
    )
    grad_wg, grad_wu, grad_wd = spread(ff_blocks, tuple(spans), width, ffp, context)

    edges = [0, model, 2 * model, 2 * model + qwp, 2 * model + qwp + kwp, small.shape[0]]
    sums = [small[edges[i] : edges[i + 1]] for i in range(5)]
    return (
        output[None],
        source_gradient[None],
        sums[0],
        grad_wq,
        sums[2],
        grad_wk,
        sums[3],
        grad_wv,
        sums[4],
        grad_wo,
        sums[1],
        grad_wg,
        grad_wu,
        grad_wd,
    )


def solution(mesh):
    return jax.shard_map(
        body,
        mesh=mesh,
        in_specs=(
            P("shard", "ctx", None),
            P("shard", "ctx", None),
            P(),
            P("shard", "tp"),
            P("tp"),
            P("shard", "tp"),
            P("tp"),
            P("shard", "tp"),
            P("tp"),
            P("shard", "tp"),
            P(),
            P("shard", "tp"),
            P("shard", "tp"),
            P("shard", "tp"),
            P("shard", None),
            P("shard", None),
            P("shard", None),
        ),
        out_specs=(
            P("shard", "ctx", None),
            P("shard", "ctx", None),
            P(),
            P("shard", "tp"),
            P("tp"),
            P("shard", "tp"),
            P("tp"),
            P("shard", "tp"),
            P("tp"),
            P("shard", "tp"),
            P(),
            P("shard", "tp"),
            P("shard", "tp"),
            P("shard", "tp"),
        ),
        check_vma=False,
    )
```

```python
import functools

import jax
import jax.numpy as jnp
from jax import lax
from jax.experimental import pallas as pl
from jax.experimental.pallas import tpu as pltpu
from jax.sharding import PartitionSpec as P

HD = 128


EPS = 1e-06
THETA = 1000000.0
NEG = -1e30


def rope_tables(pos):
    inverse = THETA ** (-jnp.arange(0, HD, 2, dtype=jnp.float32) / HD)
    angle = pos.astype(jnp.float32)[:, None] * inverse[None, :]
    return (
        jnp.concatenate([jnp.cos(angle)] * 2, axis=-1),
        jnp.concatenate([jnp.sin(angle)] * 2, axis=-1),
    )


def rotate_half(v):
    half = v.shape[-1] // 2
    return jnp.concatenate([-v[..., half:], v[..., :half]], axis=-1)


def rope(v, cosine, sine):
    return v * cosine[:, None, :] + rotate_half(v) * sine[:, None, :]


def rope_back(grad, cosine, sine):
    return grad * cosine[:, None, :] - rotate_half(grad * sine[:, None, :])


def contract_last(left, right):
    return lax.dot_general(
        left, right, (((1,), (1,)), ((), ())), preferred_element_type=jnp.float32
    )


def contract_first(left, right):
    return lax.dot_general(
        left, right, (((0,), (0,)), ((), ())), preferred_element_type=jnp.float32
    )


def norm_backward(normed_gradient, normalized_input, root_mean_square, norm_gain):
    scaled_rows = normed_gradient * norm_gain
    return root_mean_square * (
        scaled_rows
        - normalized_input * jnp.mean(scaled_rows * normalized_input, axis=-1, keepdims=True)
    )


def swap(value, axis, distance):
    size = lax.axis_size(axis)
    return lax.ppermute(value, axis, [(i, i ^ distance) for i in range(size)])


def after(value, *others):
    return lax.optimization_barrier((value, *others))[0]


def context_gather_start(value):
    return swap(value, "ctx", 1), swap(value, "ctx", 2)


def context_gather_end(value, first, second):
    half = value.shape[0] // 2
    far_low = swap(first[:half], "ctx", 2)
    far_high = swap(second[half:], "ctx", 1)
    return [[value], [first], [second], [far_low, far_high]]


def context_gather(value):
    return context_gather_end(value, *context_gather_start(value))


def context_send(blocks):
    return [blocks[0]] + [swap(blocks[k], "ctx", k) for k in range(1, len(blocks))]


def context_sum_large(blocks):
    half = blocks[0].shape[0] // 2
    narrow = [block.astype(jnp.bfloat16) for block in blocks]
    far_low = swap(narrow[3][:half], "ctx", 1)
    far_high = swap(narrow[3][half:], "ctx", 2)
    low = (blocks[2][:half].astype(jnp.float32) + far_low.astype(jnp.float32)).astype(jnp.bfloat16)
    high = (blocks[1][half:].astype(jnp.float32) + far_high.astype(jnp.float32)).astype(jnp.bfloat16)
    first = swap(jnp.concatenate([narrow[1][:half], high], axis=0), "ctx", 1)
    second = swap(jnp.concatenate([low, narrow[2][half:]], axis=0), "ctx", 2)
    return blocks[0].astype(jnp.float32) + first.astype(jnp.float32) + second.astype(jnp.float32)


def context_sum(blocks):
    received = context_send([block.astype(jnp.bfloat16) for block in blocks])
    return sum(block.astype(jnp.float32) for block in (blocks[0], *received[1:]))


def spread_kernel(spans, width, total, context_ref, *refs):
    *blocks, gate_ref, up_ref, down_ref = refs
    context = context_ref[0]
    for distance, ref in enumerate(blocks):
        start = jnp.bitwise_xor(context, distance) * width
        base = 0
        for offset, columns in spans:
            for out in (gate_ref, up_ref, down_ref):
                for piece in range(0, columns, 128):
                    place = start + offset + piece

                    @pl.when(place < total)
                    def _():
                        out[:, pl.ds(pl.multiple_of(place, 128), 128)] = ref[
                            :, pl.ds(base + piece, 128)
                        ].astype(jnp.float32)

                base += columns


def spread(blocks, spans, width, total, context):
    rows = blocks[0].shape[0]
    tile = 48 if rows % 48 == 0 else rows
    return pl.pallas_call(
        functools.partial(spread_kernel, spans, width, total),
        grid=(rows // tile,),
        in_specs=[pl.BlockSpec(memory_space=pltpu.SMEM)]
        + [pl.BlockSpec((tile, block.shape[1]), lambda i: (i, 0)) for block in blocks],
        out_specs=[pl.BlockSpec((tile, total), lambda i: (i, 0))] * 3,
        out_shape=[jax.ShapeDtypeStruct((rows, total), jnp.float32)] * 3,
        compiler_params=pltpu.CompilerParams(vmem_limit_bytes=40 * 1024 * 1024),
    )(context.reshape(1), *blocks)


def spread_far_kernel(spans, place_ref, low_ref, high_ref, *refs):
    outs = refs[3:]
    late = pl.program_id(0) >= pl.num_programs(0) // 2
    for side, ref in enumerate((low_ref, high_ref)):

        @pl.when(late == (side == 1))
        def _():
            base = 0
            for offset, columns in spans:
                for out in outs:
                    out[:, offset : offset + columns] = ref[:, base : base + columns].astype(
                        jnp.float32
                    )
                    base += columns


def spread_far(low, high, wholes, spans, width, place):
    rows, total = wholes[0].shape
    steps = 1
    tile = rows // 2
    while tile % 2 == 0 and tile > 96:
        tile //= 2
        steps *= 2
    grid_spec = pltpu.PrefetchScalarGridSpec(
        num_scalar_prefetch=1,
        grid=(2 * steps,),
        in_specs=[
            pl.BlockSpec((tile, low.shape[1]), lambda i, p: (jnp.minimum(i, steps - 1), 0)),
            pl.BlockSpec((tile, low.shape[1]), lambda i, p: (jnp.maximum(i - steps, 0), 0)),
        ]
        + [pl.BlockSpec(memory_space=pl.ANY)] * 3,
        out_specs=[pl.BlockSpec((tile, width), lambda i, p: (i, p[0]))] * 3,
    )
    return pl.pallas_call(
        functools.partial(spread_far_kernel, spans),
        grid_spec=grid_spec,
        out_shape=[jax.ShapeDtypeStruct((rows, total), jnp.float32)] * 3,
        input_output_aliases={3: 0, 4: 1, 5: 2},
        compiler_params=pltpu.CompilerParams(vmem_limit_bytes=40 * 1024 * 1024),
    )(place.reshape(1), low, high, *wholes)


def place_kernel(count, part, context_ref, *refs):
    query_ref, key_ref, value_ref, out_ref = refs[count:]
    context = context_ref[0]
    depth = query_ref.shape[0]
    quarter = refs[0].shape[1]
    whole = query_ref.shape[1] // quarter
    keys = key_ref.shape[1]
    for k in range(count):
        place = jnp.bitwise_xor(context, k)
        block = refs[k][:depth].astype(jnp.float32)

        @pl.when(place < whole)
        def _():
            query_ref[:, pl.ds(pl.multiple_of(place * quarter, 128), quarter)] = block

        @pl.when(place == whole)
        def _():
            key_ref[...] = block[:, :keys]
            value_ref[...] = block[:, keys:]

        row = pl.multiple_of(place * part, 8)
        for g in range(whole):
            start = depth + g * part
            out_ref[pl.ds(row, part), g * quarter : (g + 1) * quarter] = refs[k][
                start : start + part
            ].astype(jnp.float32)


def place_attention(blocks, depth, part, query_width, key_width, context):
    count = len(blocks)
    widths = (query_width, key_width, key_width, query_width)
    vmem = pl.BlockSpec(memory_space=pltpu.VMEM)
    return pl.pallas_call(
        functools.partial(place_kernel, count, part),
        in_specs=[pl.BlockSpec(memory_space=pltpu.SMEM)] + [vmem] * count,
        out_specs=[vmem] * 4,
        out_shape=[jax.ShapeDtypeStruct((depth, width), jnp.float32) for width in widths],
        compiler_params=pltpu.CompilerParams(vmem_limit_bytes=VMEM_LIMIT),
    )(context.reshape(1), *blocks)


NT = (((1,), (1,)), ((), ()))
NN = (((1,), (0,)), ((), ()))
TN = (((0,), (0,)), ((), ()))
VMEM_LIMIT = 56 * 1024 * 1024


def multiply(left, right, dims):
    return lax.dot_general(left, right, dims, preferred_element_type=jnp.float32)


def terms_kernel(count, core_ref, normed_ref, *refs):
    blocks, (wo_ref, small_ref, out_ref, rows_ref) = refs[:count], refs[count:]
    core = core_ref[0]
    half = blocks[0].shape[0] // 2
    depth = normed_ref.shape[1]
    part = wo_ref.shape[1]
    quarter = out_ref.shape[2]

    @pl.when(pl.program_id(0) == 0)
    def _():
        for side in range(2):
            start = pl.multiple_of((core if side == 0 else 1 - core) * half, half)
            for k, block in enumerate(blocks):
                place = (side * count + k) * half
                rows_ref[place : place + half] = block[pl.ds(start, half), :]

    out_ref[0, :depth] = multiply(normed_ref[...], rows_ref[...], TN).astype(jnp.bfloat16)
    place = depth
    for column in range(0, wo_ref.shape[2], quarter):
        out_ref[0, place : place + part] = wo_ref[0, :, column : column + quarter]
        place += part
    size = small_ref.shape[0]
    high = small_ref[...].astype(jnp.bfloat16)
    out_ref[0, place : place + size] = high
    out_ref[0, place + size :] = (small_ref[...] - high.astype(jnp.float32)).astype(jnp.bfloat16)


def attention_terms(normed, blocks, grad_wo, small, core):
    rows, model = normed.shape
    shards, part, width = grad_wo.shape
    depth = model // shards
    quarter = blocks[0].shape[1]
    count = depth + part * (width // quarter) + 2 * small.shape[0]
    if depth % 128:
        half = blocks[0].shape[0] // 2
        ordered = [
            lax.dynamic_slice_in_dim(block, side * half, half)
            for side in (core, 1 - core)
            for block in blocks
        ]
        columns = contract_first(normed, jnp.concatenate(ordered, axis=0)).astype(jnp.bfloat16)
        high = small.astype(jnp.bfloat16)
        low = (small - high.astype(jnp.float32)).astype(jnp.bfloat16)
        return jnp.concatenate(
            [columns.reshape(shards, depth, quarter)]
            + [grad_wo[:, :, i : i + quarter] for i in range(0, width, quarter)]
            + [jnp.broadcast_to(value, (shards,) + value.shape) for value in (high, low)],
            axis=1,
        )
    whole = lambda value: pl.BlockSpec(value.shape, lambda i: (0, 0))
    return pl.pallas_call(
        functools.partial(terms_kernel, len(blocks)),
        grid=(shards,),
        in_specs=[
            pl.BlockSpec(memory_space=pltpu.SMEM),
            pl.BlockSpec((rows, depth), lambda i: (0, i)),
            *(whole(block) for block in blocks),
            pl.BlockSpec((1, part, width), lambda i: (i, 0, 0)),
            whole(small),
        ],
        out_specs=pl.BlockSpec((1, count, quarter), lambda i: (i, 0, 0)),
        out_shape=jax.ShapeDtypeStruct((shards, count, quarter), jnp.bfloat16),
        scratch_shapes=[pltpu.VMEM((rows, quarter), jnp.bfloat16)],
        compiler_params=pltpu.CompilerParams(vmem_limit_bytes=VMEM_LIMIT),
        cost_estimate=pl.CostEstimate(
            flops=2 * rows * model * quarter,
            bytes_accessed=2 * (rows * model + rows * quarter + shards * count * quarter),
            transcendentals=0,
        ),
    )(core.reshape(1), normed, *blocks, grad_wo, small)


def ff_kernel(size, first, normed_ref, gradient_ref, weight_ref, *refs):
    inputs, (acts_ref, *outs) = ((), refs) if first else (refs[:4], refs[4:])
    normed = normed_ref[...]
    gate_up = multiply(normed, weight_ref[:, : 2 * size], NN)
    gate, up = gate_up[:, :size], gate_up[:, size:]
    grad_act = multiply(gradient_ref[...], weight_ref[:, 2 * size :], NN)
    sigma = 1.0 / (1.0 + jnp.exp(-gate))
    silu = gate * sigma
    act = (silu * up).astype(jnp.bfloat16)
    grad_up = (grad_act * silu).astype(jnp.bfloat16)
    grad_gate = (grad_act * up * (sigma * (1.0 + gate * (1.0 - sigma)))).astype(jnp.bfloat16)
    acts_ref[:, :size] = grad_gate
    acts_ref[:, size : 2 * size] = grad_up
    acts_ref[:, 2 * size :] = act
    back = multiply(grad_gate, weight_ref[:, :size], NT) + multiply(
        grad_up, weight_ref[:, size : 2 * size], NT
    )
    mlp = multiply(act, weight_ref[:, 2 * size :], NT)
    late = pl.program_id(0) >= pl.num_programs(0) // 2
    for side in range(2):

        @pl.when(late == (side == 1))
        def _():
            for which, value in enumerate((mlp, back)):
                if not first:
                    value = value + inputs[2 * which + side][...].astype(jnp.float32)
                outs[2 * which + side][...] = value.astype(jnp.bfloat16)


def feed_forward(normed, gradient, weights, previous=(), tile=256):
    rows, model = normed.shape
    columns = weights.shape[1]
    steps = rows // tile // 2
    row = pl.BlockSpec((tile, model), lambda i: (i, 0))
    sides = [
        pl.BlockSpec((tile, model), lambda i: (jnp.minimum(i, steps - 1), 0)),
        pl.BlockSpec((tile, model), lambda i: (jnp.maximum(i - steps, 0), 0)),
    ] * 2
    return pl.pallas_call(
        functools.partial(ff_kernel, columns // 3, not previous),
        grid=(rows // tile,),
        in_specs=[row, row, pl.BlockSpec((model, columns), lambda i: (0, 0))]
        + sides[: len(previous)],
        out_specs=[pl.BlockSpec((tile, columns), lambda i: (i, 0))] + sides,
        out_shape=[jax.ShapeDtypeStruct((rows, columns), jnp.bfloat16)]
        + [jax.ShapeDtypeStruct((rows // 2, model), jnp.bfloat16)] * 4,
        compiler_params=pltpu.CompilerParams(vmem_limit_bytes=VMEM_LIMIT),
        cost_estimate=pl.CostEstimate(
            flops=4 * rows * model * columns,
            bytes_accessed=2 * (rows * columns + 4 * rows * model + model * columns),
            transcendentals=rows * columns // 3,
        ),
    )(normed, gradient, weights, *previous)


def ff_grads_kernel(size, normed_ref, gradient_ref, acts_ref, *outs):
    gate_up = multiply(normed_ref[...], acts_ref[:, : 2 * size], TN).astype(jnp.bfloat16)
    down = multiply(gradient_ref[...], acts_ref[:, 2 * size :], TN).astype(jnp.bfloat16)
    if len(outs) == 2:
        outs[0][...] = gate_up
        outs[1][...] = down
    else:
        outs[0][:, : 2 * size] = gate_up
        outs[0][:, 2 * size :] = down


def ff_grads(normed, gradient, acts, split, tile=384):
    rows, model = normed.shape
    columns = acts.shape[1]
    widths = (columns // 3 * 2, columns // 3) if split else (columns,)
    column = pl.BlockSpec((rows, tile), lambda i: (0, i))
    return pl.pallas_call(
        functools.partial(ff_grads_kernel, columns // 3),
        grid=(model // tile,),
        in_specs=[column, column, pl.BlockSpec((rows, columns), lambda i: (0, 0))],
        out_specs=[pl.BlockSpec((tile, width), lambda i: (i, 0)) for width in widths],
        out_shape=[jax.ShapeDtypeStruct((model, width), jnp.bfloat16) for width in widths],
        compiler_params=pltpu.CompilerParams(vmem_limit_bytes=VMEM_LIMIT),
        cost_estimate=pl.CostEstimate(
            flops=2 * rows * model * columns,
            bytes_accessed=2 * (rows * columns + 2 * rows * model + model * columns),
            transcendentals=0,
        ),
    )(normed, gradient, acts)


def rotate_lanes(value):
    half = HD // 2
    rolled = pltpu.roll(value, half, 1)
    lane = lax.broadcasted_iota(jnp.int32, value.shape, 1)
    return jnp.where(lane < half, -rolled, rolled)


def set_mask(mask_ref, code_ref, pos_ref, seg_all_ref, pos_all_ref):
    allowed = (jnp.right_shift(code_ref[...], seg_all_ref[...]) & 1 == 1) & (
        pos_all_ref[...] <= pos_ref[...]
    )
    mask_ref[...] = jnp.where(allowed, 0.0, NEG)


def attend_kernel(
    query_ref,
    key_ref,
    value_ref,
    code_ref,
    pos_ref,
    seg_all_ref,
    pos_all_ref,
    mixed_ref,
    logsum_ref,
    mask_ref,
    value_t_ref,
):
    head = pl.program_id(1)

    @pl.when(head == 0)
    def _():
        set_mask(mask_ref, code_ref, pos_ref, seg_all_ref, pos_all_ref)
        value_t_ref[...] = value_ref[...].T

    scores = multiply(key_ref[...], query_ref[0], NT) * (HD ** (-0.5)) + mask_ref[...]
    top = jnp.max(scores, axis=0, keepdims=True)
    expo = jnp.exp(scores - top)
    total = jnp.sum(expo, axis=0, keepdims=True)
    mixed = multiply(value_t_ref[...], expo.astype(jnp.bfloat16), NN) * (1.0 / total)
    mixed_ref[...] = mixed.T.astype(jnp.bfloat16)
    logsum_ref[pl.ds(head, 1), :] = top + jnp.log(total)


def attention_specs(tile, total):
    query = pl.BlockSpec((1, tile, HD), lambda i, h: (h // 2, i, h % 2))
    block = pl.BlockSpec((tile, HD), lambda i, h: (i, h))
    key = pl.BlockSpec((total, HD), lambda i, h: (0, 0))
    value = pl.BlockSpec((total, HD), lambda i, h: (0, 1))
    line = pl.BlockSpec((1, tile), lambda i, h: (0, i))
    whole = pl.BlockSpec((total, 1), lambda i, h: (0, 0))
    logsum = pl.BlockSpec((8, tile), lambda i, h: (0, i))
    return query, block, key, value, line, whole, logsum


def attend(queries, pairs, code, pos, seg_all, pos_all, heads):
    rows = queries.shape[1]
    total = pairs.shape[0]
    tile = min(rows, 512)
    query, block, key, value, line, whole, logsum = attention_specs(tile, total)
    return pl.pallas_call(
        attend_kernel,
        grid=(rows // tile, heads),
        in_specs=[query, key, value, line, line, whole, whole],
        out_specs=[block, logsum],
        out_shape=[
            jax.ShapeDtypeStruct((rows, heads * HD), jnp.bfloat16),
            jax.ShapeDtypeStruct((8, rows), jnp.float32),
        ],
        scratch_shapes=[
            pltpu.VMEM((total, tile), jnp.float32),
            pltpu.VMEM((HD, total), jnp.bfloat16),
        ],
        compiler_params=pltpu.CompilerParams(vmem_limit_bytes=VMEM_LIMIT),
        cost_estimate=pl.CostEstimate(
            flops=8 * rows * total * HD * heads,
            bytes_accessed=rows * heads * HD * 6,
            transcendentals=rows * total * heads,
        ),
    )(queries, pairs, pairs, code, pos, seg_all, pos_all)


def attend_back_kernel(
    query_ref,
    grad_ref,
    cosine_ref,
    sine_ref,
    key_ref,
    value_ref,
    code_ref,
    pos_ref,
    seg_all_ref,
    pos_all_ref,
    logsum_ref,
    grad_query_ref,
    grad_pairs_ref,
    mask_ref,
    key_t_ref,
):
    head = pl.program_id(1)

    @pl.when(head == 0)
    def _():
        set_mask(mask_ref, code_ref, pos_ref, seg_all_ref, pos_all_ref)
        key_t_ref[...] = key_ref[...].T

    @pl.when((head == 0) & (pl.program_id(0) == 0))
    def _():
        grad_pairs_ref[...] = jnp.zeros_like(grad_pairs_ref)

    scale = HD ** (-0.5)
    query = query_ref[0]
    grad = grad_ref[...]
    scores = multiply(key_ref[...], query, NT) * scale + mask_ref[...]
    probs = jnp.exp(scores - logsum_ref[pl.ds(head, 1), :])
    grad_p = multiply(value_ref[...], grad, NT)
    delta = jnp.sum(probs * grad_p, axis=0, keepdims=True)
    grad_s = (probs * (grad_p - delta) * scale).astype(jnp.bfloat16)
    grad_query = multiply(key_t_ref[...], grad_s, NN).T
    grad_pairs_ref[:, :HD] += multiply(grad_s, query, NN)
    grad_pairs_ref[:, HD:] += multiply(probs.astype(jnp.bfloat16), grad, NN)
    grad_query_ref[0] = (
        grad_query * cosine_ref[...] - rotate_lanes(grad_query * sine_ref[...])
    ).astype(jnp.bfloat16)


def attend_back(queries, grad, cosine, sine, pairs, code, pos, seg_all, pos_all, logsum, heads):
    rows = queries.shape[1]
    total = pairs.shape[0]
    tile = min(rows, 512)
    query, block, key, value, line, whole, sums = attention_specs(tile, total)
    table = pl.BlockSpec((tile, HD), lambda i, h: (i, 0))
    return pl.pallas_call(
        attend_back_kernel,
        grid=(rows // tile, heads),
        in_specs=[query, block, table, table, key, value, line, line, whole, whole, sums],
        out_specs=[query, pl.BlockSpec((total, 2 * HD), lambda i, h: (0, 0))],
        out_shape=[
            jax.ShapeDtypeStruct((heads // 2, rows, 2 * HD), jnp.bfloat16),
            jax.ShapeDtypeStruct((total, 2 * HD), jnp.float32),
        ],
        scratch_shapes=[
            pltpu.VMEM((total, tile), jnp.float32),
            pltpu.VMEM((HD, total), jnp.bfloat16),
        ],
        compiler_params=pltpu.CompilerParams(vmem_limit_bytes=VMEM_LIMIT),
        cost_estimate=pl.CostEstimate(
            flops=20 * rows * total * HD * heads,
            bytes_accessed=rows * heads * HD * 6,
            transcendentals=rows * total * heads,
        ),
    )(queries, grad, cosine, sine, pairs, pairs, code, pos, seg_all, pos_all, logsum)


def shard_gather_small(piece):
    size = lax.axis_size("shard")
    me = lax.axis_index("shard")
    if size > 4:
        return lax.all_gather(piece, "shard", axis=0, tiled=False)
    parts = [piece] + [
        lax.ppermute(piece, "shard", [(i, (i + k) % size) for i in range(size)])
        for k in range(1, size)
    ]
    whole = jnp.zeros((size,) + piece.shape, piece.dtype)
    for k, part in enumerate(parts):
        whole = lax.dynamic_update_slice(whole, part[None], (lax.rem(me - k + size, size), 0, 0))
    return whole


def body(
    tokens,
    cotangent,
    norm1_gain,
    w_query,
    b_query,
    w_key,
    b_key,
    w_value,
    b_value,
    w_out,
    norm2_gain,
    w_gate,
    w_up,
    w_down,
    parents,
    segment_ids,
    positions,
):
    narrow_dtype = jnp.bfloat16
    rows = tokens.shape[1]
    half = rows // 2
    depth = w_query.shape[0]
    model = tokens.shape[2]
    qwp = w_query.shape[1]
    kwp = w_key.shape[1]
    head_loc = qwp // HD
    ffp = w_gate.shape[1]
    shards = lax.axis_size("shard")
    contexts = lax.axis_size("ctx")
    context = lax.axis_index("ctx")
    core = lax.axis_index("tp")
    inner = qwp + 2 * kwp
    quarter = inner // contexts
    distances = [jnp.bitwise_xor(context, k) for k in range(contexts)]
    bar = lax.optimization_barrier

    def core_half(value):
        return lax.dynamic_slice_in_dim(value, core * half, half)

    def core_order(mine, other):
        low = jnp.where(core == 0, mine, other)
        high = jnp.where(core == 0, other, mine)
        return jnp.concatenate([low, high], axis=0)

    def core_join(value):
        return core_order(value, swap(value, "tp", 1))

    def core_reduce(value):
        mine = lax.dynamic_slice_in_dim(value, core * half, half)
        other = lax.dynamic_slice_in_dim(value, (1 - core) * half, half)
        return mine.astype(jnp.float32) + swap(other.astype(narrow_dtype), "tp", 1).astype(
            jnp.float32
        )

    def tree_gather(value):
        mine = jnp.concatenate(sum(context_gather(value), []), axis=0)
        return jnp.concatenate([mine, swap(mine, "tp", 1)], axis=0)

    def tree_terms(mine, other):
        mine = mine.astype(jnp.float32) + other.astype(jnp.float32)
        return [mine[k * half : (k + 1) * half] for k in range(contexts)]

    def tree_block(value, k):
        count = value.shape[0] // 2
        return core_order(
            value[k * half : (k + 1) * half], value[count + k * half : count + (k + 1) * half]
        )

    def tree_line(line):
        return jnp.concatenate(
            [
                lax.dynamic_slice_in_dim(line, d * rows + side * half, half)
                for side in (core, 1 - core)
                for d in distances
            ]
        )

    first_gain = norm1_gain.astype(jnp.float32)
    second_gain = norm2_gain.astype(jnp.float32)
    source_half = core_half(tokens[0]).astype(jnp.float32)
    first_root_mean = lax.rsqrt(jnp.mean(source_half * source_half, axis=-1, keepdims=True) + EPS)
    first_normalized = source_half * first_root_mean
    first_normed = tree_gather((first_normalized * first_gain).astype(narrow_dtype))

    joined = jnp.concatenate([w_query, w_key, w_value], axis=1)
    quarter_own = lax.dynamic_slice_in_dim(joined, context * quarter, quarter, axis=1)
    columns_all = shard_gather_small(
        jnp.concatenate([quarter_own, joined[:, qwp:]], axis=1)
    ).reshape(model, quarter + 2 * kwp)

    pos_all = tree_line(positions[0])
    cosine_all, sine_all = rope_tables(pos_all)
    first_normed, w_out, parent_line, segment_line, w_gate_late, w_up_late, w_down_late = bar(
        (first_normed, w_out, parents[0], segment_ids[0], w_gate, w_up, w_down)
    )
    seg_all = tree_line(segment_line)
    first_row = context * rows
    seg_own = lax.dynamic_slice_in_dim(segment_line, first_row, rows)
    pos_own = lax.dynamic_slice_in_dim(positions[0], first_row, rows)
    labels = jnp.arange(parents.shape[1], dtype=jnp.int32)

    def parent_of(segment):
        return jnp.sum(jnp.where(segment[:, None] == labels[None], parent_line[None], 0), axis=1)

    above = parent_of(labels)
    code_line = 1 << labels | 1 << above | 1 << parent_of(above)
    code_own = jnp.sum(jnp.where(seg_own[:, None] == labels[None], code_line[None], 0), axis=1)
    mask_lines = (code_own[None], pos_own[None], seg_all[:, None], pos_all[:, None])
    cosine, sine = rope_tables(pos_own)

    lin = jnp.dot(first_normed, columns_all, preferred_element_type=jnp.float32)
    biases = jnp.concatenate([b_query, b_key, b_value]).astype(jnp.float32)

    def turned(value, bias):
        value = (value + bias).reshape(value.shape[0], -1, HD)
        return rope(value, cosine_all, sine_all).reshape(value.shape[0], -1)

    queries_all = turned(
        lin[:, :quarter], lax.dynamic_slice_in_dim(biases, context * quarter, quarter)
    ).astype(narrow_dtype)
    pairs = jnp.concatenate(
        [
            turned(lin[:, quarter : quarter + kwp], biases[qwp : qwp + kwp]),
            lin[:, quarter + kwp :] + biases[qwp + kwp :],
        ],
        axis=1,
    ).astype(narrow_dtype)
    queries = jnp.zeros((contexts, rows, quarter), narrow_dtype)
    exchanged = context_send([tree_block(queries_all, k) for k in range(contexts)])
    for k, block in enumerate(exchanged):
        queries = lax.dynamic_update_slice(queries, block[None], (distances[k], 0, 0))

    part = depth // contexts
    wo_piece = lax.dynamic_slice_in_dim(w_out, context * part, part)
    wo_all = jnp.zeros((shards, contexts, part, qwp), narrow_dtype)
    for k, block in enumerate(context_gather(shard_gather_small(wo_piece))):
        block = jnp.concatenate(block, axis=0)
        wo_all = lax.dynamic_update_slice(wo_all, block[:, None], (0, distances[k], 0, 0))
    wo_all = wo_all.reshape(model, qwp)

    width = -(-ffp // (contexts * 128)) * 128
    first_width = width // 192 * 128
    spans = [(0, first_width), (first_width, width - first_width)]
    padding = ((0, 0), (0, width * contexts - ffp))
    ff_weights = []
    for (offset, size), group in zip(
        spans, ((w_gate, w_up, w_down), (w_gate_late, w_up_late, w_down_late))
    ):
        piece = jnp.concatenate(
            [
                lax.dynamic_slice_in_dim(
                    jnp.pad(w, padding), context * width + offset, size, axis=1
                )
                for w in group
            ],
            axis=1,
        )
        ff_weights.append(lax.all_gather(piece, "shard", axis=0, tiled=True))

    queries, cotangent_late = bar((queries, cotangent))
    gradient_half = core_half(cotangent_late[0])
    tree_gradient = tree_gather(gradient_half)
    mixed_b, logsum = attend(queries, pairs, *mask_lines, head_loc)


    residual = source_half + core_reduce(contract_last(mixed_b, wo_all))
    second_root_mean = lax.rsqrt(jnp.mean(residual * residual, axis=-1, keepdims=True) + EPS)
    second_normalized = residual * second_root_mean
    second_normed = (second_normalized * second_gain).astype(narrow_dtype)
    tree_normed = tree_gather(second_normed)
    tree_normed, quarter_late = bar((tree_normed, columns_all[:, :quarter]))
    quarter_blocks = context_send([quarter_late] * contexts)

    acts, *sums = feed_forward(tree_normed, tree_gradient, ff_weights[0])
    acts, quarter_blocks = bar((acts, quarter_blocks))
    (grads,) = ff_grads(tree_normed, tree_gradient, acts, False)
    grads, late_weights = bar((grads, ff_weights[1]))
    late_acts, *sums = feed_forward(
        tree_normed, tree_gradient, late_weights, tuple(sums)
    )
    (late_grads,) = ff_grads(tree_normed, tree_gradient, late_acts, False)

    def over_shard(value):
        return lax.psum_scatter(
            value.reshape(shards, depth, value.shape[1]), "shard", scatter_dimension=0, tiled=False
        )

    ff_sums = [over_shard(grads)]

    mlp_mine, mlp_other, back_mine, back_other = sums
    back_mine, back_other, late_grads = bar((back_mine, swap(back_other, "tp", 1), late_grads))
    second_normed_gradient = context_sum_large(tree_terms(back_mine, back_other))
    second_normed_gradient, mlp_mine, mlp_other = bar(
        (second_normed_gradient, mlp_mine, mlp_other)
    )
    mlp = context_sum(tree_terms(mlp_mine, swap(mlp_other, "tp", 1)))
    residual_gradient = gradient_half.astype(jnp.float32) + norm_backward(
        second_normed_gradient, second_normalized, second_root_mean, second_gain
    )
    grad_attn_b = core_join(residual_gradient.astype(narrow_dtype))
    grad_mixed = jnp.dot(grad_attn_b, wo_all, preferred_element_type=jnp.float32).astype(
        narrow_dtype
    )

    groups = qwp // quarter
    grad_wo = contract_first(grad_attn_b, mixed_b).astype(narrow_dtype)
    grad_wo = grad_wo.reshape(shards, contexts, part, qwp)
    grad_wo = [lax.dynamic_index_in_dim(grad_wo, d, axis=1, keepdims=False) for d in distances]
    grad_wo = context_sum(grad_wo).astype(narrow_dtype)
    grad_query, grad_pairs = attend_back(
        queries, grad_mixed, cosine, sine, pairs, *mask_lines, logsum, head_loc
    )
    grad_query, grad_pairs, ff_sums[0] = bar((grad_query, grad_pairs, ff_sums[0]))
    ff_sums.append(over_shard(late_grads))
    grad_pairs, mlp = bar((grad_pairs, mlp))
    grad_pairs = context_sum([tree_block(grad_pairs, k) for k in range(contexts)])
    grad_keys = rope_back(grad_pairs[:, :kwp].reshape(rows, -1, HD), cosine, sine)
    grad_pairs = jnp.concatenate(
        [grad_keys.reshape(rows, kwp), grad_pairs[:, kwp:]], axis=1
    ).astype(narrow_dtype)
    grad_quarters = jnp.concatenate([grad_query, grad_pairs[None]], axis=0)
    relative_grads = [
        lax.dynamic_index_in_dim(grad_quarters, d, axis=0, keepdims=False) for d in distances
    ]
    exchanged = context_send(relative_grads)
    exchanged, grad_wo, *ff_sums = bar((exchanged, grad_wo, *ff_sums))
    ff_grads_own = jnp.concatenate(ff_sums, axis=1)
    ff_near = context_gather_start(ff_grads_own)
    normed_gradient = sum(
        contract_last(grads, block) for grads, block in zip(relative_grads, quarter_blocks)
    )
    first_normed_gradient = core_reduce(normed_gradient)
    source_gradient = (
        residual_gradient
        + norm_backward(first_normed_gradient, first_normalized, first_root_mean, first_gain)
    ).astype(narrow_dtype)
    source_gradient = core_join(source_gradient)
    small = jnp.concatenate(
        [
            jnp.sum(first_normed_gradient * first_normalized, axis=0),
            jnp.sum(second_normed_gradient * second_normalized, axis=0),
        ]
    )
    small = small + swap(small, "tp", 1)
    small = jnp.concatenate([small, jnp.sum(grad_quarters.astype(jnp.float32), axis=1).reshape(-1)])

    def packed(value):
        value = value.reshape(-1, quarter)
        high = value.astype(narrow_dtype)
        return high, (value - high.astype(jnp.float32)).astype(narrow_dtype)

    def unpacked(value):
        count = value.shape[-2] // 2
        value = value.astype(jnp.float32)
        return value[..., :count, :] + value[..., count:, :]

    me = lax.axis_index("shard")
    terms = attention_terms(first_normed, exchanged, grad_wo, small.reshape(-1, quarter), core)
    if shards > 4:
        received = [lax.all_to_all(terms, "shard", 0, 0)[k] for k in range(shards)]
    else:
        received = [lax.dynamic_index_in_dim(terms, me, axis=0, keepdims=False)]
        for k in range(1, shards):
            received.append(
                lax.ppermute(
                    lax.dynamic_index_in_dim(terms, lax.rem(me + k, shards), keepdims=False),
                    "shard",
                    [(i, (i + k) % shards) for i in range(shards)],
                )
            )
    received, ff_near = bar((received, ff_near))
    ff_blocks = context_gather_end(ff_grads_own, *ff_near)
    output = core_join((residual + mlp).astype(narrow_dtype))
    count = depth + groups * part
    weight_sums = sum(value[:count].astype(jnp.float32) for value in received).astype(narrow_dtype)
    small = sum(unpacked(value[count:]) for value in received)
    blocks = context_send([jnp.concatenate([weight_sums, *packed(small)], axis=0)] * contexts)
    small = sum(unpacked(block[count:]) for block in blocks).reshape(-1)
    grad_wq, grad_wk, grad_wv, grad_wo = place_attention(blocks, depth, part, qwp, kwp, context)

    wholes = spread([block[0] for block in ff_blocks[:3]], tuple(spans), width, ffp, context)
    far, wholes, output, source_gradient, small, grad_wq = bar(
        (ff_blocks[3], wholes, output, source_gradient, small, grad_wq)
    )
    grad_wg, grad_wu, grad_wd = spread_far(*far, wholes, tuple(spans), width, distances[3])

    edges = [0, model, 2 * model, 2 * model + qwp, 2 * model + qwp + kwp, small.shape[0]]
    sums = [small[edges[i] : edges[i + 1]] for i in range(5)]
    return (
        output[None],
        source_gradient[None],
        sums[0],
        grad_wq,
        sums[2],
        grad_wk,
        sums[3],
        grad_wv,
        sums[4],
        grad_wo,
        sums[1],
        grad_wg,
        grad_wu,
        grad_wd,
    )


def solution(mesh):
    return jax.shard_map(
        body,
        mesh=mesh,
        in_specs=(
            P("shard", "ctx", None),
            P("shard", "ctx", None),
            P(),
            P("shard", "tp"),
            P("tp"),
            P("shard", "tp"),
            P("tp"),
            P("shard", "tp"),
            P("tp"),
            P("shard", "tp"),
            P(),
            P("shard", "tp"),
            P("shard", "tp"),
            P("shard", "tp"),
            P("shard", None),
            P("shard", None),
            P("shard", None),
        ),
        out_specs=(
            P("shard", "ctx", None),
            P("shard", "ctx", None),
            P(),
            P("shard", "tp"),
            P("tp"),
            P("shard", "tp"),
            P("tp"),
            P("shard", "tp"),
            P("tp"),
            P("shard", "tp"),
            P(),
            P("shard", "tp"),
            P("shard", "tp"),
            P("shard", "tp"),
        ),
        check_vma=False,
    )
```

```python
import functools

import jax
import jax.numpy as jnp
from jax import lax
from jax.experimental import pallas as pl
from jax.experimental.pallas import tpu as pltpu
from jax.sharding import PartitionSpec as P

HD = 128


EPS = 1e-06
THETA = 1000000.0
NEG = -1e30


def rope_tables(pos):
    inverse = THETA ** (-jnp.arange(0, HD, 2, dtype=jnp.float32) / HD)
    angle = pos.astype(jnp.float32)[:, None] * inverse[None, :]
    return (
        jnp.concatenate([jnp.cos(angle)] * 2, axis=-1),
        jnp.concatenate([jnp.sin(angle)] * 2, axis=-1),
    )


def rotate_half(v):
    half = v.shape[-1] // 2
    return jnp.concatenate([-v[..., half:], v[..., :half]], axis=-1)


def rope(v, cosine, sine):
    return v * cosine[:, None, :] + rotate_half(v) * sine[:, None, :]


def rope_back(grad, cosine, sine):
    return grad * cosine[:, None, :] - rotate_half(grad * sine[:, None, :])


def contract_last(left, right):
    return lax.dot_general(
        left, right, (((1,), (1,)), ((), ())), preferred_element_type=jnp.float32
    )


def contract_first(left, right):
    return lax.dot_general(
        left, right, (((0,), (0,)), ((), ())), preferred_element_type=jnp.float32
    )


def norm_backward(normed_gradient, normalized_input, root_mean_square, norm_gain):
    scaled_rows = normed_gradient * norm_gain
    return root_mean_square * (
        scaled_rows
        - normalized_input * jnp.mean(scaled_rows * normalized_input, axis=-1, keepdims=True)
    )


def swap(value, axis, distance):
    size = lax.axis_size(axis)
    return lax.ppermute(value, axis, [(i, i ^ distance) for i in range(size)])


def after(value, *others):
    return lax.optimization_barrier((value, *others))[0]


def context_gather_start(value):
    return swap(value, "ctx", 1), swap(value, "ctx", 2)


def context_gather_end(value, first, second):
    half = value.shape[0] // 2
    far_low = swap(first[:half], "ctx", 2)
    far_high = swap(second[half:], "ctx", 1)
    return [[value], [first], [second], [far_low, far_high]]


def context_gather(value):
    return context_gather_end(value, *context_gather_start(value))


def context_send(blocks):
    return [blocks[0]] + [swap(blocks[k], "ctx", k) for k in range(1, len(blocks))]


def context_sum_large(blocks):
    half = blocks[0].shape[0] // 2
    narrow = [block.astype(jnp.bfloat16) for block in blocks]
    far_low = swap(narrow[3][:half], "ctx", 1)
    far_high = swap(narrow[3][half:], "ctx", 2)
    low = (blocks[2][:half].astype(jnp.float32) + far_low.astype(jnp.float32)).astype(jnp.bfloat16)
    high = (blocks[1][half:].astype(jnp.float32) + far_high.astype(jnp.float32)).astype(jnp.bfloat16)
    first = swap(jnp.concatenate([narrow[1][:half], high], axis=0), "ctx", 1)
    second = swap(jnp.concatenate([low, narrow[2][half:]], axis=0), "ctx", 2)
    return blocks[0].astype(jnp.float32) + first.astype(jnp.float32) + second.astype(jnp.float32)


def context_sum(blocks):
    received = context_send([block.astype(jnp.bfloat16) for block in blocks])
    return sum(block.astype(jnp.float32) for block in (blocks[0], *received[1:]))


def spread_kernel(spans, width, total, context_ref, *refs):
    *blocks, gate_ref, up_ref, down_ref = refs
    context = context_ref[0]
    for index, ref in enumerate(blocks):
        offset, columns = spans[index % len(spans)]
        start = jnp.bitwise_xor(context, index // len(spans)) * width + offset
        for matrix, out in enumerate((gate_ref, up_ref, down_ref)):
            for piece in range(0, columns, 128):
                place = start + piece

                @pl.when(place < total)
                def _():
                    out[:, pl.ds(pl.multiple_of(place, 128), 128)] = ref[
                        :, pl.ds(matrix * columns + piece, 128)
                    ].astype(jnp.float32)


def spread(blocks, spans, width, total, context):
    rows = blocks[0].shape[0]
    tile = 48 if rows % 48 == 0 else rows
    return pl.pallas_call(
        functools.partial(spread_kernel, spans, width, total),
        grid=(rows // tile,),
        in_specs=[pl.BlockSpec(memory_space=pltpu.SMEM)]
        + [pl.BlockSpec((tile, block.shape[1]), lambda i: (i, 0)) for block in blocks],
        out_specs=[pl.BlockSpec((tile, total), lambda i: (i, 0))] * 3,
        out_shape=[jax.ShapeDtypeStruct((rows, total), jnp.float32)] * 3,
        compiler_params=pltpu.CompilerParams(vmem_limit_bytes=40 * 1024 * 1024),
    )(context.reshape(1), *blocks)


def spread_far_kernel(spans, place_ref, *refs):
    count = 2 * len(spans)
    outs = refs[count + 3 :]
    late = pl.program_id(0) >= pl.num_programs(0) // 2
    for index, ref in enumerate(refs[:count]):
        offset, columns = spans[index // 2]

        @pl.when(late == (index % 2 == 1))
        def _():
            for matrix, out in enumerate(outs):
                out[:, offset : offset + columns] = ref[
                    :, matrix * columns : (matrix + 1) * columns
                ].astype(jnp.float32)


def spread_far(pieces, wholes, spans, width, place):
    rows, total = wholes[0].shape
    steps = 1
    tile = rows // 2
    while tile % 2 == 0 and tile > 96:
        tile //= 2
        steps *= 2
    maps = (
        lambda i, p: (jnp.minimum(i, steps - 1), 0),
        lambda i, p: (jnp.maximum(i - steps, 0), 0),
    )
    grid_spec = pltpu.PrefetchScalarGridSpec(
        num_scalar_prefetch=1,
        grid=(2 * steps,),
        in_specs=[
            pl.BlockSpec((tile, piece.shape[1]), maps[index % 2])
            for index, piece in enumerate(pieces)
        ]
        + [pl.BlockSpec(memory_space=pl.ANY)] * 3,
        out_specs=[pl.BlockSpec((tile, width), lambda i, p: (i, p[0]))] * 3,
    )
    count = len(pieces) + 1
    return pl.pallas_call(
        functools.partial(spread_far_kernel, spans),
        grid_spec=grid_spec,
        out_shape=[jax.ShapeDtypeStruct((rows, total), jnp.float32)] * 3,
        input_output_aliases={count: 0, count + 1: 1, count + 2: 2},
        compiler_params=pltpu.CompilerParams(vmem_limit_bytes=40 * 1024 * 1024),
    )(place.reshape(1), *pieces, *wholes)


def place_kernel(count, part, context_ref, *refs):
    query_ref, key_ref, value_ref, out_ref = refs[count:]
    context = context_ref[0]
    depth = query_ref.shape[0]
    quarter = refs[0].shape[1]
    whole = query_ref.shape[1] // quarter
    keys = key_ref.shape[1]
    for k in range(count):
        place = jnp.bitwise_xor(context, k)
        block = refs[k][:depth].astype(jnp.float32)

        @pl.when(place < whole)
        def _():
            query_ref[:, pl.ds(pl.multiple_of(place * quarter, 128), quarter)] = block

        @pl.when(place == whole)
        def _():
            key_ref[...] = block[:, :keys]
            value_ref[...] = block[:, keys:]

        row = pl.multiple_of(place * part, 8)
        for g in range(whole):
            start = depth + g * part
            out_ref[pl.ds(row, part), g * quarter : (g + 1) * quarter] = refs[k][
                start : start + part
            ].astype(jnp.float32)


def place_attention(blocks, depth, part, query_width, key_width, context):
    count = len(blocks)
    widths = (query_width, key_width, key_width, query_width)
    vmem = pl.BlockSpec(memory_space=pltpu.VMEM)
    return pl.pallas_call(
        functools.partial(place_kernel, count, part),
        in_specs=[pl.BlockSpec(memory_space=pltpu.SMEM)] + [vmem] * count,
        out_specs=[vmem] * 4,
        out_shape=[jax.ShapeDtypeStruct((depth, width), jnp.float32) for width in widths],
        compiler_params=pltpu.CompilerParams(vmem_limit_bytes=VMEM_LIMIT),
    )(context.reshape(1), *blocks)


NT = (((1,), (1,)), ((), ()))
NN = (((1,), (0,)), ((), ()))
TN = (((0,), (0,)), ((), ()))
VMEM_LIMIT = 56 * 1024 * 1024


def multiply(left, right, dims):
    return lax.dot_general(left, right, dims, preferred_element_type=jnp.float32)


def terms_kernel(count, core_ref, normed_ref, *refs):
    blocks, (wo_ref, small_ref, out_ref, rows_ref) = refs[:count], refs[count:]
    core = core_ref[0]
    half = blocks[0].shape[0] // 2
    depth = normed_ref.shape[1]
    part = wo_ref.shape[1]
    quarter = out_ref.shape[2]

    @pl.when(pl.program_id(0) == 0)
    def _():
        for side in range(2):
            start = pl.multiple_of((core if side == 0 else 1 - core) * half, half)
            for k, block in enumerate(blocks):
                place = (side * count + k) * half
                rows_ref[place : place + half] = block[pl.ds(start, half), :]

    out_ref[0, :depth] = multiply(normed_ref[...], rows_ref[...], TN).astype(jnp.bfloat16)
    place = depth
    for column in range(0, wo_ref.shape[2], quarter):
        out_ref[0, place : place + part] = wo_ref[0, :, column : column + quarter]
        place += part
    size = small_ref.shape[0]
    high = small_ref[...].astype(jnp.bfloat16)
    out_ref[0, place : place + size] = high
    out_ref[0, place + size :] = (small_ref[...] - high.astype(jnp.float32)).astype(jnp.bfloat16)


def attention_terms(normed, blocks, grad_wo, small, core):
    rows, model = normed.shape
    shards, part, width = grad_wo.shape
    depth = model // shards
    quarter = blocks[0].shape[1]
    count = depth + part * (width // quarter) + 2 * small.shape[0]
    if depth % 128:
        half = blocks[0].shape[0] // 2
        ordered = [
            lax.dynamic_slice_in_dim(block, side * half, half)
            for side in (core, 1 - core)
            for block in blocks
        ]
        columns = contract_first(normed, jnp.concatenate(ordered, axis=0)).astype(jnp.bfloat16)
        high = small.astype(jnp.bfloat16)
        low = (small - high.astype(jnp.float32)).astype(jnp.bfloat16)
        return jnp.concatenate(
            [columns.reshape(shards, depth, quarter)]
            + [grad_wo[:, :, i : i + quarter] for i in range(0, width, quarter)]
            + [jnp.broadcast_to(value, (shards,) + value.shape) for value in (high, low)],
            axis=1,
        )
    whole = lambda value: pl.BlockSpec(value.shape, lambda i: (0, 0))
    return pl.pallas_call(
        functools.partial(terms_kernel, len(blocks)),
        grid=(shards,),
        in_specs=[
            pl.BlockSpec(memory_space=pltpu.SMEM),
            pl.BlockSpec((rows, depth), lambda i: (0, i)),
            *(whole(block) for block in blocks),
            pl.BlockSpec((1, part, width), lambda i: (i, 0, 0)),
            whole(small),
        ],
        out_specs=pl.BlockSpec((1, count, quarter), lambda i: (i, 0, 0)),
        out_shape=jax.ShapeDtypeStruct((shards, count, quarter), jnp.bfloat16),
        scratch_shapes=[pltpu.VMEM((rows, quarter), jnp.bfloat16)],
        compiler_params=pltpu.CompilerParams(vmem_limit_bytes=VMEM_LIMIT),
        cost_estimate=pl.CostEstimate(
            flops=2 * rows * model * quarter,
            bytes_accessed=2 * (rows * model + rows * quarter + shards * count * quarter),
            transcendentals=0,
        ),
    )(core.reshape(1), normed, *blocks, grad_wo, small)


def ff_kernel(size, first, normed_ref, gradient_ref, weight_ref, *refs):
    inputs, (acts_ref, *outs) = ((), refs) if first else (refs[:4], refs[4:])
    normed = normed_ref[...]
    gate_up = multiply(normed, weight_ref[:, : 2 * size], NN)
    gate, up = gate_up[:, :size], gate_up[:, size:]
    grad_act = multiply(gradient_ref[...], weight_ref[:, 2 * size :], NN)
    sigma = 1.0 / (1.0 + jnp.exp(-gate))
    silu = gate * sigma
    act = (silu * up).astype(jnp.bfloat16)
    grad_up = (grad_act * silu).astype(jnp.bfloat16)
    grad_gate = (grad_act * up * (sigma * (1.0 + gate * (1.0 - sigma)))).astype(jnp.bfloat16)
    acts_ref[:, :size] = grad_gate
    acts_ref[:, size : 2 * size] = grad_up
    acts_ref[:, 2 * size :] = act
    back = multiply(grad_gate, weight_ref[:, :size], NT) + multiply(
        grad_up, weight_ref[:, size : 2 * size], NT
    )
    mlp = multiply(act, weight_ref[:, 2 * size :], NT)
    late = pl.program_id(0) >= pl.num_programs(0) // 2
    for side in range(2):

        @pl.when(late == (side == 1))
        def _():
            for which, value in enumerate((mlp, back)):
                if not first:
                    value = value + inputs[2 * which + side][...].astype(jnp.float32)
                outs[2 * which + side][...] = value.astype(jnp.bfloat16)


def feed_forward(normed, gradient, weights, previous=(), tile=256):
    rows, model = normed.shape
    columns = weights.shape[1]
    steps = rows // tile // 2
    row = pl.BlockSpec((tile, model), lambda i: (i, 0))
    sides = [
        pl.BlockSpec((tile, model), lambda i: (jnp.minimum(i, steps - 1), 0)),
        pl.BlockSpec((tile, model), lambda i: (jnp.maximum(i - steps, 0), 0)),
    ] * 2
    return pl.pallas_call(
        functools.partial(ff_kernel, columns // 3, not previous),
        grid=(rows // tile,),
        in_specs=[row, row, pl.BlockSpec((model, columns), lambda i: (0, 0))]
        + sides[: len(previous)],
        out_specs=[pl.BlockSpec((tile, columns), lambda i: (i, 0))] + sides,
        out_shape=[jax.ShapeDtypeStruct((rows, columns), jnp.bfloat16)]
        + [jax.ShapeDtypeStruct((rows // 2, model), jnp.bfloat16)] * 4,
        compiler_params=pltpu.CompilerParams(vmem_limit_bytes=VMEM_LIMIT),
        cost_estimate=pl.CostEstimate(
            flops=4 * rows * model * columns,
            bytes_accessed=2 * (rows * columns + 4 * rows * model + model * columns),
            transcendentals=rows * columns // 3,
        ),
    )(normed, gradient, weights, *previous)


def ff_grads_kernel(size, normed_ref, gradient_ref, acts_ref, *outs):
    gate_up = multiply(normed_ref[...], acts_ref[:, : 2 * size], TN).astype(jnp.bfloat16)
    down = multiply(gradient_ref[...], acts_ref[:, 2 * size :], TN).astype(jnp.bfloat16)
    if len(outs) == 2:
        outs[0][...] = gate_up
        outs[1][...] = down
    else:
        outs[0][:, : 2 * size] = gate_up
        outs[0][:, 2 * size :] = down


def ff_grads(normed, gradient, acts, split, tile=384):
    rows, model = normed.shape
    columns = acts.shape[1]
    widths = (columns // 3 * 2, columns // 3) if split else (columns,)
    column = pl.BlockSpec((rows, tile), lambda i: (0, i))
    return pl.pallas_call(
        functools.partial(ff_grads_kernel, columns // 3),
        grid=(model // tile,),
        in_specs=[column, column, pl.BlockSpec((rows, columns), lambda i: (0, 0))],
        out_specs=[pl.BlockSpec((tile, width), lambda i: (i, 0)) for width in widths],
        out_shape=[jax.ShapeDtypeStruct((model, width), jnp.bfloat16) for width in widths],
        compiler_params=pltpu.CompilerParams(vmem_limit_bytes=VMEM_LIMIT),
        cost_estimate=pl.CostEstimate(
            flops=2 * rows * model * columns,
            bytes_accessed=2 * (rows * columns + 2 * rows * model + model * columns),
            transcendentals=0,
        ),
    )(normed, gradient, acts)


def rotate_lanes(value):
    half = HD // 2
    rolled = pltpu.roll(value, half, 1)
    lane = lax.broadcasted_iota(jnp.int32, value.shape, 1)
    return jnp.where(lane < half, -rolled, rolled)


def set_mask(mask_ref, code_ref, pos_ref, seg_all_ref, pos_all_ref):
    allowed = (jnp.right_shift(code_ref[...], seg_all_ref[...]) & 1 == 1) & (
        pos_all_ref[...] <= pos_ref[...]
    )
    mask_ref[...] = jnp.where(allowed, 0.0, NEG)


def attend_kernel(
    query_ref,
    key_ref,
    value_ref,
    code_ref,
    pos_ref,
    seg_all_ref,
    pos_all_ref,
    mixed_ref,
    logsum_ref,
    mask_ref,
    value_t_ref,
):
    head = pl.program_id(1)

    @pl.when(head == 0)
    def _():
        set_mask(mask_ref, code_ref, pos_ref, seg_all_ref, pos_all_ref)
        value_t_ref[...] = value_ref[...].T

    scores = multiply(key_ref[...], query_ref[0], NT) * (HD ** (-0.5)) + mask_ref[...]
    top = jnp.max(scores, axis=0, keepdims=True)
    expo = jnp.exp(scores - top)
    total = jnp.sum(expo, axis=0, keepdims=True)
    mixed = multiply(value_t_ref[...], expo.astype(jnp.bfloat16), NN) * (1.0 / total)
    mixed_ref[...] = mixed.T.astype(jnp.bfloat16)
    logsum_ref[pl.ds(head, 1), :] = top + jnp.log(total)


def attention_specs(tile, total):
    query = pl.BlockSpec((1, tile, HD), lambda i, h: (h // 2, i, h % 2))
    block = pl.BlockSpec((tile, HD), lambda i, h: (i, h))
    key = pl.BlockSpec((total, HD), lambda i, h: (0, 0))
    value = pl.BlockSpec((total, HD), lambda i, h: (0, 1))
    line = pl.BlockSpec((1, tile), lambda i, h: (0, i))
    whole = pl.BlockSpec((total, 1), lambda i, h: (0, 0))
    logsum = pl.BlockSpec((8, tile), lambda i, h: (0, i))
    return query, block, key, value, line, whole, logsum


def attend(queries, pairs, code, pos, seg_all, pos_all, heads):
    rows = queries.shape[1]
    total = pairs.shape[0]
    tile = min(rows, 512)
    query, block, key, value, line, whole, logsum = attention_specs(tile, total)
    return pl.pallas_call(
        attend_kernel,
        grid=(rows // tile, heads),
        in_specs=[query, key, value, line, line, whole, whole],
        out_specs=[block, logsum],
        out_shape=[
            jax.ShapeDtypeStruct((rows, heads * HD), jnp.bfloat16),
            jax.ShapeDtypeStruct((8, rows), jnp.float32),
        ],
        scratch_shapes=[
            pltpu.VMEM((total, tile), jnp.float32),
            pltpu.VMEM((HD, total), jnp.bfloat16),
        ],
        compiler_params=pltpu.CompilerParams(vmem_limit_bytes=VMEM_LIMIT),
        cost_estimate=pl.CostEstimate(
            flops=8 * rows * total * HD * heads,
            bytes_accessed=rows * heads * HD * 6,
            transcendentals=rows * total * heads,
        ),
    )(queries, pairs, pairs, code, pos, seg_all, pos_all)


def attend_back_kernel(
    query_ref,
    grad_ref,
    cosine_ref,
    sine_ref,
    key_ref,
    value_ref,
    code_ref,
    pos_ref,
    seg_all_ref,
    pos_all_ref,
    logsum_ref,
    grad_query_ref,
    grad_pairs_ref,
    mask_ref,
    key_t_ref,
):
    head = pl.program_id(1)

    @pl.when(head == 0)
    def _():
        set_mask(mask_ref, code_ref, pos_ref, seg_all_ref, pos_all_ref)
        key_t_ref[...] = key_ref[...].T

    @pl.when((head == 0) & (pl.program_id(0) == 0))
    def _():
        grad_pairs_ref[...] = jnp.zeros_like(grad_pairs_ref)

    scale = HD ** (-0.5)
    query = query_ref[0]
    grad = grad_ref[...]
    scores = multiply(key_ref[...], query, NT) * scale + mask_ref[...]
    probs = jnp.exp(scores - logsum_ref[pl.ds(head, 1), :])
    grad_p = multiply(value_ref[...], grad, NT)
    delta = jnp.sum(probs * grad_p, axis=0, keepdims=True)
    grad_s = (probs * (grad_p - delta) * scale).astype(jnp.bfloat16)
    grad_query = multiply(key_t_ref[...], grad_s, NN).T
    grad_pairs_ref[:, :HD] += multiply(grad_s, query, NN)
    grad_pairs_ref[:, HD:] += multiply(probs.astype(jnp.bfloat16), grad, NN)
    grad_query_ref[0] = (
        grad_query * cosine_ref[...] - rotate_lanes(grad_query * sine_ref[...])
    ).astype(jnp.bfloat16)


def attend_back(queries, grad, cosine, sine, pairs, code, pos, seg_all, pos_all, logsum, heads):
    rows = queries.shape[1]
    total = pairs.shape[0]
    tile = min(rows, 512)
    query, block, key, value, line, whole, sums = attention_specs(tile, total)
    table = pl.BlockSpec((tile, HD), lambda i, h: (i, 0))
    return pl.pallas_call(
        attend_back_kernel,
        grid=(rows // tile, heads),
        in_specs=[query, block, table, table, key, value, line, line, whole, whole, sums],
        out_specs=[query, pl.BlockSpec((total, 2 * HD), lambda i, h: (0, 0))],
        out_shape=[
            jax.ShapeDtypeStruct((heads // 2, rows, 2 * HD), jnp.bfloat16),
            jax.ShapeDtypeStruct((total, 2 * HD), jnp.float32),
        ],
        scratch_shapes=[
            pltpu.VMEM((total, tile), jnp.float32),
            pltpu.VMEM((HD, total), jnp.bfloat16),
        ],
        compiler_params=pltpu.CompilerParams(vmem_limit_bytes=VMEM_LIMIT),
        cost_estimate=pl.CostEstimate(
            flops=20 * rows * total * HD * heads,
            bytes_accessed=rows * heads * HD * 6,
            transcendentals=rows * total * heads,
        ),
    )(queries, grad, cosine, sine, pairs, pairs, code, pos, seg_all, pos_all, logsum)


def shard_gather_small(piece):
    size = lax.axis_size("shard")
    me = lax.axis_index("shard")
    if size > 4:
        return lax.all_gather(piece, "shard", axis=0, tiled=False)
    parts = [piece] + [
        lax.ppermute(piece, "shard", [(i, (i + k) % size) for i in range(size)])
        for k in range(1, size)
    ]
    whole = jnp.zeros((size,) + piece.shape, piece.dtype)
    for k, part in enumerate(parts):
        whole = lax.dynamic_update_slice(whole, part[None], (lax.rem(me - k + size, size), 0, 0))
    return whole


def body(
    tokens,
    cotangent,
    norm1_gain,
    w_query,
    b_query,
    w_key,
    b_key,
    w_value,
    b_value,
    w_out,
    norm2_gain,
    w_gate,
    w_up,
    w_down,
    parents,
    segment_ids,
    positions,
):
    narrow_dtype = jnp.bfloat16
    rows = tokens.shape[1]
    half = rows // 2
    depth = w_query.shape[0]
    model = tokens.shape[2]
    qwp = w_query.shape[1]
    kwp = w_key.shape[1]
    head_loc = qwp // HD
    ffp = w_gate.shape[1]
    shards = lax.axis_size("shard")
    contexts = lax.axis_size("ctx")
    context = lax.axis_index("ctx")
    core = lax.axis_index("tp")
    inner = qwp + 2 * kwp
    quarter = inner // contexts
    distances = [jnp.bitwise_xor(context, k) for k in range(contexts)]
    bar = lax.optimization_barrier

    def core_half(value):
        return lax.dynamic_slice_in_dim(value, core * half, half)

    def core_order(mine, other):
        low = jnp.where(core == 0, mine, other)
        high = jnp.where(core == 0, other, mine)
        return jnp.concatenate([low, high], axis=0)

    def core_join(value):
        return core_order(value, swap(value, "tp", 1))

    def core_reduce(value):
        mine = lax.dynamic_slice_in_dim(value, core * half, half)
        other = lax.dynamic_slice_in_dim(value, (1 - core) * half, half)
        return mine.astype(jnp.float32) + swap(other.astype(narrow_dtype), "tp", 1).astype(
            jnp.float32
        )

    def tree_gather(value):
        mine = jnp.concatenate(sum(context_gather(value), []), axis=0)
        return jnp.concatenate([mine, swap(mine, "tp", 1)], axis=0)

    def tree_terms(mine, other):
        mine = mine.astype(jnp.float32) + other.astype(jnp.float32)
        return [mine[k * half : (k + 1) * half] for k in range(contexts)]

    def tree_block(value, k):
        count = value.shape[0] // 2
        return core_order(
            value[k * half : (k + 1) * half], value[count + k * half : count + (k + 1) * half]
        )

    def tree_line(line):
        return jnp.concatenate(
            [
                lax.dynamic_slice_in_dim(line, d * rows + side * half, half)
                for side in (core, 1 - core)
                for d in distances
            ]
        )

    first_gain = norm1_gain.astype(jnp.float32)
    second_gain = norm2_gain.astype(jnp.float32)
    source_half = core_half(tokens[0]).astype(jnp.float32)
    first_root_mean = lax.rsqrt(jnp.mean(source_half * source_half, axis=-1, keepdims=True) + EPS)
    first_normalized = source_half * first_root_mean
    first_normed = tree_gather((first_normalized * first_gain).astype(narrow_dtype))

    joined = jnp.concatenate([w_query, w_key, w_value], axis=1)
    quarter_own = lax.dynamic_slice_in_dim(joined, context * quarter, quarter, axis=1)
    columns_all = shard_gather_small(
        jnp.concatenate([quarter_own, joined[:, qwp:]], axis=1)
    ).reshape(model, quarter + 2 * kwp)

    pos_all = tree_line(positions[0])
    cosine_all, sine_all = rope_tables(pos_all)
    first_normed, w_out, parent_line, segment_line, w_gate_late, w_up_late, w_down_late = bar(
        (first_normed, w_out, parents[0], segment_ids[0], w_gate, w_up, w_down)
    )
    seg_all = tree_line(segment_line)
    first_row = context * rows
    seg_own = lax.dynamic_slice_in_dim(segment_line, first_row, rows)
    pos_own = lax.dynamic_slice_in_dim(positions[0], first_row, rows)
    labels = jnp.arange(parents.shape[1], dtype=jnp.int32)

    def parent_of(segment):
        return jnp.sum(jnp.where(segment[:, None] == labels[None], parent_line[None], 0), axis=1)

    above = parent_of(labels)
    code_line = 1 << labels | 1 << above | 1 << parent_of(above)
    code_own = jnp.sum(jnp.where(seg_own[:, None] == labels[None], code_line[None], 0), axis=1)
    mask_lines = (code_own[None], pos_own[None], seg_all[:, None], pos_all[:, None])
    cosine, sine = rope_tables(pos_own)

    lin = jnp.dot(first_normed, columns_all, preferred_element_type=jnp.float32)
    biases = jnp.concatenate([b_query, b_key, b_value]).astype(jnp.float32)

    def turned(value, bias):
        value = (value + bias).reshape(value.shape[0], -1, HD)
        return rope(value, cosine_all, sine_all).reshape(value.shape[0], -1)

    queries_all = turned(
        lin[:, :quarter], lax.dynamic_slice_in_dim(biases, context * quarter, quarter)
    ).astype(narrow_dtype)
    pairs = jnp.concatenate(
        [
            turned(lin[:, quarter : quarter + kwp], biases[qwp : qwp + kwp]),
            lin[:, quarter + kwp :] + biases[qwp + kwp :],
        ],
        axis=1,
    ).astype(narrow_dtype)
    queries = jnp.zeros((contexts, rows, quarter), narrow_dtype)
    exchanged = context_send([tree_block(queries_all, k) for k in range(contexts)])
    for k, block in enumerate(exchanged):
        queries = lax.dynamic_update_slice(queries, block[None], (distances[k], 0, 0))

    part = depth // contexts
    wo_piece = lax.dynamic_slice_in_dim(w_out, context * part, part)
    wo_all = jnp.zeros((shards, contexts, part, qwp), narrow_dtype)
    for k, block in enumerate(context_gather(shard_gather_small(wo_piece))):
        block = jnp.concatenate(block, axis=0)
        wo_all = lax.dynamic_update_slice(wo_all, block[:, None], (0, distances[k], 0, 0))
    wo_all = wo_all.reshape(model, qwp)

    width = -(-ffp // (contexts * 128)) * 128
    first_width = width // 192 * 128
    spans = [(0, first_width), (first_width, width - first_width)]
    padding = ((0, 0), (0, width * contexts - ffp))
    ff_weights = []
    for (offset, size), group in zip(
        spans, ((w_gate, w_up, w_down), (w_gate_late, w_up_late, w_down_late))
    ):
        piece = jnp.concatenate(
            [
                lax.dynamic_slice_in_dim(
                    jnp.pad(w, padding), context * width + offset, size, axis=1
                )
                for w in group
            ],
            axis=1,
        )
        ff_weights.append(lax.all_gather(piece, "shard", axis=0, tiled=True))

    queries, cotangent_late = bar((queries, cotangent))
    gradient_half = core_half(cotangent_late[0])
    tree_gradient = tree_gather(gradient_half)
    mixed_b, logsum = attend(queries, pairs, *mask_lines, head_loc)


    residual = source_half + core_reduce(contract_last(mixed_b, wo_all))
    second_root_mean = lax.rsqrt(jnp.mean(residual * residual, axis=-1, keepdims=True) + EPS)
    second_normalized = residual * second_root_mean
    second_normed = (second_normalized * second_gain).astype(narrow_dtype)
    tree_normed = tree_gather(second_normed)
    tree_normed, quarter_late = bar((tree_normed, columns_all[:, :quarter]))
    quarter_blocks = context_send([quarter_late] * contexts)

    acts, *sums = feed_forward(tree_normed, tree_gradient, ff_weights[0])
    acts, quarter_blocks = bar((acts, quarter_blocks))
    (grads,) = ff_grads(tree_normed, tree_gradient, acts, False)
    grads, late_weights = bar((grads, ff_weights[1]))
    late_acts, *sums = feed_forward(
        tree_normed, tree_gradient, late_weights, tuple(sums)
    )
    (late_grads,) = ff_grads(tree_normed, tree_gradient, late_acts, False)

    def over_shard(value):
        return lax.psum_scatter(
            value.reshape(shards, depth, value.shape[1]), "shard", scatter_dimension=0, tiled=False
        )

    ff_sums = [over_shard(grads)]

    mlp_mine, mlp_other, back_mine, back_other = sums
    back_mine, back_other, late_grads = bar((back_mine, swap(back_other, "tp", 1), late_grads))
    second_normed_gradient = context_sum_large(tree_terms(back_mine, back_other))
    second_normed_gradient, mlp_mine, mlp_other = bar(
        (second_normed_gradient, mlp_mine, mlp_other)
    )
    mlp = context_sum(tree_terms(mlp_mine, swap(mlp_other, "tp", 1)))
    residual_gradient = gradient_half.astype(jnp.float32) + norm_backward(
        second_normed_gradient, second_normalized, second_root_mean, second_gain
    )
    grad_attn_b = core_join(residual_gradient.astype(narrow_dtype))
    grad_mixed = jnp.dot(grad_attn_b, wo_all, preferred_element_type=jnp.float32).astype(
        narrow_dtype
    )

    groups = qwp // quarter
    grad_wo = contract_first(grad_attn_b, mixed_b).astype(narrow_dtype)
    grad_wo = grad_wo.reshape(shards, contexts, part, qwp)
    grad_wo = [lax.dynamic_index_in_dim(grad_wo, d, axis=1, keepdims=False) for d in distances]
    grad_wo = context_sum(grad_wo).astype(narrow_dtype)
    grad_query, grad_pairs = attend_back(
        queries, grad_mixed, cosine, sine, pairs, *mask_lines, logsum, head_loc
    )
    grad_query, grad_pairs, ff_sums[0] = bar((grad_query, grad_pairs, ff_sums[0]))
    ff_sums.append(over_shard(late_grads))
    grad_pairs, mlp = bar((grad_pairs, mlp))
    grad_pairs = context_sum([tree_block(grad_pairs, k) for k in range(contexts)])
    grad_keys = rope_back(grad_pairs[:, :kwp].reshape(rows, -1, HD), cosine, sine)
    grad_pairs = jnp.concatenate(
        [grad_keys.reshape(rows, kwp), grad_pairs[:, kwp:]], axis=1
    ).astype(narrow_dtype)
    grad_quarters = jnp.concatenate([grad_query, grad_pairs[None]], axis=0)
    relative_grads = [
        lax.dynamic_index_in_dim(grad_quarters, d, axis=0, keepdims=False) for d in distances
    ]
    exchanged = context_send(relative_grads)
    exchanged, grad_wo, ff_sums[0] = bar((exchanged, grad_wo, ff_sums[0]))
    early_near = context_gather_start(ff_sums[0])
    normed_gradient = sum(
        contract_last(grads, block) for grads, block in zip(relative_grads, quarter_blocks)
    )
    first_normed_gradient = core_reduce(normed_gradient)
    source_gradient = (
        residual_gradient
        + norm_backward(first_normed_gradient, first_normalized, first_root_mean, first_gain)
    ).astype(narrow_dtype)
    source_gradient = core_join(source_gradient)
    small = jnp.concatenate(
        [
            jnp.sum(first_normed_gradient * first_normalized, axis=0),
            jnp.sum(second_normed_gradient * second_normalized, axis=0),
        ]
    )
    small = small + swap(small, "tp", 1)
    small = jnp.concatenate([small, jnp.sum(grad_quarters.astype(jnp.float32), axis=1).reshape(-1)])

    def packed(value):
        value = value.reshape(-1, quarter)
        high = value.astype(narrow_dtype)
        return high, (value - high.astype(jnp.float32)).astype(narrow_dtype)

    def unpacked(value):
        count = value.shape[-2] // 2
        value = value.astype(jnp.float32)
        return value[..., :count, :] + value[..., count:, :]

    me = lax.axis_index("shard")
    small, early_near, ff_sums[1] = bar((small, early_near, ff_sums[1]))
    late_near = context_gather_start(ff_sums[1])
    terms = attention_terms(first_normed, exchanged, grad_wo, small.reshape(-1, quarter), core)
    if shards > 4:
        received = [lax.all_to_all(terms, "shard", 0, 0)[k] for k in range(shards)]
    else:
        received = [lax.dynamic_index_in_dim(terms, me, axis=0, keepdims=False)]
        for k in range(1, shards):
            received.append(
                lax.ppermute(
                    lax.dynamic_index_in_dim(terms, lax.rem(me + k, shards), keepdims=False),
                    "shard",
                    [(i, (i + k) % shards) for i in range(shards)],
                )
            )
    received, late_near = bar((received, late_near))
    early_blocks = context_gather_end(ff_sums[0], *early_near)
    late_blocks = context_gather_end(ff_sums[1], *late_near)
    output = core_join((residual + mlp).astype(narrow_dtype))
    count = depth + groups * part
    weight_sums = sum(value[:count].astype(jnp.float32) for value in received).astype(narrow_dtype)
    small = sum(unpacked(value[count:]) for value in received)
    blocks = context_send([jnp.concatenate([weight_sums, *packed(small)], axis=0)] * contexts)
    small = sum(unpacked(block[count:]) for block in blocks).reshape(-1)
    grad_wq, grad_wk, grad_wv, grad_wo = place_attention(blocks, depth, part, qwp, kwp, context)

    near = [blocks[k][0] for k in range(3) for blocks in (early_blocks, late_blocks)]
    wholes = spread(near, tuple(spans), width, ffp, context)
    far = early_blocks[3] + late_blocks[3]
    far, wholes, output, source_gradient, small, grad_wq = bar(
        (far, wholes, output, source_gradient, small, grad_wq)
    )
    grad_wg, grad_wu, grad_wd = spread_far(far, wholes, tuple(spans), width, distances[3])

    edges = [0, model, 2 * model, 2 * model + qwp, 2 * model + qwp + kwp, small.shape[0]]
    sums = [small[edges[i] : edges[i + 1]] for i in range(5)]
    return (
        output[None],
        source_gradient[None],
        sums[0],
        grad_wq,
        sums[2],
        grad_wk,
        sums[3],
        grad_wv,
        sums[4],
        grad_wo,
        sums[1],
        grad_wg,
        grad_wu,
        grad_wd,
    )


def solution(mesh):
    return jax.shard_map(
        body,
        mesh=mesh,
        in_specs=(
            P("shard", "ctx", None),
            P("shard", "ctx", None),
            P(),
            P("shard", "tp"),
            P("tp"),
            P("shard", "tp"),
            P("tp"),
            P("shard", "tp"),
            P("tp"),
            P("shard", "tp"),
            P(),
            P("shard", "tp"),
            P("shard", "tp"),
            P("shard", "tp"),
            P("shard", None),
            P("shard", None),
            P("shard", None),
        ),
        out_specs=(
            P("shard", "ctx", None),
            P("shard", "ctx", None),
            P(),
            P("shard", "tp"),
            P("tp"),
            P("shard", "tp"),
            P("tp"),
            P("shard", "tp"),
            P("tp"),
            P("shard", "tp"),
            P(),
            P("shard", "tp"),
            P("shard", "tp"),
            P("shard", "tp"),
        ),
        check_vma=False,
    )
```

```python
import functools

import jax
import jax.numpy as jnp
from jax import lax
from jax.experimental import pallas as pl
from jax.experimental.pallas import tpu as pltpu
from jax.sharding import PartitionSpec as P

HD = 128


EPS = 1e-06
THETA = 1000000.0
NEG = -1e30


def rope_tables(pos):
    inverse = THETA ** (-jnp.arange(0, HD, 2, dtype=jnp.float32) / HD)
    angle = pos.astype(jnp.float32)[:, None] * inverse[None, :]
    return (
        jnp.concatenate([jnp.cos(angle)] * 2, axis=-1),
        jnp.concatenate([jnp.sin(angle)] * 2, axis=-1),
    )


def rotate_half(v):
    half = v.shape[-1] // 2
    return jnp.concatenate([-v[..., half:], v[..., :half]], axis=-1)


def rope(v, cosine, sine):
    return v * cosine[:, None, :] + rotate_half(v) * sine[:, None, :]


def rope_back(grad, cosine, sine):
    return grad * cosine[:, None, :] - rotate_half(grad * sine[:, None, :])


def contract_last(left, right):
    return lax.dot_general(
        left, right, (((1,), (1,)), ((), ())), preferred_element_type=jnp.float32
    )


def contract_first(left, right):
    return lax.dot_general(
        left, right, (((0,), (0,)), ((), ())), preferred_element_type=jnp.float32
    )


def norm_backward(normed_gradient, normalized_input, root_mean_square, norm_gain):
    scaled_rows = normed_gradient * norm_gain
    return root_mean_square * (
        scaled_rows
        - normalized_input * jnp.mean(scaled_rows * normalized_input, axis=-1, keepdims=True)
    )


def swap(value, axis, distance):
    size = lax.axis_size(axis)
    return lax.ppermute(value, axis, [(i, i ^ distance) for i in range(size)])


def after(value, *others):
    return lax.optimization_barrier((value, *others))[0]


def context_gather_start(value):
    return swap(value, "ctx", 1), swap(value, "ctx", 2)


def context_gather_end(value, first, second):
    half = value.shape[0] // 2
    far_low = swap(first[:half], "ctx", 2)
    far_high = swap(second[half:], "ctx", 1)
    return [[value], [first], [second], [far_low, far_high]]


def context_gather(value):
    return context_gather_end(value, *context_gather_start(value))


def context_send(blocks):
    return [blocks[0]] + [swap(blocks[k], "ctx", k) for k in range(1, len(blocks))]


def context_sum_large(blocks):
    half = blocks[0].shape[0] // 2
    narrow = [block.astype(jnp.bfloat16) for block in blocks]
    far_low = swap(narrow[3][:half], "ctx", 1)
    far_high = swap(narrow[3][half:], "ctx", 2)
    low = (blocks[2][:half].astype(jnp.float32) + far_low.astype(jnp.float32)).astype(jnp.bfloat16)
    high = (blocks[1][half:].astype(jnp.float32) + far_high.astype(jnp.float32)).astype(jnp.bfloat16)
    first = swap(jnp.concatenate([narrow[1][:half], high], axis=0), "ctx", 1)
    second = swap(jnp.concatenate([low, narrow[2][half:]], axis=0), "ctx", 2)
    return blocks[0].astype(jnp.float32) + first.astype(jnp.float32) + second.astype(jnp.float32)


def context_sum(blocks):
    received = context_send([block.astype(jnp.bfloat16) for block in blocks])
    return sum(block.astype(jnp.float32) for block in (blocks[0], *received[1:]))


def spread_kernel(spans, width, total, context_ref, *refs):
    *blocks, gate_ref, up_ref, down_ref = refs
    context = context_ref[0]
    for distance, ref in enumerate(blocks):
        start = jnp.bitwise_xor(context, distance) * width
        base = 0
        for offset, columns in spans:
            for out in (gate_ref, up_ref, down_ref):
                for piece in range(0, columns, 128):
                    place = start + offset + piece

                    @pl.when(place < total)
                    def _():
                        out[:, pl.ds(pl.multiple_of(place, 128), 128)] = ref[
                            :, pl.ds(base + piece, 128)
                        ].astype(jnp.float32)

                base += columns


def spread(blocks, spans, width, total, context):
    rows = blocks[0].shape[0]
    tile = 48 if rows % 48 == 0 else rows
    return pl.pallas_call(
        functools.partial(spread_kernel, spans, width, total),
        grid=(rows // tile,),
        in_specs=[pl.BlockSpec(memory_space=pltpu.SMEM)]
        + [pl.BlockSpec((tile, block.shape[1]), lambda i: (i, 0)) for block in blocks],
        out_specs=[pl.BlockSpec((tile, total), lambda i: (i, 0))] * 3,
        out_shape=[jax.ShapeDtypeStruct((rows, total), jnp.float32)] * 3,
        compiler_params=pltpu.CompilerParams(vmem_limit_bytes=40 * 1024 * 1024),
    )(context.reshape(1), *blocks)


def spread_far_kernel(spans, place_ref, low_ref, high_ref, *refs):
    outs = refs[3:]
    late = pl.program_id(0) >= pl.num_programs(0) // 2
    for side, ref in enumerate((low_ref, high_ref)):

        @pl.when(late == (side == 1))
        def _():
            base = 0
            for offset, columns in spans:
                for out in outs:
                    out[:, offset : offset + columns] = ref[:, base : base + columns].astype(
                        jnp.float32
                    )
                    base += columns


def spread_far(low, high, wholes, spans, width, place):
    rows, total = wholes[0].shape
    steps = 1
    tile = rows // 2
    while tile % 2 == 0 and tile > 96:
        tile //= 2
        steps *= 2
    grid_spec = pltpu.PrefetchScalarGridSpec(
        num_scalar_prefetch=1,
        grid=(2 * steps,),
        in_specs=[
            pl.BlockSpec((tile, low.shape[1]), lambda i, p: (jnp.minimum(i, steps - 1), 0)),
            pl.BlockSpec((tile, low.shape[1]), lambda i, p: (jnp.maximum(i - steps, 0), 0)),
        ]
        + [pl.BlockSpec(memory_space=pl.ANY)] * 3,
        out_specs=[pl.BlockSpec((tile, width), lambda i, p: (i, p[0]))] * 3,
    )
    return pl.pallas_call(
        functools.partial(spread_far_kernel, spans),
        grid_spec=grid_spec,
        out_shape=[jax.ShapeDtypeStruct((rows, total), jnp.float32)] * 3,
        input_output_aliases={3: 0, 4: 1, 5: 2},
        compiler_params=pltpu.CompilerParams(vmem_limit_bytes=40 * 1024 * 1024),
    )(place.reshape(1), low, high, *wholes)


def place_kernel(count, part, context_ref, *refs):
    query_ref, key_ref, value_ref, out_ref = refs[count:]
    context = context_ref[0]
    depth = query_ref.shape[0]
    quarter = refs[0].shape[1]
    whole = query_ref.shape[1] // quarter
    keys = key_ref.shape[1]
    for k in range(count):
        place = jnp.bitwise_xor(context, k)
        block = refs[k][:depth].astype(jnp.float32)

        @pl.when(place < whole)
        def _():
            query_ref[:, pl.ds(pl.multiple_of(place * quarter, 128), quarter)] = block

        @pl.when(place == whole)
        def _():
            key_ref[...] = block[:, :keys]
            value_ref[...] = block[:, keys:]

        row = pl.multiple_of(place * part, 8)
        for g in range(whole):
            start = depth + g * part
            out_ref[pl.ds(row, part), g * quarter : (g + 1) * quarter] = refs[k][
                start : start + part
            ].astype(jnp.float32)


def place_attention(blocks, depth, part, query_width, key_width, context):
    count = len(blocks)
    widths = (query_width, key_width, key_width, query_width)
    vmem = pl.BlockSpec(memory_space=pltpu.VMEM)
    return pl.pallas_call(
        functools.partial(place_kernel, count, part),
        in_specs=[pl.BlockSpec(memory_space=pltpu.SMEM)] + [vmem] * count,
        out_specs=[vmem] * 4,
        out_shape=[jax.ShapeDtypeStruct((depth, width), jnp.float32) for width in widths],
        compiler_params=pltpu.CompilerParams(vmem_limit_bytes=VMEM_LIMIT),
    )(context.reshape(1), *blocks)


NT = (((1,), (1,)), ((), ()))
NN = (((1,), (0,)), ((), ()))
TN = (((0,), (0,)), ((), ()))
VMEM_LIMIT = 56 * 1024 * 1024


def multiply(left, right, dims):
    return lax.dot_general(left, right, dims, preferred_element_type=jnp.float32)


def terms_kernel(count, core_ref, normed_ref, *refs):
    blocks, (wo_ref, small_ref, out_ref, rows_ref) = refs[:count], refs[count:]
    core = core_ref[0]
    half = blocks[0].shape[0] // 2
    depth = normed_ref.shape[1]
    part = wo_ref.shape[1]
    quarter = out_ref.shape[2]

    @pl.when(pl.program_id(0) == 0)
    def _():
        for side in range(2):
            start = pl.multiple_of((core if side == 0 else 1 - core) * half, half)
            for k, block in enumerate(blocks):
                place = (side * count + k) * half
                rows_ref[place : place + half] = block[pl.ds(start, half), :]

    out_ref[0, :depth] = multiply(normed_ref[...], rows_ref[...], TN).astype(jnp.bfloat16)
    place = depth
    for column in range(0, wo_ref.shape[2], quarter):
        out_ref[0, place : place + part] = wo_ref[0, :, column : column + quarter]
        place += part
    size = small_ref.shape[0]
    high = small_ref[...].astype(jnp.bfloat16)
    out_ref[0, place : place + size] = high
    out_ref[0, place + size :] = (small_ref[...] - high.astype(jnp.float32)).astype(jnp.bfloat16)


def attention_terms(normed, blocks, grad_wo, small, core):
    rows, model = normed.shape
    shards, part, width = grad_wo.shape
    depth = model // shards
    quarter = blocks[0].shape[1]
    count = depth + part * (width // quarter) + 2 * small.shape[0]
    if depth % 128:
        half = blocks[0].shape[0] // 2
        ordered = [
            lax.dynamic_slice_in_dim(block, side * half, half)
            for side in (core, 1 - core)
            for block in blocks
        ]
        columns = contract_first(normed, jnp.concatenate(ordered, axis=0)).astype(jnp.bfloat16)
        high = small.astype(jnp.bfloat16)
        low = (small - high.astype(jnp.float32)).astype(jnp.bfloat16)
        return jnp.concatenate(
            [columns.reshape(shards, depth, quarter)]
            + [grad_wo[:, :, i : i + quarter] for i in range(0, width, quarter)]
            + [jnp.broadcast_to(value, (shards,) + value.shape) for value in (high, low)],
            axis=1,
        )
    whole = lambda value: pl.BlockSpec(value.shape, lambda i: (0, 0))
    return pl.pallas_call(
        functools.partial(terms_kernel, len(blocks)),
        grid=(shards,),
        in_specs=[
            pl.BlockSpec(memory_space=pltpu.SMEM),
            pl.BlockSpec((rows, depth), lambda i: (0, i)),
            *(whole(block) for block in blocks),
            pl.BlockSpec((1, part, width), lambda i: (i, 0, 0)),
            whole(small),
        ],
        out_specs=pl.BlockSpec((1, count, quarter), lambda i: (i, 0, 0)),
        out_shape=jax.ShapeDtypeStruct((shards, count, quarter), jnp.bfloat16),
        scratch_shapes=[pltpu.VMEM((rows, quarter), jnp.bfloat16)],
        compiler_params=pltpu.CompilerParams(vmem_limit_bytes=VMEM_LIMIT),
        cost_estimate=pl.CostEstimate(
            flops=2 * rows * model * quarter,
            bytes_accessed=2 * (rows * model + rows * quarter + shards * count * quarter),
            transcendentals=0,
        ),
    )(core.reshape(1), normed, *blocks, grad_wo, small)


def ff_kernel(size, first, normed_ref, gradient_ref, weight_ref, *refs):
    inputs, (acts_ref, *outs) = ((), refs) if first else (refs[:4], refs[4:])
    normed = normed_ref[...]
    gate_up = multiply(normed, weight_ref[:, : 2 * size], NN)
    gate, up = gate_up[:, :size], gate_up[:, size:]
    grad_act = multiply(gradient_ref[...], weight_ref[:, 2 * size :], NN)
    sigma = 1.0 / (1.0 + jnp.exp(-gate))
    silu = gate * sigma
    act = (silu * up).astype(jnp.bfloat16)
    grad_up = (grad_act * silu).astype(jnp.bfloat16)
    grad_gate = (grad_act * up * (sigma * (1.0 + gate * (1.0 - sigma)))).astype(jnp.bfloat16)
    acts_ref[:, :size] = grad_gate
    acts_ref[:, size : 2 * size] = grad_up
    acts_ref[:, 2 * size :] = act
    back = multiply(grad_gate, weight_ref[:, :size], NT) + multiply(
        grad_up, weight_ref[:, size : 2 * size], NT
    )
    mlp = multiply(act, weight_ref[:, 2 * size :], NT)
    late = pl.program_id(0) >= pl.num_programs(0) // 2
    for side in range(2):

        @pl.when(late == (side == 1))
        def _():
            for which, value in enumerate((mlp, back)):
                if not first:
                    value = value + inputs[2 * which + side][...].astype(jnp.float32)
                outs[2 * which + side][...] = value.astype(jnp.bfloat16)


def feed_forward(normed, gradient, weights, previous=(), tile=256):
    rows, model = normed.shape
    columns = weights.shape[1]
    steps = rows // tile // 2
    row = pl.BlockSpec((tile, model), lambda i: (i, 0))
    sides = [
        pl.BlockSpec((tile, model), lambda i: (jnp.minimum(i, steps - 1), 0)),
        pl.BlockSpec((tile, model), lambda i: (jnp.maximum(i - steps, 0), 0)),
    ] * 2
    return pl.pallas_call(
        functools.partial(ff_kernel, columns // 3, not previous),
        grid=(rows // tile,),
        in_specs=[row, row, pl.BlockSpec((model, columns), lambda i: (0, 0))]
        + sides[: len(previous)],
        out_specs=[pl.BlockSpec((tile, columns), lambda i: (i, 0))] + sides,
        out_shape=[jax.ShapeDtypeStruct((rows, columns), jnp.bfloat16)]
        + [jax.ShapeDtypeStruct((rows // 2, model), jnp.bfloat16)] * 4,
        compiler_params=pltpu.CompilerParams(vmem_limit_bytes=VMEM_LIMIT),
        cost_estimate=pl.CostEstimate(
            flops=4 * rows * model * columns,
            bytes_accessed=2 * (rows * columns + 4 * rows * model + model * columns),
            transcendentals=rows * columns // 3,
        ),
    )(normed, gradient, weights, *previous)


def ff_grads_kernel(size, normed_ref, gradient_ref, acts_ref, *outs):
    gate_up = multiply(normed_ref[...], acts_ref[:, : 2 * size], TN).astype(jnp.bfloat16)
    down = multiply(gradient_ref[...], acts_ref[:, 2 * size :], TN).astype(jnp.bfloat16)
    if len(outs) == 2:
        outs[0][...] = gate_up
        outs[1][...] = down
    else:
        outs[0][:, : 2 * size] = gate_up
        outs[0][:, 2 * size :] = down


def ff_grads(normed, gradient, acts, split, tile=384):
    rows, model = normed.shape
    columns = acts.shape[1]
    widths = (columns // 3 * 2, columns // 3) if split else (columns,)
    column = pl.BlockSpec((rows, tile), lambda i: (0, i))
    return pl.pallas_call(
        functools.partial(ff_grads_kernel, columns // 3),
        grid=(model // tile,),
        in_specs=[column, column, pl.BlockSpec((rows, columns), lambda i: (0, 0))],
        out_specs=[pl.BlockSpec((tile, width), lambda i: (i, 0)) for width in widths],
        out_shape=[jax.ShapeDtypeStruct((model, width), jnp.bfloat16) for width in widths],
        compiler_params=pltpu.CompilerParams(vmem_limit_bytes=VMEM_LIMIT),
        cost_estimate=pl.CostEstimate(
            flops=2 * rows * model * columns,
            bytes_accessed=2 * (rows * columns + 2 * rows * model + model * columns),
            transcendentals=0,
        ),
    )(normed, gradient, acts)


def rotate_lanes(value):
    half = HD // 2
    rolled = pltpu.roll(value, half, 1)
    lane = lax.broadcasted_iota(jnp.int32, value.shape, 1)
    return jnp.where(lane < half, -rolled, rolled)


def set_mask(mask_ref, code_ref, pos_ref, seg_all_ref, pos_all_ref):
    allowed = (jnp.right_shift(code_ref[...], seg_all_ref[...]) & 1 == 1) & (
        pos_all_ref[...] <= pos_ref[...]
    )
    mask_ref[...] = jnp.where(allowed, 0.0, NEG)


def attend_kernel(
    query_ref,
    key_ref,
    value_ref,
    code_ref,
    pos_ref,
    seg_all_ref,
    pos_all_ref,
    mixed_ref,
    logsum_ref,
    mask_ref,
    value_t_ref,
):
    head = pl.program_id(1)

    @pl.when(head == 0)
    def _():
        set_mask(mask_ref, code_ref, pos_ref, seg_all_ref, pos_all_ref)
        value_t_ref[...] = value_ref[...].T

    scores = multiply(key_ref[...], query_ref[0], NT) * (HD ** (-0.5)) + mask_ref[...]
    top = jnp.max(scores, axis=0, keepdims=True)
    expo = jnp.exp(scores - top)
    total = jnp.sum(expo, axis=0, keepdims=True)
    mixed = multiply(value_t_ref[...], expo.astype(jnp.bfloat16), NN) * (1.0 / total)
    mixed_ref[...] = mixed.T.astype(jnp.bfloat16)
    logsum_ref[pl.ds(head, 1), :] = top + jnp.log(total)


def attention_specs(tile, total):
    query = pl.BlockSpec((1, tile, HD), lambda i, h: (h // 2, i, h % 2))
    block = pl.BlockSpec((tile, HD), lambda i, h: (i, h))
    key = pl.BlockSpec((total, HD), lambda i, h: (0, 0))
    value = pl.BlockSpec((total, HD), lambda i, h: (0, 1))
    line = pl.BlockSpec((1, tile), lambda i, h: (0, i))
    whole = pl.BlockSpec((total, 1), lambda i, h: (0, 0))
    logsum = pl.BlockSpec((8, tile), lambda i, h: (0, i))
    return query, block, key, value, line, whole, logsum


def attend(queries, pairs, code, pos, seg_all, pos_all, heads):
    rows = queries.shape[1]
    total = pairs.shape[0]
    tile = min(rows, 512)
    query, block, key, value, line, whole, logsum = attention_specs(tile, total)
    return pl.pallas_call(
        attend_kernel,
        grid=(rows // tile, heads),
        in_specs=[query, key, value, line, line, whole, whole],
        out_specs=[block, logsum],
        out_shape=[
            jax.ShapeDtypeStruct((rows, heads * HD), jnp.bfloat16),
            jax.ShapeDtypeStruct((8, rows), jnp.float32),
        ],
        scratch_shapes=[
            pltpu.VMEM((total, tile), jnp.float32),
            pltpu.VMEM((HD, total), jnp.bfloat16),
        ],
        compiler_params=pltpu.CompilerParams(vmem_limit_bytes=VMEM_LIMIT),
        cost_estimate=pl.CostEstimate(
            flops=8 * rows * total * HD * heads,
            bytes_accessed=rows * heads * HD * 6,
            transcendentals=rows * total * heads,
        ),
    )(queries, pairs, pairs, code, pos, seg_all, pos_all)


def attend_back_kernel(
    query_ref,
    grad_ref,
    cosine_ref,
    sine_ref,
    key_ref,
    value_ref,
    code_ref,
    pos_ref,
    seg_all_ref,
    pos_all_ref,
    logsum_ref,
    grad_query_ref,
    grad_pairs_ref,
    mask_ref,
    key_t_ref,
):
    head = pl.program_id(1)

    @pl.when(head == 0)
    def _():
        set_mask(mask_ref, code_ref, pos_ref, seg_all_ref, pos_all_ref)
        key_t_ref[...] = key_ref[...].T

    @pl.when((head == 0) & (pl.program_id(0) == 0))
    def _():
        grad_pairs_ref[...] = jnp.zeros_like(grad_pairs_ref)

    scale = HD ** (-0.5)
    query = query_ref[0]
    grad = grad_ref[...]
    scores = multiply(key_ref[...], query, NT) * scale + mask_ref[...]
    probs = jnp.exp(scores - logsum_ref[pl.ds(head, 1), :])
    grad_p = multiply(value_ref[...], grad, NT)
    delta = jnp.sum(probs * grad_p, axis=0, keepdims=True)
    grad_s = (probs * (grad_p - delta) * scale).astype(jnp.bfloat16)
    grad_query = multiply(key_t_ref[...], grad_s, NN).T
    grad_pairs_ref[:, :HD] += multiply(grad_s, query, NN)
    grad_pairs_ref[:, HD:] += multiply(probs.astype(jnp.bfloat16), grad, NN)
    grad_query_ref[0] = (
        grad_query * cosine_ref[...] - rotate_lanes(grad_query * sine_ref[...])
    ).astype(jnp.bfloat16)


def attend_back(queries, grad, cosine, sine, pairs, code, pos, seg_all, pos_all, logsum, heads):
    rows = queries.shape[1]
    total = pairs.shape[0]
    tile = min(rows, 512)
    query, block, key, value, line, whole, sums = attention_specs(tile, total)
    table = pl.BlockSpec((tile, HD), lambda i, h: (i, 0))
    return pl.pallas_call(
        attend_back_kernel,
        grid=(rows // tile, heads),
        in_specs=[query, block, table, table, key, value, line, line, whole, whole, sums],
        out_specs=[query, pl.BlockSpec((total, 2 * HD), lambda i, h: (0, 0))],
        out_shape=[
            jax.ShapeDtypeStruct((heads // 2, rows, 2 * HD), jnp.bfloat16),
            jax.ShapeDtypeStruct((total, 2 * HD), jnp.float32),
        ],
        scratch_shapes=[
            pltpu.VMEM((total, tile), jnp.float32),
            pltpu.VMEM((HD, total), jnp.bfloat16),
        ],
        compiler_params=pltpu.CompilerParams(vmem_limit_bytes=VMEM_LIMIT),
        cost_estimate=pl.CostEstimate(
            flops=20 * rows * total * HD * heads,
            bytes_accessed=rows * heads * HD * 6,
            transcendentals=rows * total * heads,
        ),
    )(queries, grad, cosine, sine, pairs, pairs, code, pos, seg_all, pos_all, logsum)


def shard_gather_small(piece):
    size = lax.axis_size("shard")
    me = lax.axis_index("shard")
    if size > 4:
        return lax.all_gather(piece, "shard", axis=0, tiled=False)
    parts = [piece] + [
        lax.ppermute(piece, "shard", [(i, (i + k) % size) for i in range(size)])
        for k in range(1, size)
    ]
    whole = jnp.zeros((size,) + piece.shape, piece.dtype)
    for k, part in enumerate(parts):
        whole = lax.dynamic_update_slice(whole, part[None], (lax.rem(me - k + size, size), 0, 0))
    return whole


def body(
    tokens,
    cotangent,
    norm1_gain,
    w_query,
    b_query,
    w_key,
    b_key,
    w_value,
    b_value,
    w_out,
    norm2_gain,
    w_gate,
    w_up,
    w_down,
    parents,
    segment_ids,
    positions,
):
    narrow_dtype = jnp.bfloat16
    rows = tokens.shape[1]
    half = rows // 2
    depth = w_query.shape[0]
    model = tokens.shape[2]
    qwp = w_query.shape[1]
    kwp = w_key.shape[1]
    head_loc = qwp // HD
    ffp = w_gate.shape[1]
    shards = lax.axis_size("shard")
    contexts = lax.axis_size("ctx")
    context = lax.axis_index("ctx")
    core = lax.axis_index("tp")
    inner = qwp + 2 * kwp
    quarter = inner // contexts
    distances = [jnp.bitwise_xor(context, k) for k in range(contexts)]
    bar = lax.optimization_barrier

    def core_half(value):
        return lax.dynamic_slice_in_dim(value, core * half, half)

    def core_order(mine, other):
        low = jnp.where(core == 0, mine, other)
        high = jnp.where(core == 0, other, mine)
        return jnp.concatenate([low, high], axis=0)

    def core_join(value):
        return core_order(value, swap(value, "tp", 1))

    def core_reduce(value):
        mine = lax.dynamic_slice_in_dim(value, core * half, half)
        other = lax.dynamic_slice_in_dim(value, (1 - core) * half, half)
        return mine.astype(jnp.float32) + swap(other.astype(narrow_dtype), "tp", 1).astype(
            jnp.float32
        )

    def tree_gather(value):
        mine = jnp.concatenate(sum(context_gather(value), []), axis=0)
        return jnp.concatenate([mine, swap(mine, "tp", 1)], axis=0)

    def tree_terms(mine, other):
        mine = mine.astype(jnp.float32) + other.astype(jnp.float32)
        return [mine[k * half : (k + 1) * half] for k in range(contexts)]

    def tree_block(value, k):
        count = value.shape[0] // 2
        return core_order(
            value[k * half : (k + 1) * half], value[count + k * half : count + (k + 1) * half]
        )

    def tree_line(line):
        return jnp.concatenate(
            [
                lax.dynamic_slice_in_dim(line, d * rows + side * half, half)
                for side in (core, 1 - core)
                for d in distances
            ]
        )

    first_gain = norm1_gain.astype(jnp.float32)
    second_gain = norm2_gain.astype(jnp.float32)
    source_half = core_half(tokens[0]).astype(jnp.float32)
    first_root_mean = lax.rsqrt(jnp.mean(source_half * source_half, axis=-1, keepdims=True) + EPS)
    first_normalized = source_half * first_root_mean
    first_normed = tree_gather((first_normalized * first_gain).astype(narrow_dtype))

    joined = jnp.concatenate([w_query, w_key, w_value], axis=1)
    quarter_own = lax.dynamic_slice_in_dim(joined, context * quarter, quarter, axis=1)
    columns_all = shard_gather_small(
        jnp.concatenate([quarter_own, joined[:, qwp:]], axis=1)
    ).reshape(model, quarter + 2 * kwp)

    pos_all = tree_line(positions[0])
    cosine_all, sine_all = rope_tables(pos_all)
    first_normed, w_out, parent_line, segment_line, w_gate_late, w_up_late, w_down_late = bar(
        (first_normed, w_out, parents[0], segment_ids[0], w_gate, w_up, w_down)
    )
    seg_all = tree_line(segment_line)
    first_row = context * rows
    seg_own = lax.dynamic_slice_in_dim(segment_line, first_row, rows)
    pos_own = lax.dynamic_slice_in_dim(positions[0], first_row, rows)
    labels = jnp.arange(parents.shape[1], dtype=jnp.int32)

    def parent_of(segment):
        return jnp.sum(jnp.where(segment[:, None] == labels[None], parent_line[None], 0), axis=1)

    above = parent_of(labels)
    code_line = 1 << labels | 1 << above | 1 << parent_of(above)
    code_own = jnp.sum(jnp.where(seg_own[:, None] == labels[None], code_line[None], 0), axis=1)
    mask_lines = (code_own[None], pos_own[None], seg_all[:, None], pos_all[:, None])
    cosine, sine = rope_tables(pos_own)

    lin = jnp.dot(first_normed, columns_all, preferred_element_type=jnp.float32)
    biases = jnp.concatenate([b_query, b_key, b_value]).astype(jnp.float32)

    def turned(value, bias):
        value = (value + bias).reshape(value.shape[0], -1, HD)
        return rope(value, cosine_all, sine_all).reshape(value.shape[0], -1)

    queries_all = turned(
        lin[:, :quarter], lax.dynamic_slice_in_dim(biases, context * quarter, quarter)
    ).astype(narrow_dtype)
    pairs = jnp.concatenate(
        [
            turned(lin[:, quarter : quarter + kwp], biases[qwp : qwp + kwp]),
            lin[:, quarter + kwp :] + biases[qwp + kwp :],
        ],
        axis=1,
    ).astype(narrow_dtype)
    queries = jnp.zeros((contexts, rows, quarter), narrow_dtype)
    exchanged = context_send([tree_block(queries_all, k) for k in range(contexts)])
    for k, block in enumerate(exchanged):
        queries = lax.dynamic_update_slice(queries, block[None], (distances[k], 0, 0))

    part = depth // contexts
    wo_piece = lax.dynamic_slice_in_dim(w_out, context * part, part)
    wo_all = jnp.zeros((shards, contexts, part, qwp), narrow_dtype)
    for k, block in enumerate(context_gather(shard_gather_small(wo_piece))):
        block = jnp.concatenate(block, axis=0)
        wo_all = lax.dynamic_update_slice(wo_all, block[:, None], (0, distances[k], 0, 0))
    wo_all = wo_all.reshape(model, qwp)

    width = -(-ffp // (contexts * 128)) * 128
    first_width = width // 192 * 128
    spans = [(0, first_width), (first_width, width - first_width)]
    padding = ((0, 0), (0, width * contexts - ffp))
    ff_weights = []
    for (offset, size), group in zip(
        spans, ((w_gate, w_up, w_down), (w_gate_late, w_up_late, w_down_late))
    ):
        piece = jnp.concatenate(
            [
                lax.dynamic_slice_in_dim(
                    jnp.pad(w, padding), context * width + offset, size, axis=1
                )
                for w in group
            ],
            axis=1,
        )
        ff_weights.append(lax.all_gather(piece, "shard", axis=0, tiled=True))

    queries, cotangent_late = bar((queries, cotangent))
    gradient_half = core_half(cotangent_late[0])
    tree_gradient = tree_gather(gradient_half)
    mixed_b, logsum = attend(queries, pairs, *mask_lines, head_loc)


    residual = source_half + core_reduce(contract_last(mixed_b, wo_all))
    second_root_mean = lax.rsqrt(jnp.mean(residual * residual, axis=-1, keepdims=True) + EPS)
    second_normalized = residual * second_root_mean
    second_normed = (second_normalized * second_gain).astype(narrow_dtype)
    tree_normed = tree_gather(second_normed)
    tree_normed, quarter_late = bar((tree_normed, columns_all[:, :quarter]))
    quarter_blocks = context_send([quarter_late] * contexts)

    acts, *sums = feed_forward(tree_normed, tree_gradient, ff_weights[0])
    acts, quarter_blocks = bar((acts, quarter_blocks))
    (grads,) = ff_grads(tree_normed, tree_gradient, acts, False)
    grads, late_weights = bar((grads, ff_weights[1]))
    late_acts, *sums = feed_forward(
        tree_normed, tree_gradient, late_weights, tuple(sums)
    )
    (late_grads,) = ff_grads(tree_normed, tree_gradient, late_acts, False)

    def over_shard(value):
        return lax.psum_scatter(
            value.reshape(shards, depth, value.shape[1]), "shard", scatter_dimension=0, tiled=False
        )

    ff_sums = [over_shard(grads)]

    mlp_mine, mlp_other, back_mine, back_other = sums
    back_mine, back_other, late_grads = bar((back_mine, swap(back_other, "tp", 1), late_grads))
    second_normed_gradient = context_sum_large(tree_terms(back_mine, back_other))
    second_normed_gradient, mlp_mine, mlp_other = bar(
        (second_normed_gradient, mlp_mine, mlp_other)
    )
    mlp = context_sum(tree_terms(mlp_mine, swap(mlp_other, "tp", 1)))
    residual_gradient = gradient_half.astype(jnp.float32) + norm_backward(
        second_normed_gradient, second_normalized, second_root_mean, second_gain
    )
    grad_attn_b = core_join(residual_gradient.astype(narrow_dtype))
    grad_mixed = jnp.dot(grad_attn_b, wo_all, preferred_element_type=jnp.float32).astype(
        narrow_dtype
    )

    groups = qwp // quarter
    grad_wo = contract_first(grad_attn_b, mixed_b).astype(narrow_dtype)
    grad_wo = grad_wo.reshape(shards, contexts, part, qwp)
    grad_wo = [lax.dynamic_index_in_dim(grad_wo, d, axis=1, keepdims=False) for d in distances]
    grad_wo = context_sum(grad_wo).astype(narrow_dtype)
    grad_query, grad_pairs = attend_back(
        queries, grad_mixed, cosine, sine, pairs, *mask_lines, logsum, head_loc
    )
    grad_query, grad_pairs, ff_sums[0] = bar((grad_query, grad_pairs, ff_sums[0]))
    ff_sums.append(over_shard(late_grads))
    grad_pairs, mlp = bar((grad_pairs, mlp))
    grad_pairs = context_sum([tree_block(grad_pairs, k) for k in range(contexts)])
    grad_keys = rope_back(grad_pairs[:, :kwp].reshape(rows, -1, HD), cosine, sine)
    grad_pairs = jnp.concatenate(
        [grad_keys.reshape(rows, kwp), grad_pairs[:, kwp:]], axis=1
    ).astype(narrow_dtype)
    grad_quarters = jnp.concatenate([grad_query, grad_pairs[None]], axis=0)
    relative_grads = [
        lax.dynamic_index_in_dim(grad_quarters, d, axis=0, keepdims=False) for d in distances
    ]
    exchanged = context_send(relative_grads)
    exchanged, grad_wo, *ff_sums = bar((exchanged, grad_wo, *ff_sums))
    ff_grads_own = jnp.concatenate(ff_sums, axis=1)
    ff_near = context_gather_start(ff_grads_own)
    normed_gradient = sum(
        contract_last(grads, block) for grads, block in zip(relative_grads, quarter_blocks)
    )
    first_normed_gradient = core_reduce(normed_gradient)
    source_gradient = (
        residual_gradient
        + norm_backward(first_normed_gradient, first_normalized, first_root_mean, first_gain)
    ).astype(narrow_dtype)
    source_gradient = core_join(source_gradient)
    small = jnp.concatenate(
        [
            jnp.sum(first_normed_gradient * first_normalized, axis=0),
            jnp.sum(second_normed_gradient * second_normalized, axis=0),
        ]
    )
    small = small + swap(small, "tp", 1)
    small = jnp.concatenate([small, jnp.sum(grad_quarters.astype(jnp.float32), axis=1).reshape(-1)])

    def packed(value):
        value = value.reshape(-1, quarter)
        high = value.astype(narrow_dtype)
        return high, (value - high.astype(jnp.float32)).astype(narrow_dtype)

    def unpacked(value):
        count = value.shape[-2] // 2
        value = value.astype(jnp.float32)
        return value[..., :count, :] + value[..., count:, :]

    me = lax.axis_index("shard")
    terms = attention_terms(first_normed, exchanged, grad_wo, small.reshape(-1, quarter), core)
    if shards > 4:
        received = [lax.all_to_all(terms, "shard", 0, 0)[k] for k in range(shards)]
    else:
        received = [lax.dynamic_index_in_dim(terms, me, axis=0, keepdims=False)]
        for k in range(1, shards):
            received.append(
                lax.ppermute(
                    lax.dynamic_index_in_dim(terms, lax.rem(me + k, shards), keepdims=False),
                    "shard",
                    [(i, (i + k) % shards) for i in range(shards)],
                )
            )
    ff_blocks = context_gather_end(ff_grads_own, *ff_near)
    output = core_join((residual + mlp).astype(narrow_dtype))
    count = depth + groups * part
    weight_sums = sum(value[:count].astype(jnp.float32) for value in received).astype(narrow_dtype)
    small = sum(unpacked(value[count:]) for value in received)
    blocks = context_send([jnp.concatenate([weight_sums, *packed(small)], axis=0)] * contexts)
    small = sum(unpacked(block[count:]) for block in blocks).reshape(-1)
    grad_wq, grad_wk, grad_wv, grad_wo = place_attention(blocks, depth, part, qwp, kwp, context)

    wholes = spread([block[0] for block in ff_blocks[:3]], tuple(spans), width, ffp, context)
    far, wholes, output, source_gradient, small, grad_wq = bar(
        (ff_blocks[3], wholes, output, source_gradient, small, grad_wq)
    )
    grad_wg, grad_wu, grad_wd = spread_far(*far, wholes, tuple(spans), width, distances[3])

    edges = [0, model, 2 * model, 2 * model + qwp, 2 * model + qwp + kwp, small.shape[0]]
    sums = [small[edges[i] : edges[i + 1]] for i in range(5)]
    return (
        output[None],
        source_gradient[None],
        sums[0],
        grad_wq,
        sums[2],
        grad_wk,
        sums[3],
        grad_wv,
        sums[4],
        grad_wo,
        sums[1],
        grad_wg,
        grad_wu,
        grad_wd,
    )


def solution(mesh):
    return jax.shard_map(
        body,
        mesh=mesh,
        in_specs=(
            P("shard", "ctx", None),
            P("shard", "ctx", None),
            P(),
            P("shard", "tp"),
            P("tp"),
            P("shard", "tp"),
            P("tp"),
            P("shard", "tp"),
            P("tp"),
            P("shard", "tp"),
            P(),
            P("shard", "tp"),
            P("shard", "tp"),
            P("shard", "tp"),
            P("shard", None),
            P("shard", None),
            P("shard", None),
        ),
        out_specs=(
            P("shard", "ctx", None),
            P("shard", "ctx", None),
            P(),
            P("shard", "tp"),
            P("tp"),
            P("shard", "tp"),
            P("tp"),
            P("shard", "tp"),
            P("tp"),
            P("shard", "tp"),
            P(),
            P("shard", "tp"),
            P("shard", "tp"),
            P("shard", "tp"),
        ),
        check_vma=False,
    )
```
